128 devices in a mesh: dp: 64 (over z, y_hi, x, core), tensor: 2 (over y_lo).
Axes of the slice: x: 4, y: 4 (y_hi: 2, y_lo: 2; y = y_hi * 2 + y_lo), z: 4, core: 2. Of those that a mesh axis runs over, the one named last changes fastest.
Arguments:
- layer_input: bfloat16 [16384, 1024], P('dp'), may hold values from -16 to 16
- doc_lengths: int32 [4, 4], replicated, may hold values from 1 to 2176, as said below
- gain_attn: float32 [1024], replicated, may hold values from 0.1 to 1.9
- w_query: bfloat16 [1024, 2048], P(None, 'tensor'), may hold values from -0.1875 to 0.1875
- w_key: bfloat16 [1024, 1024], P(None, 'tensor'), may hold values from -0.1875 to 0.1875
- w_value: bfloat16 [1024, 1024], P(None, 'tensor'), may hold values from -0.1875 to 0.1875
- gain_query: float32 [128], replicated, may hold values from 0.1 to 1.9
- gain_key: float32 [128], replicated, may hold values from 0.1 to 1.9
- w_output: bfloat16 [2048, 1024], P('tensor'), may hold values from -2 to 2
- gain_ffn: float32 [1024], replicated, may hold values from 0.1 to 1.9
- w_gate: bfloat16 [1024, 3072], P(None, 'tensor'), may hold values from -0.1875 to 0.1875
- w_up: bfloat16 [1024, 3072], P(None, 'tensor'), may hold values from -0.1875 to 0.1875
- w_down: bfloat16 [3072, 1024], P('tensor'), may hold values from -0.109375 to 0.109375
- cotangent: bfloat16 [16384, 1024], P('dp'), may hold values from -16 to 16
Outputs:
- layer_output: bfloat16 [16384, 1024], P('dp')
- grad_input: float32 [16384, 1024], P('dp')
- grad_gain_attn: float32 [1024], P('dp')
- grad_query: float32 [1024, 2048], P('dp', 'tensor')
- grad_key: float32 [1024, 1024], P('dp', 'tensor')
- grad_value: float32 [1024, 1024], P('dp', 'tensor')
- grad_gain_query: float32 [128], P('dp')
- grad_gain_key: float32 [128], P('dp')
- grad_output: float32 [2048, 1024], P('tensor', 'dp')
- grad_gain_ffn: float32 [1024], P('dp')
- grad_gate: float32 [1024, 3072], P('dp', 'tensor')
- grad_up: float32 [1024, 3072], P('dp', 'tensor')
- grad_down: float32 [3072, 1024], P('tensor', 'dp')
The draws below stay inside these ranges and needn't reach their ends.
Inputs may be any that keep to these rules, and one draw needn't show every extreme that they name: `doc_lengths`: each row holds the lengths of the 4 documents of one sequence, in order, summing to 4096; the last document is the longest, of exactly the largest length.
All inputs are finite; a program needn't handle non-finite values.
Results may differ from the reference program's by a relative error of at most 0.035.
Values may be sent and summed in bfloat16 or wider, within the bound.
No kernel may reach another device: no remote copies, remote signals or barrier semaphores. Data moves between devices by JAX's collectives and lax.ppermute only.
A program may use at most 192 MiB of HBM per device.

```python
import math
import jax
import jax.numpy as jnp
from jax import lax

D = 1024
HEADS = 16
KV_HEADS = 8
HEAD_DIM = 128
FF = 3072
TOK_DEV = 256
NDOC = 4
SP = 16
SEQ = 4096
SEQS = 4
TOKENS = 16384


def draw_doc_lengths(key, part):
    key = jax.random.fold_in(key, 7)
    last_start = SEQ // 2 - TOK_DEV // 2
    slot_len = last_start // (NDOC - 1)
    reach = slot_len // 2 - 1
    offset = jax.random.randint(key, (SEQS, NDOC - 2), -reach, reach + 1).astype(jnp.int32)
    cut_number = jnp.arange(1, NDOC - 1, dtype=jnp.int32)[None, :]
    cuts = cut_number * slot_len + offset
    first = jnp.zeros((SEQS, 1), jnp.int32)
    middle = jnp.full((SEQS, 1), last_start, jnp.int32)
    final = jnp.full((SEQS, 1), SEQ, jnp.int32)
    bounds = jnp.concatenate([first, cuts.astype(jnp.int32), middle, final], axis=1)
    return (bounds[:, 1:] - bounds[:, :-1]).astype(jnp.int32)


def strengthened(drawn, own_key, source, target, shards_of, factor):
    owner, partner = [(jnp.arange(drawn.shape[position]) // (drawn.shape[position] // shards_of)).reshape([-1 if axis == position else 1 for axis in range(drawn.ndim)]) for position in (source, target)]
    chosen = jax.random.permutation(own_key, shards_of)[partner]
    strong = (owner == chosen) | (owner == (partner + shards_of // 2) % shards_of)
    return jnp.where(strong, factor * drawn, drawn)


def steps_of(own_key, dims, shards, smallest, largest):
    level = 1.0
    for axis_at, blocks in shards:
        steps = jax.random.uniform(jax.random.fold_in(jax.random.fold_in(own_key, 6), axis_at), (blocks,), jnp.float32, smallest / len(shards), largest / len(shards))
        level = level * jnp.repeat(jnp.exp(steps), dims[axis_at] // blocks).reshape((-1,) + (1,) * (len(dims) - 1 - axis_at))
    return level


def normal_values(rng, dims, width, most, shards=(), kind=jnp.bfloat16):
    level = steps_of(rng, dims, shards, -0.22, 0.18) if shards else 1.0
    array = jax.random.normal(rng, dims, jnp.float32) * width * level
    return jnp.minimum(jnp.maximum(array, -most), most).astype(kind)


def bell_draw_with(own_key, shape, deviation, limit, shards, heavy, kind=jnp.bfloat16):
    drawn = deviation * jax.random.normal(own_key, shape, jnp.float32)
    if shards:
        drawn = drawn * steps_of(own_key, shape, shards, -0.22, 0.18)
    return jnp.clip(strengthened(drawn, jax.random.fold_in(own_key, 3), *heavy), -limit, limit).astype(kind)


def setup_inputs(seed: int = 0) -> dict:
    splits = jax.random.split(jax.random.key(seed), 15)
    layer_input = bell_draw_with(splits[0], (TOKENS, D), 1.0, 16.0, ((0, 64),), (0, 1, 64, 4.0))
    doc_lengths = draw_doc_lengths(jax.random.fold_in(splits[14], 71), 0)
    gain_attn = jnp.clip(1.0 + 0.18 * jax.random.normal(splits[2], (D,), jnp.float32), 0.1, 1.9)
    w_query = normal_values(splits[3], (D, HEADS * HEAD_DIM), D ** -0.5, 0.1875, ((1, 2),))
    w_key = normal_values(splits[4], (D, KV_HEADS * HEAD_DIM), D ** -0.5, 0.1875, ((1, 2),))
    w_value = normal_values(splits[5], (D, KV_HEADS * HEAD_DIM), D ** -0.5, 0.1875, ((1, 2),))
    gain_query = jnp.clip(1.0 + 0.18 * jax.random.normal(splits[6], (HEAD_DIM,), jnp.float32), 0.1, 1.9)
    gain_key = jnp.clip(1.0 + 0.18 * jax.random.normal(splits[7], (HEAD_DIM,), jnp.float32), 0.1, 1.9)
    w_output = normal_values(splits[8], (HEADS * HEAD_DIM, D), (max(HEADS * HEAD_DIM // 256, 1)) ** -0.5, 2.0, ((0, 2),))
    gain_ffn = jnp.clip(1.0 + 0.18 * jax.random.normal(splits[9], (D,), jnp.float32), 0.1, 1.9)
    w_gate = normal_values(splits[10], (D, FF), D ** -0.5, 0.1875, ((1, 2),))
    w_up = normal_values(splits[11], (D, FF), D ** -0.5, 0.1875, ((1, 2),))
    w_down = normal_values(splits[12], (FF, D), FF ** -0.5, 0.109375, ((0, 2),))
    cotangent = bell_draw_with(splits[13], (TOKENS, D), 1.0, 16.0, ((0, 64),), (0, 1, 64, 4.0))
    return dict(layer_input=layer_input, doc_lengths=doc_lengths, gain_attn=gain_attn, w_query=w_query, w_key=w_key, w_value=w_value, gain_query=gain_query, gain_key=gain_key, w_output=w_output, gain_ffn=gain_ffn, w_gate=w_gate, w_up=w_up, w_down=w_down, cotangent=cotangent)


EPS = 1e-06
ROPE_BASE = 1000000.0
NEG = -1e+30

@jax.custom_vjp
def low(v):
    return lax.optimization_barrier(v.astype(jnp.bfloat16)).astype(jnp.float32)

@jax.custom_vjp
def low_back(v):
    return v

def low_keep(v):
    return (low(v), None)

def low_pass(kept, grad):
    return (grad,)

def back_keep(v):
    return (v, None)

def back_low(kept, grad):
    return (low(grad),)
low.defvjp(low_keep, low_pass)
low_back.defvjp(back_keep, back_low)

def matmul(left, right):
    return jnp.dot(left, right, precision=lax.Precision.HIGHEST)

def normalize(values, gain):
    return values * lax.rsqrt(lax.optimization_barrier(jnp.mean(values * values, axis=-1, keepdims=True)) + EPS) * gain

def rope_tables(positions, head_dim):
    half_dim = head_dim // 2
    freqs = jnp.exp(jnp.arange(half_dim, dtype=jnp.float32) * (-2.0 * math.log(ROPE_BASE) / head_dim))
    angles = positions.astype(jnp.float32)[:, None] * freqs[None, :]
    angles = jnp.concatenate([angles, angles], axis=-1)
    return (jnp.cos(angles), jnp.sin(angles))

def rotate(values, cosine, sine):
    half_dim = values.shape[-1] // 2
    turned = jnp.concatenate([-values[..., half_dim:], values[..., :half_dim]], axis=-1)
    return values * cosine[:, None, :] + turned * sine[:, None, :]

def doc_layout(lengths, count):
    ends = jnp.cumsum(lengths).astype(jnp.int32)
    starts = (ends - lengths).astype(jnp.int32)
    index = jnp.arange(count, dtype=jnp.int32)
    doc_ids = lax.optimization_barrier(jnp.sum((index[:, None] >= ends[None, :]).astype(jnp.int32), axis=1)).astype(jnp.int32)
    chosen = doc_ids[:, None] == jnp.arange(lengths.shape[0], dtype=jnp.int32)[None, :]
    offsets = lax.optimization_barrier(jnp.sum(jnp.where(chosen, starts[None, :], 0), axis=1)).astype(jnp.int32)
    return (index, doc_ids, index - offsets)

def stored_order(count, half_rows, devices):
    stored = jnp.arange(count, dtype=jnp.int32)
    stored_piece = stored // half_rows
    within = stored % half_rows
    holder = stored_piece // 2
    taken = jnp.where(stored_piece % 2 == 1, 2 * devices - 1 - holder, holder)
    return (taken * half_rows + within).astype(jnp.int32)

def reference(layer_input, doc_lengths, gain_attn, w_query, w_key, w_value, gain_query, gain_key, w_output, gain_ffn, w_gate, w_up, w_down, cotangent):
    index_seq = stored_order(SEQ, TOK_DEV // 2, SP)
    doc_nat, pos_nat = jax.vmap(lambda lengths: doc_layout(lengths, SEQ)[1:])(doc_lengths)
    doc_rows = jnp.take(doc_nat, index_seq, axis=1)
    pos_rows = jnp.take(pos_nat, index_seq, axis=1)
    cosine, sine = rope_tables(pos_rows.reshape(TOKENS), HEAD_DIM)
    group_size = HEADS // KV_HEADS
    q_block = math.gcd(512, SEQ)
    num_blocks = SEQ // q_block
    scale = HEAD_DIM ** (-0.5)

    def forward(inputs, g_attn, wq, wk, wv, g_query, g_key, wo, g_ffn, wg, wu, wd):
        normed = low(normalize(inputs, g_attn))
        q_raw = low_back(matmul(normed, wq)).reshape(TOKENS, HEADS, HEAD_DIM)
        k_raw = low_back(matmul(normed, wk)).reshape(TOKENS, KV_HEADS, HEAD_DIM)
        values = low(low_back(matmul(normed, wv))).reshape(TOKENS, KV_HEADS, HEAD_DIM)
        queries = low(rotate(normalize(q_raw, g_query), cosine, sine))
        keys = low(rotate(normalize(k_raw, g_key), cosine, sine))

        def attend_sequence(item):
            q_seq, k_seq, v_seq, doc_seq = item
            keys_rep = jnp.repeat(k_seq, group_size, axis=1)
            values_rep = jnp.repeat(v_seq, group_size, axis=1)

            def attend(block):
                q_part, doc_part, index_part = block
                scores = jnp.einsum('qhd,khd->hqk', q_part, keys_rep, precision=lax.Precision.HIGHEST) * scale
                scores = low_back(scores)
                mask = (doc_part[:, None] == doc_seq[None, :]) & (index_part[:, None] >= index_seq[None, :])
                scores = jnp.where(mask[None], scores, NEG)
                top = lax.optimization_barrier(jnp.max(scores, axis=-1, keepdims=True))
                expo = jnp.exp(scores - top)
                probs = low(expo / lax.optimization_barrier(jnp.sum(expo, axis=-1, keepdims=True)))
                return jnp.einsum('hqk,khd->qhd', probs, values_rep, precision=lax.Precision.HIGHEST)
            blocks = (q_seq.reshape(num_blocks, q_block, HEADS, HEAD_DIM), doc_seq.reshape(num_blocks, q_block), index_seq.reshape(num_blocks, q_block))
            return lax.map(jax.checkpoint(attend), blocks).reshape(SEQ, HEADS, HEAD_DIM)
        items = (queries.reshape(SEQS, SEQ, HEADS, HEAD_DIM), keys.reshape(SEQS, SEQ, KV_HEADS, HEAD_DIM), values.reshape(SEQS, SEQ, KV_HEADS, HEAD_DIM), doc_rows)
        attended = lax.map(attend_sequence, items).reshape(TOKENS, HEADS * HEAD_DIM)
        attended = low_back(low(attended))
        hidden = inputs + low_back(matmul(attended, wo))
        mid = low(normalize(hidden, g_ffn))
        gate = low_back(matmul(mid, wg))
        up = low_back(matmul(mid, wu))
        act = low(jax.nn.silu(gate) * up)
        return hidden + low_back(matmul(act, wd))
    floats = tuple((a.astype(jnp.float32) for a in (layer_input, gain_attn, w_query, w_key, w_value, gain_query, gain_key, w_output, gain_ffn, w_gate, w_up, w_down)))
    result, pullback = jax.vjp(forward, *floats)
    grads = pullback(cotangent.astype(jnp.float32))
    return (result.astype(jnp.bfloat16), grads[0], grads[1], grads[2], grads[3], grads[4], grads[5], grads[6], grads[7], grads[8], grads[9], grads[10], grads[11])
```

```python
import functools
import math

import jax
import jax.numpy as jnp
from jax import lax
from jax.experimental import pallas as pl
from jax.experimental.pallas import tpu as pltpu
from jax.sharding import PartitionSpec as P

EPS = 1e-06
ROPE_BASE = 1000000.0
HEAD = 128
HALF = 256
SCALE = HEAD ** (-0.5)
SCALE2 = SCALE * math.log2(math.e)
CHIPS = 8
LAST_START = 1920
SHIFTS = range(1, CHIPS)
BF = jnp.bfloat16
F32 = jnp.float32


def dp_index(core, x, y, z):
    return core | x << 1 | y << 3 | z << 4


def dp_pairs(target):
    return [
        (dp_index(core, x, y, z), dp_index(*target(core, x, y, z)))
        for core in range(2)
        for x in range(4)
        for y in range(2)
        for z in range(4)
        if target(core, x, y, z) is not None
    ]


def core_swap(value):
    return lax.ppermute(value, "dp", dp_pairs(lambda core, x, y, z: (1 - core, x, y, z)))


def tensor_swap(value):
    return lax.ppermute(value, "tensor", [(0, 1), (1, 0)])


def chip_shift(value, step):
    def target(core, x, y, z):
        chip = (y * 4 + x + step) % CHIPS
        return (core, chip % 4, chip // 4, z)

    return lax.ppermute(value, "dp", dp_pairs(target))


def chip_links(value, links):
    def target(core, x, y, z):
        chip = links.get(y * 4 + x)
        return None if chip is None else (core, chip % 4, chip // 4, z)

    return lax.ppermute(value, "dp", dp_pairs(target))


def dp_groups(key):
    groups = {}
    for index in range(64):
        core, x, y, z = index & 1, index >> 1 & 3, index >> 3 & 1, index >> 4
        groups.setdefault(key(core, x, y, z), []).append(index)
    return list(groups.values())


TREE = ({7: 3}, {7: 5, 3: 1}, {7: 6, 5: 4, 3: 2, 1: 0})


def nn(left, right):
    return lax.dot_general(left, right, (((1,), (0,)), ((), ())), preferred_element_type=F32)


def nt(left, right):
    return lax.dot_general(left, right, (((1,), (1,)), ((), ())), preferred_element_type=F32)


def tn(left, right):
    return lax.dot_general(left, right, (((0,), (0,)), ((), ())), preferred_element_type=F32)


def inv_rms(values):
    return lax.rsqrt(jnp.mean(values * values, axis=-1, keepdims=True) + EPS)


def norm_back(grad, normal, inverse, gain):
    scaled = grad * gain
    return inverse * (scaled - normal * jnp.mean(scaled * normal, axis=-1, keepdims=True))


def first_key(meta, token):
    start = jnp.zeros_like(token)
    for n in range(2, 5):
        start = jnp.where(token >= meta[n], meta[n], start)
    return start


def token_of(meta, block, offset):
    core, chip = meta[0], meta[1]
    if block == 0:
        return chip * HALF + (offset ^ (core * 128))
    return (15 - chip) * HALF + (offset ^ ((1 - core) * 128))


def full(shape, memory=None):
    return pl.BlockSpec(shape, lambda *args: (0,) * len(shape))


def halved(shape, dim):
    def index(*args):
        meta = args[-1]
        return tuple(meta[0] if d == dim else 0 for d in range(len(shape)))

    return pl.BlockSpec(shape, index)


def call(body, meta, grid, args, specs, outs, out_specs, scratch=(), flops=0, mib=40, aliases={}):
    return pl.pallas_call(
        body,
        grid_spec=pltpu.PrefetchScalarGridSpec(
            num_scalar_prefetch=1,
            grid=grid,
            in_specs=specs,
            out_specs=out_specs,
            scratch_shapes=list(scratch),
        ),
        out_shape=outs,
        compiler_params=pltpu.CompilerParams(vmem_limit_bytes=mib * 2**20),
        cost_estimate=pl.CostEstimate(
            flops=flops,
            bytes_accessed=sum(a.size * a.dtype.itemsize for a in args),
            transcendentals=0,
        ),
        input_output_aliases=aliases,
    )(meta, *args)


def shape(dims, kind=BF):
    return jax.ShapeDtypeStruct(dims, kind)


def qkv_body(
    meta, x, xo, ga, wq, wk, wv, gq, gk, cos, sin, normed, q, kv, qraw, kraw, last, *sends
):
    block = pl.program_id(0)
    core, chip = meta[0], meta[1]
    rows = jnp.concatenate([x[...], xo[...]], axis=0).astype(F32)
    n = (rows * inv_rms(rows) * ga[...]).astype(BF)
    normed[...] = n
    cosine, sine = cos[...], sin[...]

    def turned(value, gain):
        w = value * inv_rms(value) * gain
        return (w * cosine + pltpu.roll(w, 64, 1) * sine).astype(BF)

    raw = nn(n, wq[...])
    qraw[...] = raw
    for h in range(4):
        q[h] = turned(raw[:, h * 128 : (h + 1) * 128], gq[...])
    raw = nn(n, wk[...])
    kraw[...] = raw
    keys = [turned(raw[:, h * 128 : (h + 1) * 128], gk[...]) for h in range(2)]
    pair = jnp.concatenate(keys + [nn(n, wv[...]).astype(BF)], axis=1)
    kv[...] = pair
    for step in SHIFTS:

        @pl.when(jnp.where(chip + step >= CHIPS, 1, 0) == block)
        def _():
            sends[step - 1][...] = pair

    @pl.when(block == 0)
    def _():
        piece = jnp.where(core == 1, pair[:128], pair[128:])
        last[...] = jnp.where(chip == CHIPS - 1, piece, jnp.zeros_like(piece))


def with_ones(values):
    return jnp.concatenate([values, jnp.ones_like(values)], axis=1)


def self_body(meta, q, kv, acc):
    for block in range(2):
        rows = slice(block * HALF, (block + 1) * HALF)
        query = token_of(meta, block, lax.broadcasted_iota(jnp.int32, (HALF, 1), 0))
        key = token_of(meta, block, lax.broadcasted_iota(jnp.int32, (1, HALF), 1))
        mask = (key <= query) & (key >= first_key(meta, query))
        pair = kv[rows]
        for h in range(4):
            g = h // 2
            keys = pair[:, g * 128 : (g + 1) * 128]
            values = pair[:, 256 + g * 128 : 256 + (g + 1) * 128]
            weights = jnp.where(mask, jnp.exp2(nt(q[h, rows], keys) * SCALE2), 0.0).astype(BF)
            acc[h, rows] = nn(weights, with_ones(values))


def rest_body(meta, q, acc_in, last, *refs):
    recv, (wo, att, lse, own, send, acc, start) = refs[:7], refs[7:]
    chip = meta[1]
    acc[...] = acc_in[...]
    for block in range(2):
        query = token_of(meta, block, lax.broadcasted_iota(jnp.int32, (HALF, HALF), 0))
        start[block] = first_key(meta, query)
    key_off = lax.broadcasted_iota(jnp.int32, (1, HALF), 1)
    for step in SHIFTS:
        lower = step <= chip
        sel = jnp.where(lower, 0, 1)
        row0 = pl.multiple_of(sel * HALF, HALF)
        key = jnp.where(lower, (chip - step) * HALF + (key_off ^ (meta[0] * 128)), LAST_START + 128)
        mask = key >= start[sel]
        pair = recv[step - 1][...]
        for h in range(4):
            g = h // 2
            keys = pair[:, g * 128 : (g + 1) * 128]
            values = pair[:, 256 + g * 128 : 256 + (g + 1) * 128]
            raw = nt(q[h, pl.ds(row0, HALF), :], keys)
            weights = jnp.where(mask, jnp.exp2(raw * SCALE2), 0.0).astype(BF)
            acc[h, pl.ds(row0, HALF), :] += nn(weights, with_ones(values))
    pair = last[...]
    parts = []
    for h in range(4):
        g = h // 2
        keys = pair[:, g * 128 : (g + 1) * 128]
        values = pair[:, 256 + g * 128 : 256 + (g + 1) * 128]
        weights = jnp.exp2(nt(q[h, HALF:], keys) * SCALE2).astype(BF)
        acc[h, HALF:] += nn(weights, with_ones(values))
        total = acc[h, :, 128:]
        parts.append((acc[h, :, :128] / total).astype(BF))
        lse[h : h + 1] = jnp.log2(jnp.transpose(total)[0:1])
    lse[4:8] = jnp.zeros((4, 2 * HALF), F32)
    attended = jnp.concatenate(parts, axis=1)
    att[...] = attended
    out = nn(attended, wo[...]).astype(BF)
    own[0:128], send[0:128] = out[0:128], out[128:256]
    own[128:256], send[128:256] = out[256:384], out[384:512]


def ffn_body(
    meta, mid, mido, dy, dyo, wg, wu, wd, dmid, dmids, y, ys, dgate, dup, act, mid_all, dy_all, dsum, ysum
):
    step = pl.program_id(0)

    @pl.when(step == 0)
    def _():
        mid_all[:HALF], mid_all[HALF:] = mid[...], mido[...]
        dy_all[:HALF], dy_all[HALF:] = dy[...], dyo[...]
        dsum[...] = jnp.zeros_like(dsum)
        ysum[...] = jnp.zeros_like(ysum)

    gate = nn(mid_all[...], wg[...])
    up = nn(mid_all[...], wu[...])
    d_act = nt(dy_all[...], wd[...])
    sigma = 1.0 / (1.0 + jnp.exp(-gate))
    silu = gate * sigma
    act_b = (silu * up).astype(BF)
    d_gate = (d_act * up * sigma * (1.0 + gate * (1.0 - sigma))).astype(BF)
    d_up = (d_act * silu).astype(BF)
    act[...], dgate[...], dup[...] = act_b, d_gate, d_up
    dsum[...] += nt(d_gate, wg[...]) + nt(d_up, wu[...])
    ysum[...] += nn(act_b, wd[...])

    @pl.when(step == pl.num_programs(0) - 1)
    def _():
        dmid[...], dmids[...] = dsum[:HALF].astype(BF), dsum[HALF:].astype(BF)
        y[...], ys[...] = ysum[:HALF].astype(BF), ysum[HALF:].astype(BF)


def ffn_grad_body(meta, mid, mido, dy, dyo, dgate, dup, act, out):
    width = dgate.shape[1]
    for n, (own, other, right) in enumerate(((mid, mido, dgate), (mid, mido, dup), (dy, dyo, act))):
        left = jnp.concatenate([own[...], other[...]], axis=0)
        out[:, n * width : (n + 1) * width] = tn(left, right[...]).astype(BF)


def pieces(own, other):
    return jnp.concatenate([own[0:128], other[0:128], own[128:256], other[128:256]], axis=0)


def bwd_body(meta, dat, dato, wo, q, att, lse_in, last, *refs):
    recv = refs[:7]
    (d_att, dq, dlast), dpair = refs[7:10], refs[10:17]
    go, lse_out, delta_out, start = refs[17:]
    chip = meta[1]
    d_attn = pieces(dat[...], dato[...])
    go[...] = tn(d_attn, att[...]).astype(BF)
    grad = nt(d_attn, wo[...]).astype(BF)
    for h in range(4):
        part = grad[:, h * 128 : (h + 1) * 128]
        d_att[h] = part
        prod = part.astype(F32) * att[:, h * 128 : (h + 1) * 128].astype(F32)
        delta = jnp.sum(jnp.transpose(prod), axis=0, keepdims=True)
        for block in range(2):
            cols = slice(block * HALF, (block + 1) * HALF)
            delta_out[block, h : h + 1] = delta[:, cols]
            lse_out[block, h : h + 1] = lse_in[h : h + 1, cols]
    for block in range(2):
        query = token_of(meta, block, lax.broadcasted_iota(jnp.int32, (HALF, HALF), 1))
        start[block] = first_key(meta, query)
    dq[...] = jnp.zeros_like(dq)

    def one(pair, sel, row0, mask):
        key_grads, value_grads = [], []
        for g in range(2):
            keys = pair[:, g * 128 : (g + 1) * 128]
            values = pair[:, 256 + g * 128 : 256 + (g + 1) * 128]
            key_grad = value_grad = 0.0
            for h in (2 * g, 2 * g + 1):
                query, upper = q[h, pl.ds(row0, HALF), :], d_att[h, pl.ds(row0, HALF), :]
                weights = jnp.exp2(nt(keys, query) * SCALE2 - lse_out[sel, h : h + 1])
                if mask is not None:
                    weights = jnp.where(mask, weights, 0.0)
                d_score = (weights * (nt(values, upper) - delta_out[sel, h : h + 1])).astype(BF)
                value_grad += nn(weights.astype(BF), upper)
                key_grad += nn(d_score, query)
                dq[h, pl.ds(row0, HALF), :] += tn(d_score, keys)
            key_grads.append((key_grad * SCALE).astype(BF))
            value_grads.append(value_grad.astype(BF))
        return jnp.concatenate(key_grads + value_grads, axis=1)

    key_off = lax.broadcasted_iota(jnp.int32, (HALF, 1), 0)
    for step in SHIFTS:
        lower = step <= chip
        sel = jnp.where(lower, 0, 1)
        row0 = pl.multiple_of(sel * HALF, HALF)
        key = jnp.where(lower, (chip - step) * HALF + (key_off ^ (meta[0] * 128)), LAST_START + 128)
        dpair[step - 1][...] = one(recv[step - 1][...], sel, row0, key >= start[sel])
    dlast[...] = one(last[...], 1, HALF, None)


def self_bwd_body(meta, q, kv, d_att, lse, delta, dq_in, dq, dkv):
    for block in range(2):
        rows = slice(block * HALF, (block + 1) * HALF)
        key = token_of(meta, block, lax.broadcasted_iota(jnp.int32, (HALF, 1), 0))
        query = token_of(meta, block, lax.broadcasted_iota(jnp.int32, (1, HALF), 1))
        mask = (key <= query) & (key >= first_key(meta, query))
        pair = kv[rows]
        for g in range(2):
            keys = pair[:, g * 128 : (g + 1) * 128]
            values = pair[:, 256 + g * 128 : 256 + (g + 1) * 128]
            key_grad = value_grad = 0.0
            for h in (2 * g, 2 * g + 1):
                weights = jnp.exp2(nt(keys, q[h, rows]) * SCALE2 - lse[block, h : h + 1])
                weights = jnp.where(mask, weights, 0.0)
                d_score = (weights * (nt(values, d_att[h, rows]) - delta[block, h : h + 1])).astype(BF)
                value_grad += nn(weights.astype(BF), d_att[h, rows])
                key_grad += nn(d_score, q[h, rows])
                dq[h, rows] = dq_in[h, rows] + tn(d_score, keys)
            dkv[rows, g * 128 : (g + 1) * 128] = key_grad * SCALE
            dkv[rows, 256 + g * 128 : 256 + (g + 1) * 128] = value_grad


def qkv_bwd_body(
    meta, x, xo, ga, normed, qraw, kraw, cos, sin, gq, gk, wq, wk, wv, dq, dkv_in, dlast, *refs
):
    recv, (grads, own, send, gains, dkv, draw) = refs[:7], refs[7:]
    core, chip = meta[0], meta[1]
    dkv[...] = dkv_in[...]
    for step in SHIFTS:
        row0 = pl.multiple_of(jnp.where(chip + step >= CHIPS, HALF, 0), HALF)
        dkv[pl.ds(row0, HALF), :] += recv[step - 1][...].astype(F32)
    row0 = pl.multiple_of(jnp.where(core == 1, 0, 128), 128)
    piece = dlast[...].astype(F32)
    dkv[pl.ds(row0, 128), :] += jnp.where(chip == CHIPS - 1, piece, jnp.zeros_like(piece))
    cosine, sine = cos[...], sin[...]

    def back(grad, value, gain):
        turned = grad * cosine + pltpu.roll(grad * sine, 64, 1)
        inverse = inv_rms(value)
        hat = value * inverse
        gain_part = jnp.sum(turned * hat, axis=0, keepdims=True)
        return norm_back(turned, hat, inverse, gain).astype(BF), gain_part

    gain_sum = 0.0
    for h in range(4):
        cols = slice(h * 128, (h + 1) * 128)
        draw[:, cols], part = back(dq[h] * SCALE, qraw[:, cols], gq[...])
        gain_sum += part
    gains[0:1, 0:128] = gain_sum
    gain_sum = 0.0
    for h in range(2):
        cols = slice(h * 128, (h + 1) * 128)
        out, part = back(dkv[:, cols], kraw[:, cols], gk[...])
        draw[:, 512 + h * 128 : 512 + (h + 1) * 128] = out
        gain_sum += part
    gains[1:2, 0:128] = gain_sum
    draw[:, 768:1024] = dkv[:, 256:512].astype(BF)
    grads[...] = tn(normed[...], draw[...]).astype(BF)
    d_normed = nt(draw[:, :512], wq[...]) + nt(draw[:, 512:768], wk[...]) + nt(draw[:, 768:], wv[...])
    rows = pieces(x[...], xo[...]).astype(F32)
    gains[2:3] = jnp.sum(d_normed * (rows * inv_rms(rows)), axis=0, keepdims=True)
    out = d_normed.astype(BF)
    own[0:128], send[0:128] = out[0:128], out[128:256]
    own[128:256], send[128:256] = out[256:384], out[384:512]


def reduced(own, received):
    part = lax.optimization_barrier((own.astype(F32) + received.astype(F32)).astype(BF))
    return part, tensor_swap(part)


def local(
    layer_input,
    doc_lengths,
    gain_attn,
    w_query,
    w_key,
    w_value,
    gain_query,
    gain_key,
    w_output,
    gain_ffn,
    w_gate,
    w_up,
    w_down,
    cotangent,
):
    dp = lax.axis_index("dp")
    core = dp % 2
    chip = dp // 2 % CHIPS
    lengths = lax.dynamic_index_in_dim(doc_lengths, dp // 16, 0, keepdims=False)
    ends = jnp.cumsum(lengths)[:3]
    meta = jnp.concatenate(
        [jnp.stack([core, chip]).astype(jnp.int32), ends.astype(jnp.int32)]
    )
    width = w_gate.shape[1] // 2
    x, dy = layer_input, cotangent
    xo = core_swap(x)
    dyo = core_swap(dy)

    offset = jnp.arange(HALF, dtype=jnp.int32)
    tokens = jnp.concatenate([token_of(meta, 0, offset), token_of(meta, 1, offset)])
    position = (tokens - first_key(meta, tokens)).astype(F32)
    freqs = jnp.exp(jnp.arange(64, dtype=F32) * (-2.0 * math.log(ROPE_BASE) / HEAD))
    angles = position[:, None] * freqs[None, :]
    cosine, sine = jnp.cos(angles), jnp.sin(angles)
    cosine = jnp.concatenate([cosine, cosine], axis=1)
    sine = jnp.concatenate([-sine, sine], axis=1)

    ga, gf = gain_attn[None, :], gain_ffn[None, :]
    gq, gk = gain_query[None, :], gain_key[None, :]
    w_specs = [halved((1024, 512), 1), halved((1024, 256), 1), halved((1024, 256), 1)]
    step_rows = lambda n: pl.BlockSpec((n, 1024), lambda i, m: (i, 0))
    outs = call(
        qkv_body,
        meta,
        (2,),
        [x, xo, ga, w_query, w_key, w_value, gq, gk, cosine, sine],
        [step_rows(128), step_rows(128), full((1, 1024))]
        + w_specs
        + [full((1, 128)), full((1, 128))]
        + [pl.BlockSpec((HALF, 128), lambda i, m: (i, 0))] * 2,
        [
            shape((512, 1024)),
            shape((4, 512, 128)),
            shape((512, 512)),
            shape((512, 512), F32),
            shape((512, 256), F32),
            shape((128, 512)),
        ]
        + [shape((HALF, 512))] * 7,
        [
            step_rows(HALF),
            pl.BlockSpec((4, HALF, 128), lambda i, m: (0, i, 0)),
            pl.BlockSpec((HALF, 512), lambda i, m: (i, 0)),
            pl.BlockSpec((HALF, 512), lambda i, m: (i, 0)),
            pl.BlockSpec((HALF, 256), lambda i, m: (i, 0)),
            full((128, 512)),
        ]
        + [full((HALF, 512))] * 7,
        flops=2 * 512 * 1024 * 1024,
    )
    normed, q, kv, qraw, kraw, last = outs[:6]
    recv = [chip_shift(value, step) for step, value in zip(SHIFTS, outs[6:])]
    for links in TREE:
        last = last + chip_links(last, links)

    (acc,) = call(
        self_body,
        meta,
        (1,),
        [q, kv],
        [full((4, 512, 128)), full((512, 512))],
        [shape((4, 512, 256), F32)],
        [full((4, 512, 256))],
        flops=2 * 8 * 256 * 256 * 384,
    )
    att, lse, own, send = call(
        rest_body,
        meta,
        (1,),
        [q, acc, last, *recv, w_output],
        [full((4, 512, 128)), full((4, 512, 256)), full((128, 512))]
        + [full((HALF, 512))] * 7
        + [halved((512, 1024), 0)],
        [shape((512, 512)), shape((8, 512), F32), shape((HALF, 1024)), shape((HALF, 1024))],
        [full((512, 512)), full((8, 512)), full((HALF, 1024)), full((HALF, 1024))],
        [pltpu.VMEM((4, 512, 256), F32), pltpu.VMEM((2, HALF, HALF), jnp.int32)],
        flops=2 * 30 * 256 * 256 * 384 + 2 * 512 * 512 * 1024,
    )
    part, other = reduced(own, core_swap(send))
    inputs = x.astype(F32)
    hidden = inputs + (part.astype(F32) + other.astype(F32))
    inv_mid = inv_rms(hidden)
    mid_hat = hidden * inv_mid
    mid = (mid_hat * gf).astype(BF)
    mido = core_swap(mid)

    rows_spec = full((HALF, 1024))
    dmid, dmids, y, ys, dgate, dup, act = call(
        ffn_body,
        meta,
        (3,),
        [mid, mido, dy, dyo, w_gate, w_up, w_down],
        [rows_spec] * 4
        + [pl.BlockSpec((1024, 256), lambda i, m: (0, m[0] * 3 + i))] * 2
        + [pl.BlockSpec((256, 1024), lambda i, m: (m[0] * 3 + i, 0))],
        [shape((HALF, 1024))] * 4 + [shape((512, width))] * 3,
        [rows_spec] * 4 + [pl.BlockSpec((512, 256), lambda i, m: (0, i))] * 3,
        [
            pltpu.VMEM((512, 1024), BF),
            pltpu.VMEM((512, 1024), BF),
            pltpu.VMEM((512, 1024), F32),
            pltpu.VMEM((512, 1024), F32),
        ],
        flops=2 * 6 * 512 * 1024 * width,
    )
    dpart, dother = reduced(dmid, core_swap(dmids))
    (ffn_grads,) = call(
        ffn_grad_body,
        meta,
        (4,),
        [mid, mido, dy, dyo, dgate, dup, act],
        [pl.BlockSpec((HALF, 256), lambda i, m: (0, i))] * 4 + [full((512, width))] * 3,
        [shape((1024, 3 * width))],
        [pl.BlockSpec((256, 3 * width), lambda i, m: (i, 0))],
        flops=2 * 3 * 512 * 1024 * width,
    )
    d_mid = dpart.astype(F32) + dother.astype(F32)
    grad_gain_ffn = jnp.sum(d_mid * mid_hat, axis=0)
    d_hidden = dy.astype(F32) + norm_back(d_mid, mid_hat, inv_mid, gf)
    d_attn = d_hidden.astype(BF)
    d_attno = core_swap(d_attn)
    outs = call(
        bwd_body,
        meta,
        (1,),
        [d_attn, d_attno, w_output, q, att, lse, last, *recv],
        [rows_spec, rows_spec, halved((512, 1024), 0), full((4, 512, 128)), full((512, 512))]
        + [full((8, 512)), full((128, 512))]
        + [full((HALF, 512))] * 7,
        [shape((4, 512, 128)), shape((4, 512, 128), F32), shape((128, 512))]
        + [shape((HALF, 512))] * 7
        + [shape((1024, 512)), shape((2, 8, HALF), F32), shape((2, 8, HALF), F32)],
        [full((4, 512, 128)), full((4, 512, 128)), full((128, 512))]
        + [full((HALF, 512))] * 7
        + [full((1024, 512)), full((2, 8, HALF)), full((2, 8, HALF))],
        [pltpu.VMEM((2, HALF, HALF), jnp.int32)],
        flops=2 * 30 * 256 * 256 * 640 + 4 * 512 * 512 * 1024,
    )
    d_att, dq, dlast = outs[:3]
    go, lse, delta = outs[10:]
    drecv = [chip_shift(value, -step) for step, value in zip(SHIFTS, outs[3:10])]
    for links in reversed(TREE):
        dlast = dlast + chip_links(dlast, {b: a for a, b in links.items()})
    dq, dkv = call(
        self_bwd_body,
        meta,
        (1,),
        [q, kv, d_att, lse, delta, dq],
        [full((4, 512, 128)), full((512, 512)), full((4, 512, 128))]
        + [full((2, 8, HALF))] * 2
        + [full((4, 512, 128))],
        [shape((4, 512, 128), F32), shape((512, 512), F32)],
        [full((4, 512, 128)), full((512, 512))],
        flops=2 * 8 * 256 * 256 * 640,
    )
    grads, own, send, gains = call(
        qkv_bwd_body,
        meta,
        (1,),
        [x, xo, ga, normed, qraw, kraw, cosine, sine, gq, gk, w_query, w_key, w_value]
        + [dq, dkv, dlast, *drecv],
        [rows_spec, rows_spec, full((1, 1024)), full((512, 1024)), full((512, 512))]
        + [full((512, 256)), full((512, 128)), full((512, 128)), full((1, 128)), full((1, 128))]
        + w_specs
        + [full((4, 512, 128)), full((512, 512)), full((128, 512))]
        + [full((HALF, 512))] * 7,
        [shape((1024, 1024)), shape((HALF, 1024)), shape((HALF, 1024)), shape((8, 1024), F32)],
        [full((1024, 1024)), rows_spec, rows_spec, full((8, 1024))],
        [pltpu.VMEM((512, 512), F32), pltpu.VMEM((512, 1024), BF)],
        flops=4 * 512 * 1024 * 1024,
    )

    by_z = dp_groups(lambda core, x, y, z: (core, x, y))
    by_plane = dp_groups(lambda core, x, y, z: (core, z))
    by_chip = dp_groups(lambda core, x, y, z: core)
    early = jnp.concatenate([ffn_grads, go], axis=1).reshape(4, 256, -1)
    early = lax.psum_scatter(early, "dp", axis_index_groups=by_z)
    early = lax.all_to_all(early.reshape(8, 32, -1), "dp", 0, 0, axis_index_groups=by_plane)
    early = jnp.sum(early.astype(F32), axis=0)
    spread = jnp.concatenate(
        [
            gains[2].reshape(32, 32),
            grad_gain_ffn.reshape(32, 32),
            gains[0, :128].reshape(32, 4),
            gains[1, :128].reshape(32, 4),
            jnp.zeros((32, 56), F32),
        ],
        axis=1,
    )
    high = lax.reduce_precision(spread, 8, 7)
    rows = jnp.stack([high, spread - high], axis=1).astype(BF)
    rows = jnp.pad(rows, ((0, 0), (0, 30), (0, 0)))
    late = jnp.concatenate([grads.reshape(32, 32, 1024), rows], axis=2)
    late = lax.all_to_all(late, "dp", 0, 0, axis_index_groups=by_chip)
    late = jnp.sum(late.astype(F32), axis=0)

    gain_part = late[0:1, 1024:] + late[1:2, 1024:]
    gain_part = gain_part + core_swap(gain_part)
    ffn_gain = gain_part[0, 32:64]
    gain_part = (gain_part + tensor_swap(gain_part))[0]
    mine = lambda values, count: lax.dynamic_slice_in_dim(values, core * count, count)
    grad_gain_attn = mine(gain_part[0:32], 16)
    grad_gain_ffn = mine(ffn_gain, 16)
    grad_gain_query = mine(gain_part[64:68], 2)
    grad_gain_key = mine(gain_part[68:72], 2)

    whole = jnp.concatenate([early, late[:, :1024]], axis=1)
    kept = lax.dynamic_slice_in_dim(whole, core * 16, 16, 0)
    given = lax.dynamic_slice_in_dim(whole, (1 - core) * 16, 16, 0)
    taken = core_swap(given)
    low = jnp.where(core == 0, kept, taken)
    high = jnp.where(core == 0, taken, kept)
    cuts = [width, 2 * width, 3 * width, 3 * width + 512, 3 * width + 1024, 3 * width + 1280]
    parts = [
        jnp.concatenate([a, b], axis=1)
        for a, b in zip(jnp.split(low, cuts, axis=1), jnp.split(high, cuts, axis=1))
    ]
    grad_gate, grad_up, grad_down, grad_output, grad_query, grad_key, grad_value = parts

    part, other = reduced(y, core_swap(ys))
    layer_output = (hidden + (part.astype(F32) + other.astype(F32))).astype(BF)
    part, other = reduced(own, core_swap(send))
    d_normed = part.astype(F32) + other.astype(F32)
    inv_in = inv_rms(inputs)
    grad_input = d_hidden + norm_back(d_normed, inputs * inv_in, inv_in, ga)
    return (
        layer_output,
        grad_input,
        grad_gain_attn,
        grad_query,
        grad_key,
        grad_value,
        grad_gain_query,
        grad_gain_key,
        jnp.transpose(grad_output),
        grad_gain_ffn,
        grad_gate,
        grad_up,
        jnp.transpose(grad_down),
    )


def solution(mesh):
    placed = (
        P("dp", None),
        P(),
        P(),
        P(None, "tensor"),
        P(None, "tensor"),
        P(None, "tensor"),
        P(),
        P(),
        P("tensor", None),
        P(),
        P(None, "tensor"),
        P(None, "tensor"),
        P("tensor", None),
        P("dp", None),
    )
    return jax.shard_map(
        local,
        mesh=mesh,
        in_specs=placed,
        out_specs=(
            P("dp", None),
            P("dp", None),
            P("dp"),
            P("dp", "tensor"),
            P("dp", "tensor"),
            P("dp", "tensor"),
            P("dp"),
            P("dp"),
            P("tensor", "dp"),
            P("dp"),
            P("dp", "tensor"),
            P("dp", "tensor"),
            P("tensor", "dp"),
        ),
        check_vma=False,
    )
```

```python
import functools
import math

import jax
import jax.numpy as jnp
import numpy as np
from jax import lax
from jax.experimental import pallas as pl
from jax.experimental.pallas import tpu as pltpu
from jax.sharding import PartitionSpec as P

EPS = 1e-06
COST = 1.15e9
ROPE_BASE = 1000000.0
HEAD = 128
HALF = 256
SCALE = HEAD ** (-0.5)
SCALE2 = SCALE * math.log2(math.e)
CHIPS = 8
LAST_START = 1920
STEPS = (1, 2, 3)
BF = jnp.bfloat16
F32 = jnp.float32


def dp_index(core, x, y, z):
    return core | x << 1 | y << 3 | z << 4


def dp_pairs(target):
    return [
        (dp_index(core, x, y, z), dp_index(*target(core, x, y, z)))
        for core in range(2)
        for x in range(4)
        for y in range(2)
        for z in range(4)
        if target(core, x, y, z) is not None
    ]


def core_swap(value):
    return lax.ppermute(value, "dp", dp_pairs(lambda core, x, y, z: (1 - core, x, y, z)))


def tensor_swap(value):
    return lax.ppermute(value, "tensor", [(0, 1), (1, 0)])


def x_shift(value, step):
    return lax.ppermute(
        value, "dp", dp_pairs(lambda core, x, y, z: (core, (x + step) % 4, y, z))
    )


def y_swap(value):
    return lax.ppermute(value, "dp", dp_pairs(lambda core, x, y, z: (core, x, 1 - y, z)))


def x_pair(value, bits):
    return lax.ppermute(value, "dp", dp_pairs(lambda core, x, y, z: (core, x ^ bits, y, z)))


def z_pair(value, bits):
    return lax.ppermute(value, "dp", dp_pairs(lambda core, x, y, z: (core, x, y, z ^ bits)))


def z_shift(value, step):
    return lax.ppermute(
        value, "dp", dp_pairs(lambda core, x, y, z: (core, x, y, (z + step) % 4))
    )


def chip_links(value, links):
    def target(core, x, y, z):
        chip = links.get(y * 4 + x)
        return None if chip is None else (core, chip % 4, chip // 4, z)

    return lax.ppermute(value, "dp", dp_pairs(target))


def dp_groups(key):
    groups = {}
    for index in range(64):
        core, x, y, z = index & 1, index >> 1 & 3, index >> 3 & 1, index >> 4
        groups.setdefault(key(core, x, y, z), []).append(index)
    return list(groups.values())


TREE = ({7: 3}, {7: 5, 3: 1}, {7: 6, 5: 4, 3: 2, 1: 0})


def nn(left, right):
    return lax.dot_general(left, right, (((1,), (0,)), ((), ())), preferred_element_type=F32)


def nt(left, right):
    return lax.dot_general(left, right, (((1,), (1,)), ((), ())), preferred_element_type=F32)


def tn(left, right):
    return lax.dot_general(left, right, (((0,), (0,)), ((), ())), preferred_element_type=F32)


def inv_rms(values):
    return lax.rsqrt(jnp.mean(values * values, axis=-1, keepdims=True) + EPS)


def norm_back(grad, normal, inverse, gain):
    scaled = grad * gain
    return inverse * (scaled - normal * jnp.mean(scaled * normal, axis=-1, keepdims=True))


class Place:
    def __init__(self, ids, lengths):
        dp = ids[0]
        self.core, self.x, self.y, self.z = dp & 1, dp >> 1 & 3, dp >> 3 & 1, dp >> 4
        self.chip = self.y * 4 + self.x
        first = lengths[self.z, 0]
        second = first + lengths[self.z, 1]
        self.starts = (first, second, second + lengths[self.z, 2])

    def first_key(self, token):
        start = jnp.zeros_like(token)
        for end in self.starts:
            start = jnp.where(token >= end, end, start)
        return start

    def token(self, block, offset):
        if block == 0:
            return self.chip * HALF + (offset ^ (self.core * 128))
        return (15 - self.chip) * HALF + (offset ^ ((1 - self.core) * 128))

    def row_block(self, step):
        lower = step <= self.x
        sel = jnp.where(lower, 0, 1)

        def keys(offset):
            token = (self.chip - step) * HALF + (offset ^ (self.core * 128))
            return jnp.where(lower, token, LAST_START + 128)

        return sel, keys

    def far_block(self, step):
        source = (self.x - step) & 3

        def keys(offset):
            token = source * HALF + (offset ^ (self.core * 128))
            return jnp.where(self.y == 1, token, LAST_START + 128)

        return 1 - self.y, keys


def rows_of(sel):
    return pl.ds(pl.multiple_of(sel * HALF, HALF), HALF)


def full(shape):
    return pl.BlockSpec(shape, lambda *args: (0,) * len(shape), memory_space=pltpu.VMEM)


HBM = pl.BlockSpec(memory_space=pltpu.HBM)


def pinned(value):
    return pltpu.with_memory_space_constraint(value, pltpu.HBM)


def call(body, cost_us, prefetch, args, specs, outs, out_specs, scratch=(), grid=(1,), mib=16, aliases={}):
    return pl.pallas_call(
        body,
        grid_spec=pltpu.PrefetchScalarGridSpec(
            num_scalar_prefetch=len(prefetch),
            grid=grid,
            in_specs=[full(a.shape) if spec is None else spec for a, spec in zip(args, specs)],
            out_specs=[full(o.shape) if spec is None else spec for o, spec in zip(outs, out_specs)],
            scratch_shapes=list(scratch),
        ),
        out_shape=outs,
        compiler_params=pltpu.CompilerParams(vmem_limit_bytes=mib * 2**20),
        cost_estimate=pl.CostEstimate(flops=int(cost_us * COST), bytes_accessed=1, transcendentals=0),
        input_output_aliases=aliases,
    )(*prefetch, *args)


def shape(dims, kind=BF):
    return jax.ShapeDtypeStruct(dims, kind)


def stored(dims, kind=BF):
    return pltpu.HBM(dims, kind)


def columns(ref, core, size):
    return ref.at[:, pl.ds(pl.multiple_of(core * size, size), size)]


def rows(ref, core, size):
    return ref.at[pl.ds(pl.multiple_of(core * size, size), size), :]


def started(source, target, sem):
    copy = pltpu.make_async_copy(source, target, sem)
    copy.start()
    return copy


def pieces(own, other):
    return jnp.concatenate([own[0:128], other[0:128], own[128:256], other[128:256]], axis=0)


def split_rows(value, own, other):
    own[0:128], other[0:128] = value[0:128], value[128:256]
    own[128:256], other[128:256] = value[256:384], value[384:512]


def turned(value, gain, cosine, sine):
    w = value * inv_rms(value) * gain
    return (w * cosine + pltpu.roll(w, 64, 1) * sine).astype(BF)


def key_value_body(
    ids, lengths, x, xo, ga, wk, wv, gk, tab_c, tab_s, normed, kv, kraw, cos, sin, s1, s2, s3, sr, wk_v, wv_v, sem
):
    at = Place(ids, lengths)
    copy_k = started(columns(wk, at.core, 256), wk_v, sem.at[0])
    copy_v = started(columns(wv, at.core, 256), wv_v, sem.at[1])
    row = lax.broadcasted_iota(jnp.int32, (1, 128), 1)
    freq = jnp.exp((row & 63).astype(F32) * (-2.0 * math.log(ROPE_BASE) / HEAD))
    offset = lax.broadcasted_iota(jnp.int32, (128, 128), 0)
    tab_c, tab_s = tab_c[...], tab_s[...]
    for piece in range(4):
        base = at.token(piece // 2, jnp.int32(piece % 2 * 128))
        start = at.first_key(base + offset)
        shift_c = shift_s = None
        for first in (jnp.int32(0),) + at.starts:
            angle = (base - first).astype(F32) * freq
            c, s = jnp.cos(angle), jnp.sin(angle)
            if shift_c is None:
                shift_c, shift_s = jnp.broadcast_to(c, (128, 128)), jnp.broadcast_to(s, (128, 128))
            else:
                shift_c = jnp.where(start == first, c, shift_c)
                shift_s = jnp.where(start == first, s, shift_s)
        cos[piece * 128 : (piece + 1) * 128] = shift_c * tab_c - shift_s * tab_s
        sine = shift_s * tab_c + shift_c * tab_s
        sin[piece * 128 : (piece + 1) * 128] = jnp.where(row < 64, -sine, sine)
    for block in range(2):
        cut = slice(block * 128, (block + 1) * 128)
        here = slice(block * HALF, (block + 1) * HALF)
        value = jnp.concatenate([x[cut], xo[cut]], axis=0).astype(F32)
        n = (value * inv_rms(value) * ga[...]).astype(BF)
        normed[here] = n
        if block == 0:
            copy_k.wait()
            copy_v.wait()
        raw = nn(n, wk_v[...])
        kraw[here] = raw.astype(BF)
        for h in range(2):
            head = slice(h * 128, (h + 1) * 128)
            kv[here, head] = turned(raw[:, head], gk[...], cos[here], sin[here])
        kv[here, 256:] = nn(n, wv_v[...]).astype(BF)
    copies = [
        started(kv.at[rows_of(jnp.where(at.x + step < 4, 0, 1))], out, sem.at[1 + step])
        for step, out in zip(STEPS, (s1, s2, s3))
    ]
    copies.append(started(kv.at[rows_of(at.y)], sr, sem.at[5]))
    for copy in copies:
        copy.wait()


def attend(q, acc, where, pair, mask):
    ones = jnp.ones((pair.shape[0], 128), BF)
    for h in range(4):
        g = h // 2
        keys = pair[:, g * 128 : (g + 1) * 128]
        values = pair[:, 256 + g * 128 : 256 + (g + 1) * 128]
        weights = jnp.exp2(nt(q[h, where, :], keys) * SCALE2)
        if mask is not None:
            weights = jnp.where(mask, weights, 0.0)
        acc[h, where, :] += nn(weights.astype(BF), jnp.concatenate([values, ones], axis=1))


def query_body(
    ids, lengths, normed, wq, gq, cos, sin, kv, q, qraw, acc, wq_v, sem
):
    at = Place(ids, lengths)
    copy = started(columns(wq, at.core, 512), wq_v, sem.at[0])
    acc[...] = jnp.zeros_like(acc)
    copy.wait()
    for block in range(2):
        here = slice(block * HALF, (block + 1) * HALF)
        raw = nn(normed[here], wq_v[...])
        qraw[here] = raw.astype(BF)
        for h in range(4):
            q[h, here] = turned(raw[:, h * 128 : (h + 1) * 128], gq[...], cos[here], sin[here])
        query = at.token(block, lax.broadcasted_iota(jnp.int32, (HALF, 1), 0))
        key = at.token(block, lax.broadcasted_iota(jnp.int32, (1, HALF), 1))
        attend(q, acc, here, kv[here], (key <= query) & (key >= at.first_key(query)))


def set_starts(at, start, dim):
    for block in range(2):
        start[block] = at.first_key(at.token(block, lax.broadcasted_iota(jnp.int32, (HALF, HALF), dim)))


def near_body(
    ids, lengths, q, acc_in, r1, r2, r3, rr, x15, ga, wk, wv, gk, tab_c, tab_s, acc, last, start, wk_v, wv_v, sem
):
    at = Place(ids, lengths)
    copy_k = started(columns(wk, at.core, 256), wk_v, sem.at[0])
    copy_v = started(columns(wv, at.core, 256), wv_v, sem.at[1])
    acc[...] = acc_in[...]
    set_starts(at, start, 0)
    offset = lax.broadcasted_iota(jnp.int32, (1, HALF), 1)
    for step, pair in zip(STEPS, (r1, r2, r3)):
        sel, keys = at.row_block(step)
        attend(q, acc, rows_of(sel), pair[...], keys(offset) >= start[sel])
    sel, keys = at.far_block(0)
    attend(q, acc, rows_of(sel), rr[...], keys(offset) >= start[sel])
    value = x15[...].astype(F32)
    n = (value * inv_rms(value) * ga[...]).astype(BF)
    copy_k.wait()
    copy_v.wait()
    raw = nn(n, wk_v[...])
    sine = tab_s[...]
    sine = jnp.where(lax.broadcasted_iota(jnp.int32, (1, 128), 1) < 64, -sine, sine)
    for h in range(2):
        head = slice(h * 128, (h + 1) * 128)
        last[:, head] = turned(raw[:, head], gk[...], tab_c[...], sine)
    last[:, 256:] = nn(n, wv_v[...]).astype(BF)
    attend(q, acc, pl.ds(HALF, HALF), last[...], None)


def far_body(ids, lengths, q, acc_in, r1, r2, r3, wo, att, lse, own, send, acc, start, wo_v, sem):
    at = Place(ids, lengths)
    copy = started(rows(wo, at.core, 512), wo_v, sem.at[0])
    acc[...] = acc_in[...]
    set_starts(at, start, 0)
    offset = lax.broadcasted_iota(jnp.int32, (1, HALF), 1)
    for step, pair in zip(STEPS, (r1, r2, r3)):
        sel, keys = at.far_block(step)
        attend(q, acc, rows_of(sel), pair[...], keys(offset) >= start[sel])
    for h in range(4):
        total = acc[h, :, 128:]
        att[:, h * 128 : (h + 1) * 128] = (acc[h, :, :128] / total).astype(BF)
        lse[h : h + 1] = jnp.log2(jnp.transpose(total)[0:1])
    lse[4:8] = jnp.zeros((4, 2 * HALF), F32)
    copy.wait()
    split_rows(nn(att[...], wo_v[...]).astype(BF), own, send)


def ffn_body(
    ids, lengths, mid, mido, dy, dyo, wg, wu, wd, dmid, dmids, y, ys, dgate, dup, act, wg_v, wu_v, wd_v, mid_all, dy_all, dsum, ysum, sem
):
    at = Place(ids, lengths)
    step = pl.program_id(0)

    def copies(n):
        cut = pl.multiple_of(at.core * 768 + n * 256, 256)
        return [
            pltpu.make_async_copy(wg.at[:, pl.ds(cut, 256)], wg_v.at[n], sem.at[n, 0]),
            pltpu.make_async_copy(wu.at[:, pl.ds(cut, 256)], wu_v.at[n], sem.at[n, 1]),
            pltpu.make_async_copy(wd.at[pl.ds(cut, 256), :], wd_v.at[n], sem.at[n, 2]),
        ]

    @pl.when(step == 0)
    def _():
        for n in range(3):
            for copy in copies(n):
                copy.start()
        mid_all[:HALF], mid_all[HALF:] = mid[...], mido[...]
        dy_all[:HALF], dy_all[HALF:] = dy[...], dyo[...]
        dsum[...] = jnp.zeros_like(dsum)
        ysum[...] = jnp.zeros_like(ysum)

    for copy in copies(step):
        copy.wait()
    w_g, w_u, w_d = wg_v[step], wu_v[step], wd_v[step]
    gate = nn(mid_all[...], w_g)
    up = nn(mid_all[...], w_u)
    d_act = nt(dy_all[...], w_d)
    sigma = 1.0 / (1.0 + jnp.exp(-gate))
    silu = gate * sigma
    act_b = (silu * up).astype(BF)
    d_gate = (d_act * up * sigma * (1.0 + gate * (1.0 - sigma))).astype(BF)
    d_up = (d_act * silu).astype(BF)
    act[...], dgate[...], dup[...] = act_b, d_gate, d_up
    dsum[...] += nt(d_gate, w_g) + nt(d_up, w_u)
    ysum[...] += nn(act_b, w_d)

    @pl.when(step == pl.num_programs(0) - 1)
    def _():
        dmid[...], dmids[...] = dsum[:HALF].astype(BF), dsum[HALF:].astype(BF)
        y[...], ys[...] = ysum[:HALF].astype(BF), ysum[HALF:].astype(BF)


def ffn_grad_body(mid, mido, dy, dyo, dgate, dup, act, out):
    width = dgate.shape[1]
    left = jnp.concatenate([mid[...], mido[...]], axis=0)
    out[:, :width] = tn(left, dgate[...]).astype(BF)
    out[:, width : 2 * width] = tn(left, dup[...]).astype(BF)
    left = jnp.concatenate([dy[...], dyo[...]], axis=0)
    out[:, 2 * width :] = tn(left, act[...]).astype(BF)


def spread(grads, at, outs, sem, first=0):
    return [
        started(grads.at[at(step)], out, sem.at[first + step])
        for step, out in zip((0,) + STEPS, outs)
    ]


def attend_back(q, d_att, lse, delta, dq, sel, where, pair, mask):
    key_grads, value_grads = [], []
    for g in range(2):
        keys = pair[:, g * 128 : (g + 1) * 128]
        values = pair[:, 256 + g * 128 : 256 + (g + 1) * 128]
        key_grad = value_grad = 0.0
        for h in (2 * g, 2 * g + 1):
            query, upper = q[h, where, :], d_att[h, where, :]
            weights = jnp.exp2(nt(keys, query) * SCALE2 - lse[sel, h : h + 1])
            if mask is not None:
                weights = jnp.where(mask, weights, 0.0)
            d_score = (weights * (nt(values, upper) - delta[sel, h : h + 1])).astype(BF)
            value_grad += nn(weights.astype(BF), upper)
            key_grad += nn(d_score, query)
            dq[h, where, :] += tn(d_score, keys)
        key_grads.append(key_grad * SCALE)
        value_grads.append(value_grad)
    return jnp.concatenate(key_grads + value_grads, axis=1)


def far_back_body(
    ids, lengths, dat, dato, wo, q_h, att_h, lse_in, r1, r2, r3, last_h, d_att, lse, delta, dq, g1, g2, g3, glast, wo_v, q, att, far_v, last, stage, stage_last, start, sem
):
    at = Place(ids, lengths)
    copy = started(rows(wo, at.core, 512), wo_v, sem.at[0])
    loads = [
        started(source, target, sem.at[5 + n])
        for n, (source, target) in enumerate(
            ((att_h, att), (q_h, q), (last_h, last), (r1, far_v.at[0]), (r2, far_v.at[1]), (r3, far_v.at[2]))
        )
    ]
    set_starts(at, start, 1)
    dq[...] = jnp.zeros_like(dq)
    d_attn = pieces(dat[...], dato[...])
    copy.wait()
    grad = nt(d_attn, wo_v[...]).astype(BF)
    lse[...] = jnp.zeros_like(lse)
    delta[...] = jnp.zeros_like(delta)
    loads[0].wait()
    for h in range(4):
        part = grad[:, h * 128 : (h + 1) * 128]
        d_att[h] = part
        prod = part.astype(F32) * att[:, h * 128 : (h + 1) * 128].astype(F32)
        total = jnp.sum(jnp.transpose(prod), axis=0, keepdims=True)
        for block in range(2):
            cut = slice(block * HALF, (block + 1) * HALF)
            delta[block, h : h + 1] = total[:, cut]
            lse[block, h : h + 1] = lse_in[h : h + 1, cut]
    loads[1].wait()
    loads[2].wait()
    out = attend_back(q, d_att, lse, delta, dq, 1, pl.ds(HALF, HALF), last[...], None)
    stage_last[...] = out.astype(BF)
    copies = [started(stage_last, glast, sem.at[1])]
    offset = lax.broadcasted_iota(jnp.int32, (HALF, 1), 0)
    for step, target in zip(STEPS, (g1, g2, g3)):
        sel, keys = at.far_block(step)
        loads[2 + step].wait()
        pair = far_v[step - 1]
        out = attend_back(q, d_att, lse, delta, dq, sel, rows_of(sel), pair, keys(offset) >= start[sel])
        stage[step - 1] = out.astype(BF)
        copies.append(started(stage.at[step - 1], target, sem.at[1 + step]))
    for copy in copies:
        copy.wait()


def near_back_body(
    ids, lengths, q, d_att, lse, delta, dq_in, r1, r2, r3, rr, dq, gr, g1, g2, g3, stage, start, sem
):
    at = Place(ids, lengths)
    set_starts(at, start, 1)
    dq[...] = dq_in[...]
    offset = lax.broadcasted_iota(jnp.int32, (HALF, 1), 0)
    copies = []
    sel, keys = at.far_block(0)
    out = attend_back(q, d_att, lse, delta, dq, sel, rows_of(sel), rr[...], keys(offset) >= start[sel])
    gr[...] = out.astype(BF)
    for step, pair, target in zip(STEPS, (r1, r2, r3), (g1, g2, g3)):
        sel, keys = at.row_block(step)
        out = attend_back(q, d_att, lse, delta, dq, sel, rows_of(sel), pair[...], keys(offset) >= start[sel])
        stage[step - 1] = out.astype(BF)
        copies.append(started(stage.at[step - 1], target, sem.at[step - 1]))
    for copy in copies:
        copy.wait()


def head_back(grad, value, gain, cosine, sine):
    turned_back = grad * cosine + pltpu.roll(grad * sine, 64, 1)
    inverse = inv_rms(value)
    hat = value * inverse
    gain_part = jnp.sum(turned_back * hat, axis=0, keepdims=True)
    return norm_back(turned_back, hat, inverse, gain).astype(BF), gain_part


def own_back_body(
    ids, lengths, q, kv, d_att, lse, delta, dq_in, dat, dato, att_h, dq, dkv, grads_h, att, grads, sem
):
    at = Place(ids, lengths)
    load = started(att_h, att, sem.at[0])
    dq[...] = dq_in[...]
    for block in range(2):
        here = slice(block * HALF, (block + 1) * HALF)
        key = at.token(block, lax.broadcasted_iota(jnp.int32, (HALF, 1), 0))
        query = at.token(block, lax.broadcasted_iota(jnp.int32, (1, HALF), 1))
        mask = (key <= query) & (key >= at.first_key(query))
        dkv[here] = attend_back(q, d_att, lse, delta, dq, block, here, kv[here], mask)
    load.wait()
    grads[...] = tn(pieces(dat[...], dato[...]), att[...]).astype(BF)
    started(grads, grads_h.at[:, :512], sem.at[1]).wait()


def query_back_body(
    ids, dq, normed_h, qraw, cos, sin, gq, wq, grads_in, grads_h, dn, gain, wq_v, normed, grads, sem
):
    copy = started(columns(wq, ids[0] & 1, 512), wq_v, sem.at[0])
    load = started(normed_h, normed, sem.at[1])
    cosine, sine = cos[...], sin[...]
    gain_sum, raw = 0.0, []
    for h in range(4):
        value = qraw[:, h * 128 : (h + 1) * 128].astype(F32)
        out, part = head_back(dq[h] * SCALE, value, gq[...], cosine, sine)
        gain_sum += part
        raw.append(out)
    gain[...] = gain_sum
    dq_raw = jnp.concatenate(raw, axis=1)
    load.wait()
    grads[...] = tn(normed[...], dq_raw).astype(BF)
    store = started(grads, grads_h.at[:, 512:], sem.at[2])
    copy.wait()
    dn[...] = nt(dq_raw, wq_v[...]).astype(BF)
    store.wait()


def key_back_body(
    ids, lengths, x_h, xo_h, ga, kraw, cos, sin, gk, wk, wv, dkv_in, dlast, r1, r2, r3, rr, dn_h, gain_q, gain_f, kept, s1, s2, s3, own, send, wk_v, wv_v, dkv, x, xo, dn, grads, sem
):
    at = Place(ids, lengths)
    copy_k = started(columns(wk, at.core, 256), wk_v, sem.at[0])
    copy_v = started(columns(wv, at.core, 256), wv_v, sem.at[1])
    loads = [
        started(source, target, sem.at[6 + n])
        for n, (source, target) in enumerate(((x_h, x), (xo_h, xo), (dn_h, dn)))
    ]
    dkv[...] = dkv_in[...]
    for step, pair in zip(STEPS, (r1, r2, r3)):
        dkv[rows_of(jnp.where(at.x + step < 4, 0, 1)), :] += pair[...].astype(F32)
    dkv[rows_of(at.y), :] += rr[...].astype(F32)
    row0 = pl.multiple_of(jnp.where(at.core == 1, 0, 128), 128)
    piece = dlast[...].astype(F32)
    dkv[pl.ds(row0, 128), :] += jnp.where(at.chip == CHIPS - 1, piece, jnp.zeros_like(piece))
    gain_k, raw = 0.0, []
    for h in range(2):
        head = slice(h * 128, (h + 1) * 128)
        out, part = head_back(dkv[:, head], kraw[:, head].astype(F32), gk[...], cos[...], sin[...])
        raw.append(out)
        gain_k += part
    dk_raw = jnp.concatenate(raw, axis=1)
    dv_raw = dkv[:, 256:512].astype(BF)
    for load in loads:
        load.wait()
    value = pieces(x[...], xo[...]).astype(F32)
    hat = value * inv_rms(value)
    out = tn((hat * ga[...]).astype(BF), jnp.concatenate([dk_raw, dv_raw], axis=1)).astype(BF)
    grads[:, :, :, :512] = out.reshape(8, 4, 32, 512)
    copy_k.wait()
    copy_v.wait()
    d_normed = dn[...].astype(F32) + nt(dk_raw, wk_v[...]) + nt(dv_raw, wv_v[...])
    gain_a = jnp.sum(d_normed * hat, axis=0, keepdims=True)
    split_rows(d_normed.astype(BF), own, send)
    gains = jnp.concatenate([gain_a, gain_f[...], gain_q[...], gain_k], axis=1)
    count = gains.shape[1]

    def spot(lane):
        wide = lane < 2048
        index = jnp.where(wide, lane & 1023, lane & 127)
        size = jnp.where(wide, 5, 2)
        base = jnp.where(lane < 1024, 0, jnp.where(wide, 32, jnp.where(lane < 2176, 64, 68)))
        return index >> size, base + (index & ((1 << size) - 1))

    holder, _ = spot(lax.broadcasted_iota(jnp.int32, (32, count), 1))
    _, lane = spot(lax.broadcasted_iota(jnp.int32, (count, 128), 0))
    held = holder == lax.broadcasted_iota(jnp.int32, (32, count), 0)
    fold = jnp.where(lane == lax.broadcasted_iota(jnp.int32, (count, 128), 1), 1.0, 0.0).astype(BF)
    picked = nn(jnp.where(held, gains, 0.0).astype(BF), fold)
    first = lax.broadcasted_iota(jnp.int32, (32, 128), 0) == 0
    for n in range(32):
        grads[n // 4, n % 4, :, 512:] = jnp.where(first, picked[n : n + 1], 0.0).astype(BF)
    for copy in spread(grads, lambda step: (slice(None), at.x + step & 3), (kept, s1, s2, s3), sem, 2):
        copy.wait()


def four(refs):
    a, b, c, d = (ref[...].astype(F32) for ref in refs)
    return (a + b) + (c + d)


def z_turn_body(ids, r0, r1, r2, r3, kept, s1, s2, s3, total, sem):
    z = ids[0] >> 4
    total[...] = four((r0, r1, r2, r3)).astype(BF).reshape(total.shape)
    for copy in spread(total, lambda step: z + step & 3, (kept, s1, s2, s3), sem):
        copy.wait()


def y_turn_body(ids, came, kept, send):
    y = ids[0] >> 3 & 1
    for n in range(2):
        part = (came[0, n].astype(F32) + came[1, n].astype(F32)) + (
            came[2, n].astype(F32) + came[3, n].astype(F32)
        )
        part = part.astype(BF)

        @pl.when(y == n)
        def _():
            kept[...] = part

        @pl.when(y != n)
        def _():
            send[...] = part


def x_turn_body(ids, own, came, kept, s1, s2, s3, total, sem):
    x = ids[0] >> 1 & 3
    total[...] = (own[...].astype(F32) + came[...].astype(F32)).astype(BF)
    for copy in spread(total, lambda step: x + step & 3, (kept, s1, s2, s3), sem):
        copy.wait()


def halve_body(ids, *refs):
    y = ids[0] >> 3 & 1
    own, send = refs[-2:]
    at = 0
    for n in range(0, len(refs) - 2, 4):
        part = four(refs[n : n + 4])
        size = part.shape[2]
        own[:, at : at + size] = jnp.where(y == 0, part[0], part[1])
        send[:, at : at + size] = jnp.where(y == 0, part[1], part[0]).astype(BF)
        at += size


def sum_body(ids, *refs):
    mine, theirs, kept, given, gains = refs[8:]
    core = ids[0] & 1
    row = lax.broadcasted_iota(jnp.int32, (16, 128), 0)
    at = 0
    for total in (four(refs[0:4]), four(refs[4:8]), mine[...] + theirs[...].astype(F32)):
        size = total.shape[1]
        kept[:, at : at + size] = jnp.where(core == 0, total[:16], total[16:])
        given[:, at : at + size] = jnp.where(core == 0, total[16:], total[:16])
        at += size
    gain = total[0:1, size - 128 :]
    gains[...] = gain
    given[:, at - 128 :] = jnp.where(row == 0, gain, 0.0)


def final_body(ids, kept, taken, own, by_tensor, by_both, *outs):
    core = ids[0] & 1
    mine, theirs = kept[...], taken[...]
    low = jnp.where(core == 0, mine, theirs)
    high = jnp.where(core == 0, theirs, mine)
    at = 0
    for out in outs[:-1]:
        size = out.shape[1] // 2
        out[:, :size], out[:, size:] = low[:, at : at + size], high[:, at : at + size]
        at += size
    pair = own[...] + taken[0:1, taken.shape[1] - 128 :]
    both = pair + (by_tensor[...] + by_both[...])
    lane = lax.broadcasted_iota(jnp.int32, (1, 128), 1)
    total = jnp.where((lane >= 32) & (lane < 64), pair, both)
    for row, (first, size) in enumerate(((0, 16), (32, 16), (64, 2), (68, 2))):
        part = jnp.where(core == 0, total, pltpu.roll(total, 128 - size, 1))
        outs[-1][row : row + 1] = pltpu.roll(part, (128 - first) % 128, 1) if first else part
    outs[-1][4:8] = jnp.zeros((4, 128), F32)


def reduced(own, received):
    part = lax.optimization_barrier((own.astype(F32) + received.astype(F32)).astype(BF))
    return part, tensor_swap(part)


def local(
    layer_input,
    doc_lengths,
    gain_attn,
    w_query,
    w_key,
    w_value,
    gain_query,
    gain_key,
    w_output,
    gain_ffn,
    w_gate,
    w_up,
    w_down,
    cotangent,
):
    dp = lax.axis_index("dp")
    core, chip = dp % 2, dp // 2 % CHIPS
    where = (jnp.reshape(dp, (1,)).astype(jnp.int32), pinned(doc_lengths))
    width = w_gate.shape[1] // 2
    x, dy = layer_input, cotangent
    xo = core_swap(x)
    w_query, w_key, w_value, w_output, w_gate, w_up, w_down = map(
        pinned, (w_query, w_key, w_value, w_output, w_gate, w_up, w_down)
    )
    gf = gain_ffn[None, :]
    ga, gq, gk = pinned(gain_attn[None, :]), pinned(gain_query[None, :]), pinned(gain_key[None, :])
    freqs = np.exp(np.arange(64) * (-2.0 * math.log(ROPE_BASE) / HEAD))
    angles = np.tile(np.arange(128)[:, None] * freqs[None, :], (1, 2))
    tab_c, tab_s = pinned(jnp.asarray(np.cos(angles), F32)), pinned(jnp.asarray(np.sin(angles), F32))
    dma = pltpu.SemaphoreType.DMA
    vmem = pltpu.VMEM
    block = shape((HALF, 512))
    token_rows = shape((HALF, 1024))

    def halved(parts):
        width = sum(part.shape[-1] for part in parts[::4])
        own, send = call(
            halve_body,
            0.5,
            where[:1],
            parts,
            [None] * len(parts),
            [shape((32, width), F32), shape((32, width))],
            [None] * 2,
        )
        return own, y_swap(send)

    x15 = jnp.where(core == 1, x[:128], xo[:128])
    x15 = jnp.where(chip == CHIPS - 1, x15, jnp.zeros_like(x15))
    x15 = x15 + chip_links(x15, TREE[0])

    normed, kv, kraw, cosine, sine, s1, s2, s3, sr = call(
        key_value_body,
        2.4,
        where,
        [pinned(x), xo, ga, w_key, w_value, gk, tab_c, tab_s],
        [None, None, None, HBM, HBM, None, None, None],
        [stored((512, 1024)), stored((512, 512)), stored((512, 256))]
        + [stored((512, 128), F32)] * 2
        + [block] * 4,
        [None] * 5 + [HBM] * 4,
        [vmem((1024, 256), BF)] * 2 + [dma((6,))],
    )
    normed, kv, kraw, cosine, sine = map(pinned, (normed, kv, kraw, cosine, sine))
    rr = y_swap(sr)
    r1, r2, r3 = [x_shift(value, step) for step, value in zip(STEPS, (s1, s2, s3))]
    kv, x15 = lax.optimization_barrier((kv, x15))
    x15 = x15 + chip_links(x15, TREE[1])
    q, qraw, acc = call(
        query_body,
        4.5,
        where,
        [normed, w_query, gq, cosine, sine, kv],
        [None, HBM, None, None, None, None],
        [stored((4, 512, 128)), stored((512, 512)), shape((4, 512, 256), F32)],
        [None] * 3,
        [vmem((1024, 512), BF), dma((1,))],
    )
    q, qraw = pinned(q), pinned(qraw)
    rr, r1, r2, r3, x15, acc = lax.optimization_barrier((rr, r1, r2, r3, x15, acc))
    f1, f2, f3 = [x_shift(rr, step) for step in STEPS]
    x15 = x15 + chip_links(x15, TREE[2])
    starts = vmem((2, HALF, HALF), jnp.int32)
    acc, last = call(
        near_body,
        3,
        where,
        [q, acc, r1, r2, r3, rr, x15, ga, w_key, w_value, gk, tab_c, tab_s],
        [None] * 8 + [HBM, HBM] + [None] * 3,
        [shape((4, 512, 256), F32), stored((128, 512))],
        [None] * 2,
        [starts] + [vmem((1024, 256), BF)] * 2 + [dma((2,))],
    )
    att, lse, own, send = call(
        far_body,
        3.1,
        where,
        [q, acc, f1, f2, f3, w_output],
        [None] * 5 + [HBM],
        [stored((512, 512)), stored((8, 512), F32), token_rows, token_rows],
        [None] * 4,
        [vmem((4, 512, 256), F32), starts, vmem((512, 1024), BF), dma((1,))],
    )
    att, lse, last = pinned(att), pinned(lse), pinned(last)
    send, dy_late = lax.optimization_barrier((send, dy))
    part, other = reduced(own, core_swap(send))
    dyo = core_swap(dy_late)
    inputs = x.astype(F32)
    hidden = inputs + (part.astype(F32) + other.astype(F32))
    inv_mid = inv_rms(hidden)
    mid_hat = hidden * inv_mid
    mid = (mid_hat * gf).astype(BF)
    mido = core_swap(mid)

    dmid, dmids, y, ys, dgate, dup, act = call(
        ffn_body,
        9.9,
        where,
        [mid, mido, dy, dyo, w_gate, w_up, w_down],
        [None] * 4 + [HBM] * 3,
        [token_rows] * 4 + [shape((512, width))] * 3,
        [None] * 4 + [pl.BlockSpec((512, 256), lambda i, *_: (0, i))] * 3,
        [vmem((3, 1024, 256), BF)] * 2
        + [vmem((3, 256, 1024), BF)]
        + [vmem((512, 1024), BF)] * 2
        + [vmem((512, 1024), F32)] * 2
        + [dma((3, 3))],
        grid=(3,),
        mib=28,
    )
    dpart, dother = reduced(dmid, core_swap(dmids))
    dpart, dgate, dup, act = lax.optimization_barrier((dpart, dgate, dup, act))
    part_width = 3 * width // 2
    chunk = pl.BlockSpec((HALF, 256), lambda i: (0, i), memory_space=pltpu.VMEM)
    (ffn_grads,) = call(
        ffn_grad_body,
        4,
        (),
        [mid, mido, dy, dyo, dgate, dup, act],
        [chunk] * 4 + [None] * 3,
        [stored((1024, 3 * width))],
        [pl.BlockSpec((256, 3 * width), lambda i: (i, 0), memory_space=pltpu.VMEM)],
        grid=(4,),
    )
    by_z = dp_groups(lambda core, x, y, z: (core, x, y))
    trade = lambda value: lax.all_to_all(value, "dp", 0, 0, axis_index_groups=by_z)
    early = trade(ffn_grads.reshape(4, 256, -1))
    dother, ffn_grads = lax.optimization_barrier((dother, ffn_grads))
    d_mid = dpart.astype(F32) + dother.astype(F32)
    gain_f = jnp.sum(d_mid * mid_hat, axis=0, keepdims=True)
    d_hidden = dy.astype(F32) + norm_back(d_mid, mid_hat, inv_mid, gf)
    d_attn = d_hidden.astype(BF)
    d_attno = core_swap(d_attn)

    rows8 = shape((2, 8, HALF), F32)
    d_att, lse, delta, dq, g1, g2, g3, glast = call(
        far_back_body,
        60,
        where,
        [d_attn, d_attno, w_output, q, att, lse, pinned(f1), pinned(f2), pinned(f3), last],
        [None, None, HBM, HBM, HBM, None] + [HBM] * 4,
        [shape((4, 512, 128)), rows8, rows8, shape((4, 512, 128), F32)] + [block] * 3 + [shape((128, 512))],
        [None] * 4 + [HBM] * 4,
        [vmem((512, 1024), BF), vmem((4, 512, 128), BF), vmem((512, 512), BF), vmem((3, HALF, 512), BF)]
        + [vmem((128, 512), BF), vmem((3, HALF, 512), BF), vmem((128, 512), BF), starts, dma((11,))],
    )
    back = [{b: a for a, b in links.items()} for links in TREE]
    g1, g2, g3, ys = lax.optimization_barrier((g1, g2, g3, ys))
    far = [x_shift(value, -step) for step, value in zip(STEPS, (g1, g2, g3))]
    y_part, y_other = reduced(y, core_swap(ys))
    dq, gr, g1, g2, g3 = call(
        near_back_body,
        6,
        where,
        [q, d_att, lse, delta, dq, pinned(r1), pinned(r2), pinned(r3), pinned(rr)],
        [None] * 9,
        [shape((4, 512, 128), F32), shape((HALF, 512))] + [block] * 3,
        [None, None] + [HBM] * 3,
        [vmem((3, HALF, 512), BF), starts, dma((3,))],
    )
    glast, dq = lax.optimization_barrier((glast, dq))
    glast = glast + chip_links(glast, back[2])
    dq, dkv, mid_grads = call(
        own_back_body,
        4,
        where,
        [q, kv, d_att, lse, delta, dq, d_attn, d_attno, att],
        [None] * 8 + [HBM],
        [shape((4, 512, 128), F32), stored((512, 512), F32), stored((1024, 1024))],
        [None, None, HBM],
        [vmem((512, 512), BF), vmem((1024, 512), BF), dma((2,))],
    )
    dkv = pinned(dkv)
    glast, g1, g2, g3, dkv, *far = lax.optimization_barrier((glast, g1, g2, g3, dkv, *far))
    near = [x_shift(value, -step) for step, value in zip(STEPS, (g1, g2, g3))]
    glast = glast + chip_links(glast, back[1])
    gr = (sum(value.astype(F32) for value in far) + gr.astype(F32)).astype(BF)
    gr, dq = lax.optimization_barrier((gr, dq))
    gr = y_swap(gr)
    glast = glast + chip_links(glast, back[0])
    mid_grads, dn, gain_q = call(
        query_back_body,
        8,
        where[:1],
        [dq, normed, qraw, cosine, sine, gq, w_query, pinned(mid_grads)],
        [None, HBM] + [None] * 4 + [HBM, HBM],
        [stored((1024, 1024)), stored((512, 1024)), shape((1, 128), F32)],
        [HBM, None, None],
        [vmem((1024, 512), BF), vmem((512, 1024), BF), vmem((1024, 512), BF), dma((3,))],
        aliases={8: 0},
    )
    dn = pinned(dn)
    def y_turn(total):
        size = total.shape[-1]
        kept, send = call(
            y_turn_body,
            1,
            where[:1],
            [pinned(total.reshape(4, 2, 4, 32, size))],
            [None],
            [shape((4, 32, size))] * 2,
            [None] * 2,
            mib=24,
        )
        return kept, y_swap(send)

    early, mid_grads = lax.optimization_barrier((early, mid_grads))
    early = y_turn(early)
    middle = trade(mid_grads.reshape(4, 256, -1))
    glast, y_other = lax.optimization_barrier((glast, y_other))
    x_kept, s1, s2, s3, own, send = call(
        key_back_body,
        60,
        where,
        [pinned(x), pinned(xo), ga, kraw, cosine, sine, gk, w_key, w_value, dkv, glast, *near, gr, dn, gain_q, gain_f],
        [HBM] * 2 + [None] * 5 + [HBM, HBM] + [None] * 6 + [HBM] + [None] * 2,
        [shape((8, 32, 640))] * 4 + [token_rows] * 2,
        [HBM] * 4 + [None] * 2,
        [vmem((1024, 256), BF)] * 2
        + [vmem((512, 512), F32), vmem((HALF, 1024), BF), vmem((HALF, 1024), BF), vmem((512, 1024), BF)]
        + [vmem((8, 4, 32, 640), BF), dma((9,))],
    )
    late = [x_shift(value, step) for step, value in zip(STEPS, (s1, s2, s3))]
    layer_output = (hidden + (y_part.astype(F32) + y_other.astype(F32))).astype(BF)
    part, other = reduced(own, core_swap(send))
    own, *early = lax.optimization_barrier((own, *early))

    def x_turn(kept, came):
        size = kept.shape[-1]
        parts = call(
            x_turn_body,
            1,
            where[:1],
            [kept, came],
            [None] * 2,
            [shape((32, size))] * 4,
            [HBM] * 4,
            [vmem((4, 32, size), BF), dma((4,))],
        )
        return [parts[0]] + [x_shift(value, step) for step, value in zip(STEPS, parts[1:])]

    early = x_turn(*early)
    other, x_kept = lax.optimization_barrier((other, x_kept))
    late = call(
        z_turn_body,
        1,
        where[:1],
        [x_kept, *late],
        [None] * 4,
        [shape((2, 32, 640))] * 4,
        [HBM] * 4,
        [vmem((4, 2, 32, 640), BF), dma((4,))],
    )
    late = [late[0]] + [z_shift(value, step) for step, value in zip(STEPS, late[1:])]
    middle = x_turn(*y_turn(middle))
    mine, theirs = halved(late)
    count = 3 * width + 1024 + 640
    kept, given, gains = call(
        sum_body,
        1,
        where[:1],
        [*early, *middle, mine, theirs],
        [None] * 10,
        [shape((16, count), F32)] * 2 + [shape((1, 128), F32)],
        [None] * 3,
    )
    both = lax.ppermute(
        gains,
        ("dp", "tensor"),
        [(i * 2 + t, (i ^ 1) * 2 + 1 - t) for i in range(64) for t in range(2)],
    )
    widths = [2 * width, 2 * width, 2 * width, 1024, 1024, 512, 512]
    grad_gate, grad_up, grad_down, grad_output, grad_query, grad_key, grad_value, gains = call(
        final_body,
        1.4,
        where[:1],
        [kept, core_swap(given), gains, tensor_swap(gains), both],
        [None] * 5,
        [shape((16, n), F32) for n in widths] + [shape((8, 128), F32)],
        [None] * 8,
    )

    d_normed = part.astype(F32) + other.astype(F32)
    inv_in = inv_rms(inputs)
    grad_input = d_hidden + norm_back(d_normed, inputs * inv_in, inv_in, gain_attn[None, :])
    return (
        layer_output,
        grad_input,
        gains[0, :16],
        grad_query,
        grad_key,
        grad_value,
        gains[2, :2],
        gains[3, :2],
        jnp.transpose(grad_output),
        gains[1, :16],
        grad_gate,
        grad_up,
        jnp.transpose(grad_down),
    )


def solution(mesh):
    placed = (
        P("dp", None),
        P(),
        P(),
        P(None, "tensor"),
        P(None, "tensor"),
        P(None, "tensor"),
        P(),
        P(),
        P("tensor", None),
        P(),
        P(None, "tensor"),
        P(None, "tensor"),
        P("tensor", None),
        P("dp", None),
    )
    return jax.shard_map(
        local,
        mesh=mesh,
        in_specs=placed,
        out_specs=(
            P("dp", None),
            P("dp", None),
            P("dp"),
            P("dp", "tensor"),
            P("dp", "tensor"),
            P("dp", "tensor"),
            P("dp"),
            P("dp"),
            P("tensor", "dp"),
            P("dp"),
            P("dp", "tensor"),
            P("dp", "tensor"),
            P("tensor", "dp"),
        ),
        check_vma=False,
    )
```

```python
import functools
import math

import jax
import jax.numpy as jnp
import numpy as np
from jax import lax
from jax.experimental import pallas as pl
from jax.experimental.pallas import tpu as pltpu
from jax.sharding import PartitionSpec as P

EPS = 1e-06
COST = 1.15e9
ROPE_BASE = 1000000.0
HEAD = 128
HALF = 256
SCALE = HEAD ** (-0.5)
SCALE2 = SCALE * math.log2(math.e)
CHIPS = 8
LAST_START = 1920
STEPS = (1, 2, 3)
BF = jnp.bfloat16
F32 = jnp.float32


def dp_index(core, x, y, z):
    return core | x << 1 | y << 3 | z << 4


def dp_pairs(target):
    return [
        (dp_index(core, x, y, z), dp_index(*target(core, x, y, z)))
        for core in range(2)
        for x in range(4)
        for y in range(2)
        for z in range(4)
        if target(core, x, y, z) is not None
    ]


def core_swap(value):
    return lax.ppermute(value, "dp", dp_pairs(lambda core, x, y, z: (1 - core, x, y, z)))


def tensor_swap(value):
    return lax.ppermute(value, "tensor", [(0, 1), (1, 0)])


def x_shift(value, step):
    return lax.ppermute(
        value, "dp", dp_pairs(lambda core, x, y, z: (core, (x + step) % 4, y, z))
    )


def y_swap(value):
    return lax.ppermute(value, "dp", dp_pairs(lambda core, x, y, z: (core, x, 1 - y, z)))


def x_pair(value, bits):
    return lax.ppermute(value, "dp", dp_pairs(lambda core, x, y, z: (core, x ^ bits, y, z)))


def z_pair(value, bits):
    return lax.ppermute(value, "dp", dp_pairs(lambda core, x, y, z: (core, x, y, z ^ bits)))


def z_shift(value, step):
    return lax.ppermute(
        value, "dp", dp_pairs(lambda core, x, y, z: (core, x, y, (z + step) % 4))
    )


def chip_links(value, links, cores=(0, 1)):
    def target(core, x, y, z):
        chip = links.get(y * 4 + x)
        return None if chip is None or core not in cores else (core, chip % 4, chip // 4, z)

    return lax.ppermute(value, "dp", dp_pairs(target))


def dp_groups(key):
    groups = {}
    for index in range(64):
        core, x, y, z = index & 1, index >> 1 & 3, index >> 3 & 1, index >> 4
        groups.setdefault(key(core, x, y, z), []).append(index)
    return list(groups.values())


TREE = ({7: 3}, {7: 5, 3: 1}, {7: 6, 5: 4, 3: 2, 1: 0})


def nn(left, right):
    return lax.dot_general(left, right, (((1,), (0,)), ((), ())), preferred_element_type=F32)


def nt(left, right):
    return lax.dot_general(left, right, (((1,), (1,)), ((), ())), preferred_element_type=F32)


def tn(left, right):
    return lax.dot_general(left, right, (((0,), (0,)), ((), ())), preferred_element_type=F32)


def inv_rms(values):
    return lax.rsqrt(jnp.mean(values * values, axis=-1, keepdims=True) + EPS)


def norm_back(grad, normal, inverse, gain):
    scaled = grad * gain
    return inverse * (scaled - normal * jnp.mean(scaled * normal, axis=-1, keepdims=True))


class Place:
    def __init__(self, ids, lengths):
        dp = ids[0]
        self.core, self.x, self.y, self.z = dp & 1, dp >> 1 & 3, dp >> 3 & 1, dp >> 4
        self.chip = self.y * 4 + self.x
        first = lengths[self.z, 0]
        second = first + lengths[self.z, 1]
        self.starts = (first, second, second + lengths[self.z, 2])

    def first_key(self, token):
        start = jnp.zeros_like(token)
        for end in self.starts:
            start = jnp.where(token >= end, end, start)
        return start

    def token(self, block, offset):
        if block == 0:
            return self.chip * HALF + (offset ^ (self.core * 128))
        return (15 - self.chip) * HALF + (offset ^ ((1 - self.core) * 128))

    def row_block(self, step):
        lower = step <= self.x
        sel = jnp.where(lower, 0, 1)

        def keys(offset):
            token = (self.chip - step) * HALF + (offset ^ (self.core * 128))
            return jnp.where(lower, token, LAST_START + 128)

        return sel, keys

    def far_block(self, step):
        source = (self.x - step) & 3

        def keys(offset):
            token = source * HALF + (offset ^ (self.core * 128))
            return jnp.where(self.y == 1, token, LAST_START + 128)

        return 1 - self.y, keys


def rows_of(sel):
    return pl.ds(pl.multiple_of(sel * HALF, HALF), HALF)


def full(shape):
    return pl.BlockSpec(shape, lambda *args: (0,) * len(shape), memory_space=pltpu.VMEM)


HBM = pl.BlockSpec(memory_space=pltpu.HBM)


def pinned(value):
    return pltpu.with_memory_space_constraint(value, pltpu.HBM)


def call(body, cost_us, prefetch, args, specs, outs, out_specs, scratch=(), grid=(1,), mib=16, aliases={}):
    return pl.pallas_call(
        body,
        grid_spec=pltpu.PrefetchScalarGridSpec(
            num_scalar_prefetch=len(prefetch),
            grid=grid,
            in_specs=[full(a.shape) if spec is None else spec for a, spec in zip(args, specs)],
            out_specs=[full(o.shape) if spec is None else spec for o, spec in zip(outs, out_specs)],
            scratch_shapes=list(scratch),
        ),
        out_shape=outs,
        compiler_params=pltpu.CompilerParams(vmem_limit_bytes=mib * 2**20),
        cost_estimate=pl.CostEstimate(flops=int(cost_us * COST), bytes_accessed=1, transcendentals=0),
        input_output_aliases=aliases,
    )(*prefetch, *args)


def shape(dims, kind=BF):
    return jax.ShapeDtypeStruct(dims, kind)


def stored(dims, kind=BF):
    return pltpu.HBM(dims, kind)


def columns(ref, core, size):
    return ref.at[:, pl.ds(pl.multiple_of(core * size, size), size)]


def rows(ref, core, size):
    return ref.at[pl.ds(pl.multiple_of(core * size, size), size), :]


def started(source, target, sem):
    copy = pltpu.make_async_copy(source, target, sem)
    copy.start()
    return copy


def pieces(own, other):
    return jnp.concatenate([own[0:128], other[0:128], own[128:256], other[128:256]], axis=0)


def split_rows(value, own, other):
    own[0:128], other[0:128] = value[0:128], value[128:256]
    own[128:256], other[128:256] = value[256:384], value[384:512]


def turned(value, gain, cosine, sine):
    w = value * inv_rms(value) * gain
    return (w * cosine + pltpu.roll(w, 64, 1) * sine).astype(BF)


def key_value_body(
    ids, lengths, x, xo, ga, wk, wv, gk, tab_c, tab_s, normed, kv, kraw, cos, sin, s1, s2, s3, sr, wk_v, wv_v, sem
):
    at = Place(ids, lengths)
    copy_k = started(columns(wk, at.core, 256), wk_v, sem.at[0])
    copy_v = started(columns(wv, at.core, 256), wv_v, sem.at[1])
    row = lax.broadcasted_iota(jnp.int32, (1, 128), 1)
    freq = jnp.exp((row & 63).astype(F32) * (-2.0 * math.log(ROPE_BASE) / HEAD))
    offset = lax.broadcasted_iota(jnp.int32, (128, 128), 0)
    tab_c, tab_s = tab_c[...], tab_s[...]
    for piece in range(4):
        base = at.token(piece // 2, jnp.int32(piece % 2 * 128))
        start = at.first_key(base + offset)
        shift_c = shift_s = None
        for first in (jnp.int32(0),) + at.starts:
            angle = (base - first).astype(F32) * freq
            c, s = jnp.cos(angle), jnp.sin(angle)
            if shift_c is None:
                shift_c, shift_s = jnp.broadcast_to(c, (128, 128)), jnp.broadcast_to(s, (128, 128))
            else:
                shift_c = jnp.where(start == first, c, shift_c)
                shift_s = jnp.where(start == first, s, shift_s)
        cos[piece * 128 : (piece + 1) * 128] = shift_c * tab_c - shift_s * tab_s
        sine = shift_s * tab_c + shift_c * tab_s
        sin[piece * 128 : (piece + 1) * 128] = jnp.where(row < 64, -sine, sine)
    for block in range(2):
        cut = slice(block * 128, (block + 1) * 128)
        here = slice(block * HALF, (block + 1) * HALF)
        value = jnp.concatenate([x[cut], xo[cut]], axis=0).astype(F32)
        n = (value * inv_rms(value) * ga[...]).astype(BF)
        normed[here] = n
        if block == 0:
            copy_k.wait()
            copy_v.wait()
        raw = nn(n, wk_v[...])
        kraw[here] = raw.astype(BF)
        for h in range(2):
            head = slice(h * 128, (h + 1) * 128)
            kv[here, head] = turned(raw[:, head], gk[...], cos[here], sin[here])
        kv[here, 256:] = nn(n, wv_v[...]).astype(BF)
    copies = [
        started(kv.at[rows_of(jnp.where(at.x + step < 4, 0, 1))], out, sem.at[1 + step])
        for step, out in zip(STEPS, (s1, s2, s3))
    ]
    copies.append(started(kv.at[rows_of(at.y)], sr, sem.at[5]))
    for copy in copies:
        copy.wait()


def attend(q, acc, where, pair, mask):
    ones = jnp.ones((pair.shape[0], 128), BF)
    for h in range(4):
        g = h // 2
        keys = pair[:, g * 128 : (g + 1) * 128]
        values = pair[:, 256 + g * 128 : 256 + (g + 1) * 128]
        weights = jnp.exp2(nt(q[h, where, :], keys) * SCALE2)
        if mask is not None:
            weights = jnp.where(mask, weights, 0.0)
        acc[h, where, :] += nn(weights.astype(BF), jnp.concatenate([values, ones], axis=1))


def query_body(
    ids, lengths, normed, wq, gq, cos, sin, kv, q, qraw, acc, wq_v, sem
):
    at = Place(ids, lengths)
    copy = started(columns(wq, at.core, 512), wq_v, sem.at[0])
    acc[...] = jnp.zeros_like(acc)
    copy.wait()
    for block in range(2):
        here = slice(block * HALF, (block + 1) * HALF)
        raw = nn(normed[here], wq_v[...])
        qraw[here] = raw.astype(BF)
        for h in range(4):
            q[h, here] = turned(raw[:, h * 128 : (h + 1) * 128], gq[...], cos[here], sin[here])
        query = at.token(block, lax.broadcasted_iota(jnp.int32, (HALF, 1), 0))
        key = at.token(block, lax.broadcasted_iota(jnp.int32, (1, HALF), 1))
        attend(q, acc, here, kv[here], (key <= query) & (key >= at.first_key(query)))


def set_starts(at, start, dim):
    for block in range(2):
        start[block] = at.first_key(at.token(block, lax.broadcasted_iota(jnp.int32, (HALF, HALF), dim)))


def near_body(
    ids, lengths, q, acc_in, r1, r2, r3, rr, x15, ga, wk, wv, gk, tab_c, tab_s, acc, last, start, wk_v, wv_v, sem
):
    at = Place(ids, lengths)
    copy_k = started(columns(wk, at.core, 256), wk_v, sem.at[0])
    copy_v = started(columns(wv, at.core, 256), wv_v, sem.at[1])
    acc[...] = acc_in[...]
    set_starts(at, start, 0)
    offset = lax.broadcasted_iota(jnp.int32, (1, HALF), 1)
    for step, pair in zip(STEPS, (r1, r2, r3)):
        sel, keys = at.row_block(step)
        attend(q, acc, rows_of(sel), pair[...], keys(offset) >= start[sel])
    sel, keys = at.far_block(0)
    attend(q, acc, rows_of(sel), rr[...], keys(offset) >= start[sel])
    value = x15[...].astype(F32)
    n = (value * inv_rms(value) * ga[...]).astype(BF)
    copy_k.wait()
    copy_v.wait()
    raw = nn(n, wk_v[...])
    sine = tab_s[...]
    sine = jnp.where(lax.broadcasted_iota(jnp.int32, (1, 128), 1) < 64, -sine, sine)
    for h in range(2):
        head = slice(h * 128, (h + 1) * 128)
        last[:, head] = turned(raw[:, head], gk[...], tab_c[...], sine)
    last[:, 256:] = nn(n, wv_v[...]).astype(BF)
    attend(q, acc, pl.ds(HALF, HALF), last[...], None)


def far_body(ids, lengths, q, acc_in, r1, r2, r3, wo, att, lse, own, send, acc, start, wo_v, sem):
    at = Place(ids, lengths)
    copy = started(rows(wo, at.core, 512), wo_v, sem.at[0])
    acc[...] = acc_in[...]
    set_starts(at, start, 0)
    offset = lax.broadcasted_iota(jnp.int32, (1, HALF), 1)
    for step, pair in zip(STEPS, (r1, r2, r3)):
        sel, keys = at.far_block(step)
        attend(q, acc, rows_of(sel), pair[...], keys(offset) >= start[sel])
    for h in range(4):
        total = acc[h, :, 128:]
        att[:, h * 128 : (h + 1) * 128] = (acc[h, :, :128] / total).astype(BF)
        lse[h : h + 1] = jnp.log2(jnp.transpose(total)[0:1])
    lse[4:8] = jnp.zeros((4, 2 * HALF), F32)
    copy.wait()
    split_rows(nn(att[...], wo_v[...]).astype(BF), own, send)


def ffn_body(
    ids, mid, mido, dy, dyo, wg, wu, wd, dmid, dmids, y, ys, dgate, dup, act, wg_v, wu_v, wd_v, sem
):
    copies = []
    for n in range(3):
        cut = pl.multiple_of((ids[0] & 1) * 768 + n * 256, 256)
        here = slice(n * 256, (n + 1) * 256)
        copies.append(
            [
                started(wg.at[:, pl.ds(cut, 256)], wg_v.at[:, here], sem.at[n, 0]),
                started(wu.at[:, pl.ds(cut, 256)], wu_v.at[:, here], sem.at[n, 1]),
                started(wd.at[pl.ds(cut, 256), :], wd_v.at[here], sem.at[n, 2]),
            ]
        )
    mid_all = jnp.concatenate([mid[...], mido[...]], axis=0)
    dy_all = jnp.concatenate([dy[...], dyo[...]], axis=0)
    for n in range(3):
        here = slice(n * 256, (n + 1) * 256)
        for copy in copies[n]:
            copy.wait()
        gate = nn(mid_all, wg_v[:, here])
        up = nn(mid_all, wu_v[:, here])
        d_act = nt(dy_all, wd_v[here])
        sigma = 1.0 / (1.0 + jnp.exp(-gate))
        silu = gate * sigma
        act[:, here] = (silu * up).astype(BF)
        dgate[:, here] = (d_act * up * sigma * (1.0 + gate * (1.0 - sigma))).astype(BF)
        dup[:, here] = (d_act * silu).astype(BF)
    out = (nt(dgate[...], wg_v[...]) + nt(dup[...], wu_v[...])).astype(BF)
    dmid[...], dmids[...] = out[:HALF], out[HALF:]
    out = nn(act[...], wd_v[...]).astype(BF)
    y[...], ys[...] = out[:HALF], out[HALF:]


def ffn_grad_body(mid, mido, dy, dyo, dgate, dup, act, out):
    width = dgate.shape[1]
    left = jnp.concatenate([mid[...], mido[...]], axis=0)
    out[:, :width] = tn(left, dgate[...]).astype(BF)
    out[:, width : 2 * width] = tn(left, dup[...]).astype(BF)
    left = jnp.concatenate([dy[...], dyo[...]], axis=0)
    out[:, 2 * width :] = tn(left, act[...]).astype(BF)


def spread(grads, at, outs, sem, first=0):
    return [
        started(grads.at[at(step)], out, sem.at[first + step])
        for step, out in zip((0,) + STEPS, outs)
    ]


def attend_back(q, d_att, lse, delta, dq, sel, where, pair, mask):
    key_grads, value_grads = [], []
    for g in range(2):
        keys = pair[:, g * 128 : (g + 1) * 128]
        values = pair[:, 256 + g * 128 : 256 + (g + 1) * 128]
        key_grad = value_grad = 0.0
        for h in (2 * g, 2 * g + 1):
            query, upper = q[h, where, :], d_att[h, where, :]
            weights = jnp.exp2(nt(keys, query) * SCALE2 - lse[sel, h : h + 1])
            if mask is not None:
                weights = jnp.where(mask, weights, 0.0)
            d_score = (weights * (nt(values, upper) - delta[sel, h : h + 1])).astype(BF)
            value_grad += nn(weights.astype(BF), upper)
            key_grad += nn(d_score, query)
            dq[h, where, :] += tn(d_score, keys)
        key_grads.append(key_grad * SCALE)
        value_grads.append(value_grad)
    return jnp.concatenate(key_grads + value_grads, axis=1)


def far_back_body(
    ids, lengths, dat_h, dato_h, wo, q_h, att_h, lse_in, r1, r2, r3, last_h, d_att, lse, delta, dq, g1, g2, g3, glast, wo_v, q, att, far_v, last, dat, dato, stage, stage_last, start, sem
):
    at = Place(ids, lengths)
    copy = started(rows(wo, at.core, 512), wo_v, sem.at[0])
    first = [started(dat_h, dat, sem.at[11]), started(dato_h, dato, sem.at[12])]
    loads = [
        started(source, target, sem.at[5 + n])
        for n, (source, target) in enumerate(
            ((att_h, att), (q_h, q), (last_h, last), (r1, far_v.at[0]), (r2, far_v.at[1]), (r3, far_v.at[2]))
        )
    ]
    set_starts(at, start, 1)
    dq[...] = jnp.zeros_like(dq)
    first[0].wait()
    first[1].wait()
    d_attn = pieces(dat[...], dato[...])
    copy.wait()
    grad = nt(d_attn, wo_v[...]).astype(BF)
    lse[...] = jnp.zeros_like(lse)
    delta[...] = jnp.zeros_like(delta)
    loads[0].wait()
    for h in range(4):
        part = grad[:, h * 128 : (h + 1) * 128]
        d_att[h] = part
        prod = part.astype(F32) * att[:, h * 128 : (h + 1) * 128].astype(F32)
        total = jnp.sum(jnp.transpose(prod), axis=0, keepdims=True)
        for block in range(2):
            cut = slice(block * HALF, (block + 1) * HALF)
            delta[block, h : h + 1] = total[:, cut]
            lse[block, h : h + 1] = lse_in[h : h + 1, cut]
    loads[1].wait()
    loads[2].wait()
    out = attend_back(q, d_att, lse, delta, dq, 1, pl.ds(HALF, HALF), last[...], None)
    stage_last[...] = out.astype(BF)
    copies = [started(stage_last, glast, sem.at[1])]
    offset = lax.broadcasted_iota(jnp.int32, (HALF, 1), 0)
    for step, target in zip(STEPS, (g1, g2, g3)):
        sel, keys = at.far_block(step)
        loads[2 + step].wait()
        pair = far_v[step - 1]
        out = attend_back(q, d_att, lse, delta, dq, sel, rows_of(sel), pair, keys(offset) >= start[sel])
        stage[step - 1] = out.astype(BF)
        copies.append(started(stage.at[step - 1], target, sem.at[1 + step]))
    for copy in copies:
        copy.wait()


def near_back_body(
    ids, lengths, q_h, d_att, lse, delta, dq_in, r1, r2, r3, rr, dq, gr, g1, g2, g3, q, near_v, stage, start, sem
):
    at = Place(ids, lengths)
    loads = [
        started(source, target, sem.at[3 + n])
        for n, (source, target) in enumerate(
            ((q_h, q), (rr, near_v.at[0]), (r1, near_v.at[1]), (r2, near_v.at[2]), (r3, near_v.at[3]))
        )
    ]
    set_starts(at, start, 1)
    dq[...] = dq_in[...]
    loads[0].wait()
    loads[1].wait()
    offset = lax.broadcasted_iota(jnp.int32, (HALF, 1), 0)
    copies = []
    sel, keys = at.far_block(0)
    out = attend_back(q, d_att, lse, delta, dq, sel, rows_of(sel), near_v[0], keys(offset) >= start[sel])
    gr[...] = out.astype(BF)
    for step, target in zip(STEPS, (g1, g2, g3)):
        sel, keys = at.row_block(step)
        loads[1 + step].wait()
        out = attend_back(q, d_att, lse, delta, dq, sel, rows_of(sel), near_v[step], keys(offset) >= start[sel])
        stage[step - 1] = out.astype(BF)
        copies.append(started(stage.at[step - 1], target, sem.at[step - 1]))
    for copy in copies:
        copy.wait()


def head_back(grad, value, gain, cosine, sine):
    turned_back = grad * cosine + pltpu.roll(grad * sine, 64, 1)
    inverse = inv_rms(value)
    hat = value * inverse
    gain_part = jnp.sum(turned_back * hat, axis=0, keepdims=True)
    return norm_back(turned_back, hat, inverse, gain).astype(BF), gain_part


def own_back_body(
    ids, lengths, q, kv, d_att, lse, delta, dq_in, dat, dato, att_h, dq, dkv, grads_h, att, grads, sem
):
    at = Place(ids, lengths)
    load = started(att_h, att, sem.at[0])
    dq[...] = dq_in[...]
    for block in range(2):
        here = slice(block * HALF, (block + 1) * HALF)
        key = at.token(block, lax.broadcasted_iota(jnp.int32, (HALF, 1), 0))
        query = at.token(block, lax.broadcasted_iota(jnp.int32, (1, HALF), 1))
        mask = (key <= query) & (key >= at.first_key(query))
        dkv[here] = attend_back(q, d_att, lse, delta, dq, block, here, kv[here], mask)
    load.wait()
    grads[...] = tn(pieces(dat[...], dato[...]), att[...]).astype(BF)
    started(grads, grads_h.at[:, :512], sem.at[1]).wait()


def query_back_body(
    ids, dq, normed_h, qraw, cos, sin, gq, wq, grads_in, grads_h, dn, gain, wq_v, normed, grads, sem
):
    copy = started(columns(wq, ids[0] & 1, 512), wq_v, sem.at[0])
    load = started(normed_h, normed, sem.at[1])
    cosine, sine = cos[...], sin[...]
    gain_sum, raw = 0.0, []
    for h in range(4):
        value = qraw[:, h * 128 : (h + 1) * 128].astype(F32)
        out, part = head_back(dq[h] * SCALE, value, gq[...], cosine, sine)
        gain_sum += part
        raw.append(out)
    gain[...] = gain_sum
    dq_raw = jnp.concatenate(raw, axis=1)
    load.wait()
    grads[...] = tn(normed[...], dq_raw).astype(BF)
    store = started(grads, grads_h.at[:, 512:], sem.at[2])
    copy.wait()
    dn[...] = nt(dq_raw, wq_v[...]).astype(BF)
    store.wait()


def key_back_body(
    ids, lengths, x_h, xo_h, ga, kraw, cos, sin, gk, wk, wv, dkv_in, dlast, r1, r2, r3, rr, dn_h, gain_q, gain_f, kept, s1, s2, s3, own, send, wk_v, wv_v, dkv, x, xo, dn, grads, sem
):
    at = Place(ids, lengths)
    copy_k = started(columns(wk, at.core, 256), wk_v, sem.at[0])
    copy_v = started(columns(wv, at.core, 256), wv_v, sem.at[1])
    loads = [
        started(source, target, sem.at[6 + n])
        for n, (source, target) in enumerate(((x_h, x), (xo_h, xo), (dn_h, dn)))
    ]
    dkv[...] = dkv_in[...]
    for step, pair in zip(STEPS, (r1, r2, r3)):
        dkv[rows_of(jnp.where(at.x + step < 4, 0, 1)), :] += pair[...].astype(F32)
    dkv[rows_of(at.y), :] += rr[...].astype(F32)
    row0 = pl.multiple_of(jnp.where(at.core == 1, 0, 128), 128)
    piece = dlast[...].astype(F32)
    dkv[pl.ds(row0, 128), :] += jnp.where(at.chip == CHIPS - 1, piece, jnp.zeros_like(piece))
    gain_k, raw = 0.0, []
    for h in range(2):
        head = slice(h * 128, (h + 1) * 128)
        out, part = head_back(dkv[:, head], kraw[:, head].astype(F32), gk[...], cos[...], sin[...])
        raw.append(out)
        gain_k += part
    dk_raw = jnp.concatenate(raw, axis=1)
    dv_raw = dkv[:, 256:512].astype(BF)
    for load in loads:
        load.wait()
    value = pieces(x[...], xo[...]).astype(F32)
    hat = value * inv_rms(value)
    out = tn((hat * ga[...]).astype(BF), jnp.concatenate([dk_raw, dv_raw], axis=1)).astype(BF)
    grads[:, :, :, :512] = out.reshape(8, 4, 32, 512)
    copy_k.wait()
    copy_v.wait()
    d_normed = dn[...].astype(F32) + nt(dk_raw, wk_v[...]) + nt(dv_raw, wv_v[...])
    gain_a = jnp.sum(d_normed * hat, axis=0, keepdims=True)
    split_rows(d_normed.astype(BF), own, send)
    gains = jnp.concatenate([gain_a, gain_f[...], gain_q[...], gain_k], axis=1)
    count = gains.shape[1]

    def spot(lane):
        wide = lane < 2048
        index = jnp.where(wide, lane & 1023, lane & 127)
        size = jnp.where(wide, 5, 2)
        base = jnp.where(lane < 1024, 0, jnp.where(wide, 32, jnp.where(lane < 2176, 64, 68)))
        return index >> size, base + (index & ((1 << size) - 1))

    holder, _ = spot(lax.broadcasted_iota(jnp.int32, (32, count), 1))
    _, lane = spot(lax.broadcasted_iota(jnp.int32, (count, 128), 0))
    held = holder == lax.broadcasted_iota(jnp.int32, (32, count), 0)
    fold = jnp.where(lane == lax.broadcasted_iota(jnp.int32, (count, 128), 1), 1.0, 0.0).astype(BF)
    picked = nn(jnp.where(held, gains, 0.0).astype(BF), fold)
    first = lax.broadcasted_iota(jnp.int32, (32, 128), 0) == 0
    for n in range(32):
        grads[n // 4, n % 4, :, 512:] = jnp.where(first, picked[n : n + 1], 0.0).astype(BF)
    for copy in spread(grads, lambda step: (slice(None), at.x + step & 3), (kept, s1, s2, s3), sem, 2):
        copy.wait()


def four(refs):
    a, b, c, d = (ref[...].astype(F32) for ref in refs)
    return (a + b) + (c + d)


def z_turn_body(ids, r0, r1, r2, r3, kept, s1, s2, s3, total, sem):
    z = ids[0] >> 4
    total[...] = four((r0, r1, r2, r3)).astype(BF).reshape(total.shape)
    for copy in spread(total, lambda step: z + step & 3, (kept, s1, s2, s3), sem):
        copy.wait()


def y_turn_body(ids, came, kept, send):
    y = ids[0] >> 3 & 1
    for n in range(2):
        part = (came[0, n].astype(F32) + came[1, n].astype(F32)) + (
            came[2, n].astype(F32) + came[3, n].astype(F32)
        )
        part = part.astype(BF)

        @pl.when(y == n)
        def _():
            kept[...] = part

        @pl.when(y != n)
        def _():
            send[...] = part


def x_turn_body(ids, own, came, kept, s1, s2, s3, total, sem):
    x = ids[0] >> 1 & 3
    total[...] = (own[...].astype(F32) + came[...].astype(F32)).astype(BF)
    for copy in spread(total, lambda step: x + step & 3, (kept, s1, s2, s3), sem):
        copy.wait()


def halve_body(ids, *refs):
    y = ids[0] >> 3 & 1
    own, send = refs[-2:]
    at = 0
    for n in range(0, len(refs) - 2, 4):
        part = four(refs[n : n + 4])
        size = part.shape[2]
        own[:, at : at + size] = jnp.where(y == 0, part[0], part[1])
        send[:, at : at + size] = jnp.where(y == 0, part[1], part[0]).astype(BF)
        at += size


def sum_body(ids, *refs):
    mine, theirs, kept, given, gains = refs[8:]
    core = ids[0] & 1
    row = lax.broadcasted_iota(jnp.int32, (16, 128), 0)
    at = 0
    for total in (four(refs[0:4]), four(refs[4:8]), mine[...] + theirs[...].astype(F32)):
        size = total.shape[1]
        kept[:, at : at + size] = jnp.where(core == 0, total[:16], total[16:])
        given[:, at : at + size] = jnp.where(core == 0, total[16:], total[:16])
        at += size
    gain = total[0:1, size - 128 :]
    gains[...] = gain
    given[:, at - 128 :] = jnp.where(row == 0, gain, 0.0)


def final_body(ids, kept, taken, own, by_tensor, by_both, *outs):
    core = ids[0] & 1
    mine, theirs = kept[...], taken[...]
    low = jnp.where(core == 0, mine, theirs)
    high = jnp.where(core == 0, theirs, mine)
    at = 0
    for out in outs[:-1]:
        size = out.shape[1] // 2
        out[:, :size], out[:, size:] = low[:, at : at + size], high[:, at : at + size]
        at += size
    pair = own[...] + taken[0:1, taken.shape[1] - 128 :]
    both = pair + (by_tensor[...] + by_both[...])
    lane = lax.broadcasted_iota(jnp.int32, (1, 128), 1)
    total = jnp.where((lane >= 32) & (lane < 64), pair, both)
    for row, (first, size) in enumerate(((0, 16), (32, 16), (64, 2), (68, 2))):
        part = jnp.where(core == 0, total, pltpu.roll(total, 128 - size, 1))
        outs[-1][row : row + 1] = pltpu.roll(part, (128 - first) % 128, 1) if first else part
    outs[-1][4:8] = jnp.zeros((4, 128), F32)


def reduced(own, received):
    part = lax.optimization_barrier((own.astype(F32) + received.astype(F32)).astype(BF))
    return part, tensor_swap(part)


def local(
    layer_input,
    doc_lengths,
    gain_attn,
    w_query,
    w_key,
    w_value,
    gain_query,
    gain_key,
    w_output,
    gain_ffn,
    w_gate,
    w_up,
    w_down,
    cotangent,
):
    dp = lax.axis_index("dp")
    core, chip = dp % 2, dp // 2 % CHIPS
    where = (jnp.reshape(dp, (1,)).astype(jnp.int32), pinned(doc_lengths))
    width = w_gate.shape[1] // 2
    x, dy = layer_input, cotangent
    xo = core_swap(x)
    w_query, w_key, w_value, w_output, w_gate, w_up, w_down = map(
        pinned, (w_query, w_key, w_value, w_output, w_gate, w_up, w_down)
    )
    gf = gain_ffn[None, :]
    ga, gq, gk = pinned(gain_attn[None, :]), pinned(gain_query[None, :]), pinned(gain_key[None, :])
    freqs = np.exp(np.arange(64) * (-2.0 * math.log(ROPE_BASE) / HEAD))
    angles = np.tile(np.arange(128)[:, None] * freqs[None, :], (1, 2))
    tab_c, tab_s = pinned(jnp.asarray(np.cos(angles), F32)), pinned(jnp.asarray(np.sin(angles), F32))
    dma = pltpu.SemaphoreType.DMA
    vmem = pltpu.VMEM
    block = shape((HALF, 512))
    token_rows = shape((HALF, 1024))

    def halved(parts):
        width = sum(part.shape[-1] for part in parts[::4])
        own, send = call(
            halve_body,
            0.5,
            where[:1],
            parts,
            [None] * len(parts),
            [shape((32, width), F32), shape((32, width))],
            [None] * 2,
        )
        return own, y_swap(send)

    x15 = x[:128]
    x15 = jnp.where((chip == CHIPS - 1) & (core == 1), x15, jnp.zeros_like(x15))
    x15 = x15 + chip_links(x15, TREE[0], (1,))
    x15 = x15 + chip_links(x15, TREE[1], (1,))

    normed, kv, kraw, cosine, sine, s1, s2, s3, sr = call(
        key_value_body,
        2.4,
        where,
        [pinned(x), xo, ga, w_key, w_value, gk, tab_c, tab_s],
        [None, None, None, HBM, HBM, None, None, None],
        [stored((512, 1024)), stored((512, 512)), stored((512, 256))]
        + [stored((512, 128), F32)] * 2
        + [block] * 4,
        [None] * 5 + [HBM] * 4,
        [vmem((1024, 256), BF)] * 2 + [dma((6,))],
    )
    normed, kv, kraw, cosine, sine = map(pinned, (normed, kv, kraw, cosine, sine))
    rr = y_swap(sr)
    r1, r2, r3 = [x_shift(value, step) for step, value in zip(STEPS, (s1, s2, s3))]
    kv, x15 = lax.optimization_barrier((kv, x15))
    x15 = x15 + chip_links(x15, TREE[2], (1,))
    q, qraw, acc = call(
        query_body,
        4.5,
        where,
        [normed, w_query, gq, cosine, sine, kv],
        [None, HBM, None, None, None, None],
        [shape((4, 512, 128)), stored((512, 512)), shape((4, 512, 256), F32)],
        [None] * 3,
        [vmem((1024, 512), BF), dma((1,))],
    )
    qraw = pinned(qraw)
    rr, r1, r2, r3, x15, acc = lax.optimization_barrier((rr, r1, r2, r3, x15, acc))
    f1, f2, f3 = [x_shift(rr, step) for step in STEPS]
    x15 = x15 + core_swap(jnp.where(core == 1, x15, jnp.zeros_like(x15)))
    starts = vmem((2, HALF, HALF), jnp.int32)
    acc, last = call(
        near_body,
        3,
        where,
        [q, acc, r1, r2, r3, rr, x15, ga, w_key, w_value, gk, tab_c, tab_s],
        [None] * 8 + [HBM, HBM] + [None] * 3,
        [shape((4, 512, 256), F32), stored((128, 512))],
        [None] * 2,
        [starts] + [vmem((1024, 256), BF)] * 2 + [dma((2,))],
    )
    att, lse, own, send = call(
        far_body,
        3.1,
        where,
        [q, acc, f1, f2, f3, w_output],
        [None] * 5 + [HBM],
        [stored((512, 512)), stored((8, 512), F32), token_rows, token_rows],
        [None] * 4,
        [vmem((4, 512, 256), F32), starts, vmem((512, 1024), BF), dma((1,))],
    )
    q, att, lse, last = map(pinned, (q, att, lse, last))
    send, dy_late = lax.optimization_barrier((send, dy))
    part, other = reduced(own, core_swap(send))
    dyo = core_swap(dy_late)
    inputs = x.astype(F32)
    hidden = inputs + (part.astype(F32) + other.astype(F32))
    inv_mid = inv_rms(hidden)
    mid_hat = hidden * inv_mid
    mid = (mid_hat * gf).astype(BF)
    mido = core_swap(mid)

    dmid, dmids, y, ys, dgate, dup, act = call(
        ffn_body,
        9.9,
        where[:1],
        [mid, mido, dy, dyo, w_gate, w_up, w_down],
        [None] * 4 + [HBM] * 3,
        [token_rows] * 4 + [shape((512, width))] * 3,
        [None] * 7,
        [vmem((1024, width), BF)] * 2 + [vmem((width, 1024), BF), dma((3, 3))],
        mib=28,
    )
    dpart, dother = reduced(dmid, core_swap(dmids))
    dpart, dgate, dup, act = lax.optimization_barrier((dpart, dgate, dup, act))
    part_width = 3 * width // 2
    chunk = pl.BlockSpec((HALF, 256), lambda i: (0, i), memory_space=pltpu.VMEM)
    (ffn_grads,) = call(
        ffn_grad_body,
        4,
        (),
        [mid, mido, dy, dyo, dgate, dup, act],
        [chunk] * 4 + [None] * 3,
        [stored((1024, 3 * width))],
        [pl.BlockSpec((256, 3 * width), lambda i: (i, 0), memory_space=pltpu.VMEM)],
        grid=(4,),
    )
    by_z = dp_groups(lambda core, x, y, z: (core, x, y))
    trade = lambda value: lax.all_to_all(value, "dp", 0, 0, axis_index_groups=by_z)
    early = trade(ffn_grads.reshape(4, 256, -1))
    dother, ffn_grads = lax.optimization_barrier((dother, ffn_grads))
    d_mid = dpart.astype(F32) + dother.astype(F32)
    gain_f = jnp.sum(d_mid * mid_hat, axis=0, keepdims=True)
    d_hidden = dy.astype(F32) + norm_back(d_mid, mid_hat, inv_mid, gf)
    d_attn = d_hidden.astype(BF)
    d_attno = core_swap(d_attn)

    rows8 = shape((2, 8, HALF), F32)
    d_att, lse, delta, dq, g1, g2, g3, glast = call(
        far_back_body,
        8,
        where,
        [d_attn, d_attno, w_output, q, att, lse, pinned(f1), pinned(f2), pinned(f3), last],
        [HBM] * 5 + [None] + [HBM] * 4,
        [shape((4, 512, 128)), rows8, rows8, shape((4, 512, 128), F32)] + [block] * 3 + [shape((128, 512))],
        [None] * 4 + [HBM] * 4,
        [vmem((512, 1024), BF), vmem((4, 512, 128), BF), vmem((512, 512), BF), vmem((3, HALF, 512), BF)]
        + [vmem((128, 512), BF), vmem((HALF, 1024), BF), vmem((HALF, 1024), BF)]
        + [vmem((3, HALF, 512), BF), vmem((128, 512), BF), starts, dma((13,))],
    )
    back = [{b: a for a, b in links.items()} for links in TREE]
    g1, g2, g3, ys = lax.optimization_barrier((g1, g2, g3, ys))
    y_part, y_other = reduced(y, core_swap(ys))
    far = [x_shift(value, -step) for step, value in zip(STEPS, (g1, g2, g3))]
    dq, gr, g1, g2, g3 = call(
        near_back_body,
        6,
        where,
        [q, d_att, lse, delta, dq, pinned(r1), pinned(r2), pinned(r3), pinned(rr)],
        [HBM] + [None] * 4 + [HBM] * 4,
        [shape((4, 512, 128), F32), shape((HALF, 512))] + [block] * 3,
        [None, None] + [HBM] * 3,
        [vmem((4, 512, 128), BF), vmem((4, HALF, 512), BF), vmem((3, HALF, 512), BF), starts, dma((8,))],
    )
    glast, dq = lax.optimization_barrier((glast, dq))
    glast = glast + chip_links(glast, back[2])
    dq, dkv, mid_grads = call(
        own_back_body,
        4,
        where,
        [q, kv, d_att, lse, delta, dq, d_attn, d_attno, att],
        [None] * 8 + [HBM],
        [shape((4, 512, 128), F32), stored((512, 512), F32), stored((1024, 1024))],
        [None, None, HBM],
        [vmem((512, 512), BF), vmem((1024, 512), BF), dma((2,))],
    )
    dkv = pinned(dkv)
    glast, g1, g2, g3, dkv, *far = lax.optimization_barrier((glast, g1, g2, g3, dkv, *far))
    near = [x_shift(value, -step) for step, value in zip(STEPS, (g1, g2, g3))]
    glast = glast + chip_links(glast, back[1])
    gr = (sum(value.astype(F32) for value in far) + gr.astype(F32)).astype(BF)
    gr, dq, y_other = lax.optimization_barrier((gr, dq, y_other))
    gr = y_swap(gr)
    glast = glast + chip_links(glast, back[0])
    mid_grads, dn, gain_q = call(
        query_back_body,
        0.5,
        where[:1],
        [dq, normed, qraw, cosine, sine, gq, w_query, pinned(mid_grads)],
        [None, HBM] + [None] * 4 + [HBM, HBM],
        [stored((1024, 1024)), stored((512, 1024)), shape((1, 128), F32)],
        [HBM, None, None],
        [vmem((1024, 512), BF), vmem((512, 1024), BF), vmem((1024, 512), BF), dma((3,))],
        aliases={8: 0},
    )
    dn = pinned(dn)
    def y_turn(total):
        size = total.shape[-1]
        kept, send = call(
            y_turn_body,
            1,
            where[:1],
            [pinned(total.reshape(4, 2, 4, 32, size))],
            [None],
            [shape((4, 32, size))] * 2,
            [None] * 2,
            mib=24,
        )
        return kept, send

    x_kept, s1, s2, s3, own, send = call(
        key_back_body,
        0.5,
        where,
        [pinned(x), pinned(xo), ga, kraw, cosine, sine, gk, w_key, w_value, dkv, glast, *near, gr, dn, gain_q, gain_f],
        [HBM] * 2 + [None] * 5 + [HBM, HBM] + [None] * 6 + [HBM] + [None] * 2,
        [shape((8, 32, 640))] * 4 + [token_rows] * 2,
        [HBM] * 4 + [None] * 2,
        [vmem((1024, 256), BF)] * 2
        + [vmem((512, 512), F32), vmem((HALF, 1024), BF), vmem((HALF, 1024), BF), vmem((512, 1024), BF)]
        + [vmem((8, 4, 32, 640), BF), dma((9,))],
    )
    def y_turn(total):
        size = total.shape[-1]
        kept, send = call(
            y_turn_body,
            1,
            where[:1],
            [pinned(total.reshape(4, 2, 4, 32, size))],
            [None],
            [shape((4, 32, size))] * 2,
            [None] * 2,
            mib=24,
        )
        return kept, send

    early, mid_grads = lax.optimization_barrier((early, mid_grads))
    own, early, mid_grads = lax.optimization_barrier((own, early, mid_grads))
    middle = trade(mid_grads.reshape(4, 256, -1))
    early_kept, early_send = y_turn(early)
    early = early_kept, y_swap(early_send)
    late = [x_shift(value, step) for step, value in zip(STEPS, (s1, s2, s3))]
    layer_output = (hidden + (y_part.astype(F32) + y_other.astype(F32))).astype(BF)
    part, other = reduced(own, core_swap(send))

    def x_turn(kept, came):
        size = kept.shape[-1]
        parts = call(
            x_turn_body,
            1,
            where[:1],
            [kept, came],
            [None] * 2,
            [shape((32, size))] * 4,
            [HBM] * 4,
            [vmem((4, 32, size), BF), dma((4,))],
        )
        return [parts[0]] + [x_shift(value, step) for step, value in zip(STEPS, parts[1:])]

    early = x_turn(*early)
    late = call(
        z_turn_body,
        1,
        where[:1],
        [x_kept, *late],
        [None] * 4,
        [shape((2, 32, 640))] * 4,
        [HBM] * 4,
        [vmem((4, 2, 32, 640), BF), dma((4,))],
    )
    late = [late[0]] + [z_shift(value, step) for step, value in zip(STEPS, late[1:])]
    middle_kept, middle_send = y_turn(middle)
    middle = x_turn(middle_kept, y_swap(middle_send))
    late[0], *early = lax.optimization_barrier((late[0], *early))
    late[0], middle[0] = lax.optimization_barrier((late[0], middle[0]))
    mine, theirs = halved(late)
    mine, theirs, other = lax.optimization_barrier((mine, theirs, other))
    count = 3 * width + 1024 + 640
    kept, given, gains = call(
        sum_body,
        1,
        where[:1],
        [*early, *middle, mine, theirs],
        [None] * 10,
        [shape((16, count), F32)] * 2 + [shape((1, 128), F32)],
        [None] * 3,
    )
    both = lax.ppermute(
        gains,
        ("dp", "tensor"),
        [(i * 2 + t, (i ^ 1) * 2 + 1 - t) for i in range(64) for t in range(2)],
    )
    widths = [2 * width, 2 * width, 2 * width, 1024, 1024, 512, 512]
    grad_gate, grad_up, grad_down, grad_output, grad_query, grad_key, grad_value, gains = call(
        final_body,
        1.4,
        where[:1],
        [kept, core_swap(given), gains, tensor_swap(gains), both],
        [None] * 5,
        [shape((16, n), F32) for n in widths] + [shape((8, 128), F32)],
        [None] * 8,
    )

    d_normed = part.astype(F32) + other.astype(F32)
    inv_in = inv_rms(inputs)
    grad_input = d_hidden + norm_back(d_normed, inputs * inv_in, inv_in, gain_attn[None, :])
    return (
        layer_output,
        grad_input,
        gains[0, :16],
        grad_query,
        grad_key,
        grad_value,
        gains[2, :2],
        gains[3, :2],
        jnp.transpose(grad_output),
        gains[1, :16],
        grad_gate,
        grad_up,
        jnp.transpose(grad_down),
    )


def solution(mesh):
    placed = (
        P("dp", None),
        P(),
        P(),
        P(None, "tensor"),
        P(None, "tensor"),
        P(None, "tensor"),
        P(),
        P(),
        P("tensor", None),
        P(),
        P(None, "tensor"),
        P(None, "tensor"),
        P("tensor", None),
        P("dp", None),
    )
    return jax.shard_map(
        local,
        mesh=mesh,
        in_specs=placed,
        out_specs=(
            P("dp", None),
            P("dp", None),
            P("dp"),
            P("dp", "tensor"),
            P("dp", "tensor"),
            P("dp", "tensor"),
            P("dp"),
            P("dp"),
            P("tensor", "dp"),
            P("dp"),
            P("dp", "tensor"),
            P("dp", "tensor"),
            P("tensor", "dp"),
        ),
        check_vma=False,
    )
```

```python
import functools
import math

import jax
import jax.numpy as jnp
import numpy as np
from jax import lax
from jax.experimental import pallas as pl
from jax.experimental.pallas import tpu as pltpu
from jax.sharding import PartitionSpec as P

EPS = 1e-06
COST = 1.15e9
ROPE_BASE = 1000000.0
HEAD = 128
HALF = 256
SCALE = HEAD ** (-0.5)
SCALE2 = SCALE * math.log2(math.e)
CHIPS = 8
LAST_START = 1920
STEPS = (1, 2, 3)
BF = jnp.bfloat16
F32 = jnp.float32


def dp_index(core, x, y, z):
    return core | x << 1 | y << 3 | z << 4


def dp_pairs(target):
    return [
        (dp_index(core, x, y, z), dp_index(*target(core, x, y, z)))
        for core in range(2)
        for x in range(4)
        for y in range(2)
        for z in range(4)
        if target(core, x, y, z) is not None
    ]


def core_swap(value):
    return lax.ppermute(value, "dp", dp_pairs(lambda core, x, y, z: (1 - core, x, y, z)))


def tensor_swap(value):
    return lax.ppermute(value, "tensor", [(0, 1), (1, 0)])


def x_shift(value, step):
    return lax.ppermute(
        value, "dp", dp_pairs(lambda core, x, y, z: (core, (x + step) % 4, y, z))
    )


def y_swap(value):
    return lax.ppermute(value, "dp", dp_pairs(lambda core, x, y, z: (core, x, 1 - y, z)))


def x_pair(value, bits):
    return lax.ppermute(value, "dp", dp_pairs(lambda core, x, y, z: (core, x ^ bits, y, z)))


def z_pair(value, bits):
    return lax.ppermute(value, "dp", dp_pairs(lambda core, x, y, z: (core, x, y, z ^ bits)))


def z_shift(value, step):
    return lax.ppermute(
        value, "dp", dp_pairs(lambda core, x, y, z: (core, x, y, (z + step) % 4))
    )


def chip_links(value, links, cores=(0, 1)):
    def target(core, x, y, z):
        chip = links.get(y * 4 + x)
        return None if chip is None or core not in cores else (core, chip % 4, chip // 4, z)

    return lax.ppermute(value, "dp", dp_pairs(target))


def dp_groups(key):
    groups = {}
    for index in range(64):
        core, x, y, z = index & 1, index >> 1 & 3, index >> 3 & 1, index >> 4
        groups.setdefault(key(core, x, y, z), []).append(index)
    return list(groups.values())


TREE = ({7: 3}, {7: 5, 3: 1}, {7: 6, 5: 4, 3: 2, 1: 0})


def nn(left, right):
    return lax.dot_general(left, right, (((1,), (0,)), ((), ())), preferred_element_type=F32)


def nt(left, right):
    return lax.dot_general(left, right, (((1,), (1,)), ((), ())), preferred_element_type=F32)


def tn(left, right):
    return lax.dot_general(left, right, (((0,), (0,)), ((), ())), preferred_element_type=F32)


def inv_rms(values):
    return lax.rsqrt(jnp.mean(values * values, axis=-1, keepdims=True) + EPS)


def norm_back(grad, normal, inverse, gain):
    scaled = grad * gain
    return inverse * (scaled - normal * jnp.mean(scaled * normal, axis=-1, keepdims=True))


class Place:
    def __init__(self, ids, lengths):
        dp = ids[0]
        self.core, self.x, self.y, self.z = dp & 1, dp >> 1 & 3, dp >> 3 & 1, dp >> 4
        self.chip = self.y * 4 + self.x
        first = lengths[self.z, 0]
        second = first + lengths[self.z, 1]
        self.starts = (first, second, second + lengths[self.z, 2])

    def first_key(self, token):
        start = jnp.zeros_like(token)
        for end in self.starts:
            start = jnp.where(token >= end, end, start)
        return start

    def token(self, block, offset):
        if block == 0:
            return self.chip * HALF + (offset ^ (self.core * 128))
        return (15 - self.chip) * HALF + (offset ^ ((1 - self.core) * 128))

    def row_block(self, step):
        lower = step <= self.x
        sel = jnp.where(lower, 0, 1)

        def keys(offset):
            token = (self.chip - step) * HALF + (offset ^ (self.core * 128))
            return jnp.where(lower, token, LAST_START + 128)

        return sel, keys

    def far_block(self, step):
        source = (self.x - step) & 3

        def keys(offset):
            token = source * HALF + (offset ^ (self.core * 128))
            return jnp.where(self.y == 1, token, LAST_START + 128)

        return 1 - self.y, keys


def rows_of(sel):
    return pl.ds(pl.multiple_of(sel * HALF, HALF), HALF)


def full(shape):
    return pl.BlockSpec(shape, lambda *args: (0,) * len(shape), memory_space=pltpu.VMEM)


HBM = pl.BlockSpec(memory_space=pltpu.HBM)


def pinned(value):
    return pltpu.with_memory_space_constraint(value, pltpu.HBM)


def call(body, cost_us, prefetch, args, specs, outs, out_specs, scratch=(), grid=(1,), mib=16, aliases={}):
    return pl.pallas_call(
        body,
        grid_spec=pltpu.PrefetchScalarGridSpec(
            num_scalar_prefetch=len(prefetch),
            grid=grid,
            in_specs=[full(a.shape) if spec is None else spec for a, spec in zip(args, specs)],
            out_specs=[full(o.shape) if spec is None else spec for o, spec in zip(outs, out_specs)],
            scratch_shapes=list(scratch),
        ),
        out_shape=outs,
        compiler_params=pltpu.CompilerParams(vmem_limit_bytes=mib * 2**20),
        cost_estimate=pl.CostEstimate(flops=int(cost_us * COST), bytes_accessed=1, transcendentals=0),
        input_output_aliases=aliases,
    )(*prefetch, *args)


def shape(dims, kind=BF):
    return jax.ShapeDtypeStruct(dims, kind)


def stored(dims, kind=BF):
    return pltpu.HBM(dims, kind)


def columns(ref, core, size):
    return ref.at[:, pl.ds(pl.multiple_of(core * size, size), size)]


def rows(ref, core, size):
    return ref.at[pl.ds(pl.multiple_of(core * size, size), size), :]


def started(source, target, sem):
    copy = pltpu.make_async_copy(source, target, sem)
    copy.start()
    return copy


def pieces(own, other):
    return jnp.concatenate([own[0:128], other[0:128], own[128:256], other[128:256]], axis=0)


def split_rows(value, own, other):
    own[0:128], other[0:128] = value[0:128], value[128:256]
    own[128:256], other[128:256] = value[256:384], value[384:512]


def turned(value, gain, cosine, sine):
    w = value * inv_rms(value) * gain
    return (w * cosine + pltpu.roll(w, 64, 1) * sine).astype(BF)


def key_value_body(
    ids, lengths, x, xo, ga, wk, wv, gk, tab_c, tab_s, normed, kv, kraw, cos, sin, s1, s2, s3, sr, wk_v, wv_v, sem
):
    at = Place(ids, lengths)
    copy_k = started(columns(wk, at.core, 256), wk_v, sem.at[0])
    copy_v = started(columns(wv, at.core, 256), wv_v, sem.at[1])
    row = lax.broadcasted_iota(jnp.int32, (1, 128), 1)
    freq = jnp.exp((row & 63).astype(F32) * (-2.0 * math.log(ROPE_BASE) / HEAD))
    offset = lax.broadcasted_iota(jnp.int32, (128, 128), 0)
    tab_c, tab_s = tab_c[...], tab_s[...]
    for piece in range(4):
        base = at.token(piece // 2, jnp.int32(piece % 2 * 128))
        start = at.first_key(base + offset)
        shift_c = shift_s = None
        for first in (jnp.int32(0),) + at.starts:
            angle = (base - first).astype(F32) * freq
            c, s = jnp.cos(angle), jnp.sin(angle)
            if shift_c is None:
                shift_c, shift_s = jnp.broadcast_to(c, (128, 128)), jnp.broadcast_to(s, (128, 128))
            else:
                shift_c = jnp.where(start == first, c, shift_c)
                shift_s = jnp.where(start == first, s, shift_s)
        cos[piece * 128 : (piece + 1) * 128] = shift_c * tab_c - shift_s * tab_s
        sine = shift_s * tab_c + shift_c * tab_s
        sin[piece * 128 : (piece + 1) * 128] = jnp.where(row < 64, -sine, sine)
    for block in range(2):
        cut = slice(block * 128, (block + 1) * 128)
        here = slice(block * HALF, (block + 1) * HALF)
        value = jnp.concatenate([x[cut], xo[cut]], axis=0).astype(F32)
        n = (value * inv_rms(value) * ga[...]).astype(BF)
        normed[here] = n
        if block == 0:
            copy_k.wait()
            copy_v.wait()
        raw = nn(n, wk_v[...])
        kraw[here] = raw.astype(BF)
        for h in range(2):
            head = slice(h * 128, (h + 1) * 128)
            kv[here, head] = turned(raw[:, head], gk[...], cos[here], sin[here])
        kv[here, 256:] = nn(n, wv_v[...]).astype(BF)
    copies = [
        started(kv.at[rows_of(jnp.where(at.x + step < 4, 0, 1))], out, sem.at[1 + step])
        for step, out in zip(STEPS, (s1, s2, s3))
    ]
    copies.append(started(kv.at[rows_of(at.y)], sr, sem.at[5]))
    for copy in copies:
        copy.wait()


def attend(q, acc, where, pair, mask):
    ones = jnp.ones((pair.shape[0], 128), BF)
    for h in range(4):
        g = h // 2
        keys = pair[:, g * 128 : (g + 1) * 128]
        values = pair[:, 256 + g * 128 : 256 + (g + 1) * 128]
        weights = jnp.exp2(nt(q[h, where, :], keys) * SCALE2)
        if mask is not None:
            weights = jnp.where(mask, weights, 0.0)
        acc[h, where, :] += nn(weights.astype(BF), jnp.concatenate([values, ones], axis=1))


def query_body(
    ids, lengths, normed, wq, gq, cos, sin, kv, q, qraw, acc, wq_v, sem
):
    at = Place(ids, lengths)
    copy = started(columns(wq, at.core, 512), wq_v, sem.at[0])
    acc[...] = jnp.zeros_like(acc)
    copy.wait()
    for block in range(2):
        here = slice(block * HALF, (block + 1) * HALF)
        raw = nn(normed[here], wq_v[...])
        qraw[here] = raw.astype(BF)
        for h in range(4):
            q[h, here] = turned(raw[:, h * 128 : (h + 1) * 128], gq[...], cos[here], sin[here])
        query = at.token(block, lax.broadcasted_iota(jnp.int32, (HALF, 1), 0))
        key = at.token(block, lax.broadcasted_iota(jnp.int32, (1, HALF), 1))
        attend(q, acc, here, kv[here], (key <= query) & (key >= at.first_key(query)))


def set_starts(at, start, dim):
    for block in range(2):
        start[block] = at.first_key(at.token(block, lax.broadcasted_iota(jnp.int32, (HALF, HALF), dim)))


def near_body(
    ids, lengths, q, acc_in, r1, r2, r3, rr, x15, ga, wk, wv, gk, tab_c, tab_s, acc, last, start, wk_v, wv_v, sem
):
    at = Place(ids, lengths)
    copy_k = started(columns(wk, at.core, 256), wk_v, sem.at[0])
    copy_v = started(columns(wv, at.core, 256), wv_v, sem.at[1])
    acc[...] = acc_in[...]
    set_starts(at, start, 0)
    offset = lax.broadcasted_iota(jnp.int32, (1, HALF), 1)
    for step, pair in zip(STEPS, (r1, r2, r3)):
        sel, keys = at.row_block(step)
        attend(q, acc, rows_of(sel), pair[...], keys(offset) >= start[sel])
    sel, keys = at.far_block(0)
    attend(q, acc, rows_of(sel), rr[...], keys(offset) >= start[sel])
    value = x15[...].astype(F32)
    n = (value * inv_rms(value) * ga[...]).astype(BF)
    copy_k.wait()
    copy_v.wait()
    raw = nn(n, wk_v[...])
    sine = tab_s[...]
    sine = jnp.where(lax.broadcasted_iota(jnp.int32, (1, 128), 1) < 64, -sine, sine)
    for h in range(2):
        head = slice(h * 128, (h + 1) * 128)
        last[:, head] = turned(raw[:, head], gk[...], tab_c[...], sine)
    last[:, 256:] = nn(n, wv_v[...]).astype(BF)
    attend(q, acc, pl.ds(HALF, HALF), last[...], None)


def far_body(ids, lengths, q, acc_in, r1, r2, r3, wo, att, lse, own, send, acc, start, wo_v, sem):
    at = Place(ids, lengths)
    copy = started(rows(wo, at.core, 512), wo_v, sem.at[0])
    acc[...] = acc_in[...]
    set_starts(at, start, 0)
    offset = lax.broadcasted_iota(jnp.int32, (1, HALF), 1)
    for step, pair in zip(STEPS, (r1, r2, r3)):
        sel, keys = at.far_block(step)
        attend(q, acc, rows_of(sel), pair[...], keys(offset) >= start[sel])
    for h in range(4):
        total = acc[h, :, 128:]
        att[:, h * 128 : (h + 1) * 128] = (acc[h, :, :128] / total).astype(BF)
        lse[h : h + 1] = jnp.log2(jnp.transpose(total)[0:1])
    lse[4:8] = jnp.zeros((4, 2 * HALF), F32)
    copy.wait()
    split_rows(nn(att[...], wo_v[...]).astype(BF), own, send)


def ffn_body(
    ids, mid, mido, dy, dyo, wg, wu, wd, dmid, dmids, y, ys, dgate, dup, act, wg_v, wu_v, wd_v, sem
):
    copies = []
    for n in range(3):
        cut = pl.multiple_of((ids[0] & 1) * 768 + n * 256, 256)
        here = slice(n * 256, (n + 1) * 256)
        copies.append(
            [
                started(wg.at[:, pl.ds(cut, 256)], wg_v.at[:, here], sem.at[n, 0]),
                started(wu.at[:, pl.ds(cut, 256)], wu_v.at[:, here], sem.at[n, 1]),
                started(wd.at[pl.ds(cut, 256), :], wd_v.at[here], sem.at[n, 2]),
            ]
        )
    mid_all = jnp.concatenate([mid[...], mido[...]], axis=0)
    dy_all = jnp.concatenate([dy[...], dyo[...]], axis=0)
    for n in range(3):
        here = slice(n * 256, (n + 1) * 256)
        for copy in copies[n]:
            copy.wait()
        gate = nn(mid_all, wg_v[:, here])
        up = nn(mid_all, wu_v[:, here])
        d_act = nt(dy_all, wd_v[here])
        sigma = 1.0 / (1.0 + jnp.exp(-gate))
        silu = gate * sigma
        act[:, here] = (silu * up).astype(BF)
        dgate[:, here] = (d_act * up * sigma * (1.0 + gate * (1.0 - sigma))).astype(BF)
        dup[:, here] = (d_act * silu).astype(BF)
    out = (nt(dgate[...], wg_v[...]) + nt(dup[...], wu_v[...])).astype(BF)
    dmid[...], dmids[...] = out[:HALF], out[HALF:]
    out = nn(act[...], wd_v[...]).astype(BF)
    y[...], ys[...] = out[:HALF], out[HALF:]


def ffn_grad_body(mid, mido, dy, dyo, dgate, dup, act, out):
    width = dgate.shape[1]
    left = jnp.concatenate([mid[...], mido[...]], axis=0)
    out[:, :width] = tn(left, dgate[...]).astype(BF)
    out[:, width : 2 * width] = tn(left, dup[...]).astype(BF)
    left = jnp.concatenate([dy[...], dyo[...]], axis=0)
    out[:, 2 * width :] = tn(left, act[...]).astype(BF)


def spread(grads, at, outs, sem, first=0):
    return [
        started(grads.at[at(step)], out, sem.at[first + step])
        for step, out in zip((0,) + STEPS, outs)
    ]


def attend_back(q, d_att, lse, delta, dq, sel, where, pair, mask):
    key_grads, value_grads = [], []
    for g in range(2):
        keys = pair[:, g * 128 : (g + 1) * 128]
        values = pair[:, 256 + g * 128 : 256 + (g + 1) * 128]
        key_grad = value_grad = 0.0
        for h in (2 * g, 2 * g + 1):
            query, upper = q[h, where, :], d_att[h, where, :]
            weights = jnp.exp2(nt(keys, query) * SCALE2 - lse[sel, h : h + 1])
            if mask is not None:
                weights = jnp.where(mask, weights, 0.0)
            d_score = (weights * (nt(values, upper) - delta[sel, h : h + 1])).astype(BF)
            value_grad += nn(weights.astype(BF), upper)
            key_grad += nn(d_score, query)
            dq[h, where, :] += tn(d_score, keys)
        key_grads.append(key_grad * SCALE)
        value_grads.append(value_grad)
    return jnp.concatenate(key_grads + value_grads, axis=1)


def far_back_body(
    ids, lengths, dat_h, dato_h, wo, q_h, att_h, lse_in, r1, r2, r3, last_h, d_att, lse, delta, dq, g1, g2, g3, glast, wo_v, q, att, far_v, last, dat, dato, stage, stage_last, start, sem
):
    at = Place(ids, lengths)
    copy = started(rows(wo, at.core, 512), wo_v, sem.at[0])
    first = [started(dat_h, dat, sem.at[11]), started(dato_h, dato, sem.at[12])]
    loads = [
        started(source, target, sem.at[5 + n])
        for n, (source, target) in enumerate(
            ((att_h, att), (q_h, q), (last_h, last), (r1, far_v.at[0]), (r2, far_v.at[1]), (r3, far_v.at[2]))
        )
    ]
    set_starts(at, start, 1)
    dq[...] = jnp.zeros_like(dq)
    first[0].wait()
    first[1].wait()
    d_attn = pieces(dat[...], dato[...])
    copy.wait()
    grad = nt(d_attn, wo_v[...]).astype(BF)
    lse[...] = jnp.zeros_like(lse)
    delta[...] = jnp.zeros_like(delta)
    loads[0].wait()
    for h in range(4):
        part = grad[:, h * 128 : (h + 1) * 128]
        d_att[h] = part
        prod = part.astype(F32) * att[:, h * 128 : (h + 1) * 128].astype(F32)
        total = jnp.sum(jnp.transpose(prod), axis=0, keepdims=True)
        for block in range(2):
            cut = slice(block * HALF, (block + 1) * HALF)
            delta[block, h : h + 1] = total[:, cut]
            lse[block, h : h + 1] = lse_in[h : h + 1, cut]
    loads[1].wait()
    loads[2].wait()
    out = attend_back(q, d_att, lse, delta, dq, 1, pl.ds(HALF, HALF), last[...], None)
    stage_last[...] = out.astype(BF)
    copies = [started(stage_last, glast, sem.at[1])]
    offset = lax.broadcasted_iota(jnp.int32, (HALF, 1), 0)
    for step, target in zip(STEPS, (g1, g2, g3)):
        sel, keys = at.far_block(step)
        loads[2 + step].wait()
        pair = far_v[step - 1]
        out = attend_back(q, d_att, lse, delta, dq, sel, rows_of(sel), pair, keys(offset) >= start[sel])
        stage[step - 1] = out.astype(BF)
        copies.append(started(stage.at[step - 1], target, sem.at[1 + step]))
    for copy in copies:
        copy.wait()


def near_back_body(
    ids, lengths, q_h, d_att, lse, delta, dq_in, r1, r2, r3, rr, dq, gr, g1, g2, g3, q, near_v, stage, start, sem
):
    at = Place(ids, lengths)
    loads = [
        started(source, target, sem.at[3 + n])
        for n, (source, target) in enumerate(
            ((q_h, q), (rr, near_v.at[0]), (r1, near_v.at[1]), (r2, near_v.at[2]), (r3, near_v.at[3]))
        )
    ]
    set_starts(at, start, 1)
    dq[...] = dq_in[...]
    loads[0].wait()
    loads[1].wait()
    offset = lax.broadcasted_iota(jnp.int32, (HALF, 1), 0)
    copies = []
    sel, keys = at.far_block(0)
    out = attend_back(q, d_att, lse, delta, dq, sel, rows_of(sel), near_v[0], keys(offset) >= start[sel])
    gr[...] = out.astype(BF)
    for step, target in zip(STEPS, (g1, g2, g3)):
        sel, keys = at.row_block(step)
        loads[1 + step].wait()
        out = attend_back(q, d_att, lse, delta, dq, sel, rows_of(sel), near_v[step], keys(offset) >= start[sel])
        stage[step - 1] = out.astype(BF)
        copies.append(started(stage.at[step - 1], target, sem.at[step - 1]))
    for copy in copies:
        copy.wait()


def head_back(grad, value, gain, cosine, sine):
    turned_back = grad * cosine + pltpu.roll(grad * sine, 64, 1)
    inverse = inv_rms(value)
    hat = value * inverse
    gain_part = jnp.sum(turned_back * hat, axis=0, keepdims=True)
    return norm_back(turned_back, hat, inverse, gain).astype(BF), gain_part


def own_back_body(ids, lengths, q, kv, d_att, lse, delta, dq_in, dq, dkv):
    at = Place(ids, lengths)
    dq[...] = dq_in[...]
    for block in range(2):
        here = slice(block * HALF, (block + 1) * HALF)
        key = at.token(block, lax.broadcasted_iota(jnp.int32, (HALF, 1), 0))
        query = at.token(block, lax.broadcasted_iota(jnp.int32, (1, HALF), 1))
        mask = (key <= query) & (key >= at.first_key(query))
        dkv[here] = attend_back(q, d_att, lse, delta, dq, block, here, kv[here], mask)


def query_back_body(
    ids, dq, dat, dato, att_h, normed_h, qraw, cos, sin, gq, wq, grads_h, dn, gain, wq_v, att, normed, grads, sem
):
    copy = started(columns(wq, ids[0] & 1, 512), wq_v, sem.at[0])
    load = started(normed_h, normed, sem.at[1])
    load_att = started(att_h, att, sem.at[3])
    cosine, sine = cos[...], sin[...]
    gain_sum, raw = 0.0, []
    for h in range(4):
        value = qraw[:, h * 128 : (h + 1) * 128].astype(F32)
        out, part = head_back(dq[h] * SCALE, value, gq[...], cosine, sine)
        gain_sum += part
        raw.append(out)
    gain[...] = gain_sum
    dq_raw = jnp.concatenate(raw, axis=1)
    load.wait()
    grads[:, 512:] = tn(normed[...], dq_raw).astype(BF)
    load_att.wait()
    grads[:, :512] = tn(pieces(dat[...], dato[...]), att[...]).astype(BF)
    store = started(grads, grads_h, sem.at[2])
    copy.wait()
    dn[...] = nt(dq_raw, wq_v[...]).astype(BF)
    store.wait()


def key_back_body(
    ids, lengths, x_h, xo_h, ga, kraw, cos, sin, gk, wk, wv, dkv_in, dlast, r1, r2, r3, rr, dn_h, gain_q, gain_f, kept, s1, s2, s3, own, send, wk_v, wv_v, dkv, x, xo, dn, grads, sem
):
    at = Place(ids, lengths)
    copy_k = started(columns(wk, at.core, 256), wk_v, sem.at[0])
    copy_v = started(columns(wv, at.core, 256), wv_v, sem.at[1])
    loads = [
        started(source, target, sem.at[6 + n])
        for n, (source, target) in enumerate(((x_h, x), (xo_h, xo), (dn_h, dn)))
    ]
    dkv[...] = dkv_in[...]
    for step, pair in zip(STEPS, (r1, r2, r3)):
        dkv[rows_of(jnp.where(at.x + step < 4, 0, 1)), :] += pair[...].astype(F32)
    dkv[rows_of(at.y), :] += rr[...].astype(F32)
    row0 = pl.multiple_of(jnp.where(at.core == 1, 0, 128), 128)
    piece = dlast[...].astype(F32)
    dkv[pl.ds(row0, 128), :] += jnp.where(at.chip == CHIPS - 1, piece, jnp.zeros_like(piece))
    gain_k, raw = 0.0, []
    for h in range(2):
        head = slice(h * 128, (h + 1) * 128)
        out, part = head_back(dkv[:, head], kraw[:, head].astype(F32), gk[...], cos[...], sin[...])
        raw.append(out)
        gain_k += part
    dk_raw = jnp.concatenate(raw, axis=1)
    dv_raw = dkv[:, 256:512].astype(BF)
    for load in loads:
        load.wait()
    value = pieces(x[...], xo[...]).astype(F32)
    hat = value * inv_rms(value)
    out = tn((hat * ga[...]).astype(BF), jnp.concatenate([dk_raw, dv_raw], axis=1)).astype(BF)
    grads[:, :, :, :512] = out.reshape(8, 4, 32, 512)
    copy_k.wait()
    copy_v.wait()
    d_normed = dn[...].astype(F32) + nt(dk_raw, wk_v[...]) + nt(dv_raw, wv_v[...])
    gain_a = jnp.sum(d_normed * hat, axis=0, keepdims=True)
    split_rows(d_normed.astype(BF), own, send)
    gains = jnp.concatenate([gain_a, gain_f[...], gain_q[...], gain_k], axis=1)
    count = gains.shape[1]

    def spot(lane):
        wide = lane < 2048
        index = jnp.where(wide, lane & 1023, lane & 127)
        size = jnp.where(wide, 5, 2)
        base = jnp.where(lane < 1024, 0, jnp.where(wide, 32, jnp.where(lane < 2176, 64, 68)))
        return index >> size, base + (index & ((1 << size) - 1))

    holder, _ = spot(lax.broadcasted_iota(jnp.int32, (32, count), 1))
    _, lane = spot(lax.broadcasted_iota(jnp.int32, (count, 128), 0))
    held = holder == lax.broadcasted_iota(jnp.int32, (32, count), 0)
    fold = jnp.where(lane == lax.broadcasted_iota(jnp.int32, (count, 128), 1), 1.0, 0.0).astype(BF)
    picked = nn(jnp.where(held, gains, 0.0).astype(BF), fold)
    first = lax.broadcasted_iota(jnp.int32, (32, 128), 0) == 0
    for n in range(32):
        grads[n // 4, n % 4, :, 512:] = jnp.where(first, picked[n : n + 1], 0.0).astype(BF)
    for copy in spread(grads, lambda step: (slice(None), at.x + step & 3), (kept, s1, s2, s3), sem, 2):
        copy.wait()


def four(refs):
    a, b, c, d = (ref[...].astype(F32) for ref in refs)
    return (a + b) + (c + d)


def z_turn_body(ids, r0, r1, r2, r3, kept, s1, s2, s3, total, sem):
    z = ids[0] >> 4
    total[...] = four((r0, r1, r2, r3)).astype(BF).reshape(total.shape)
    for copy in spread(total, lambda step: z + step & 3, (kept, s1, s2, s3), sem):
        copy.wait()


def y_turn_body(ids, came, kept, send):
    y = ids[0] >> 3 & 1
    for n in range(2):
        part = (came[0, n].astype(F32) + came[1, n].astype(F32)) + (
            came[2, n].astype(F32) + came[3, n].astype(F32)
        )
        part = part.astype(BF)

        @pl.when(y == n)
        def _():
            kept[...] = part

        @pl.when(y != n)
        def _():
            send[...] = part


def x_turn_body(ids, own, came, kept, s1, s2, s3, total, sem):
    x = ids[0] >> 1 & 3
    total[...] = (own[...].astype(F32) + came[...].astype(F32)).astype(BF)
    for copy in spread(total, lambda step: x + step & 3, (kept, s1, s2, s3), sem):
        copy.wait()


def halve_body(ids, *refs):
    y = ids[0] >> 3 & 1
    own, send = refs[-2:]
    at = 0
    for n in range(0, len(refs) - 2, 4):
        part = four(refs[n : n + 4])
        size = part.shape[2]
        own[:, at : at + size] = jnp.where(y == 0, part[0], part[1])
        send[:, at : at + size] = jnp.where(y == 0, part[1], part[0]).astype(BF)
        at += size


def sum_body(ids, *refs):
    mine, theirs, kept, given, gains = refs[8:]
    core = ids[0] & 1
    row = lax.broadcasted_iota(jnp.int32, (16, 128), 0)
    at = 0
    for total in (four(refs[0:4]), four(refs[4:8]), mine[...] + theirs[...].astype(F32)):
        size = total.shape[1]
        kept[:, at : at + size] = jnp.where(core == 0, total[:16], total[16:])
        given[:, at : at + size] = jnp.where(core == 0, total[16:], total[:16])
        at += size
    gain = total[0:1, size - 128 :]
    gains[...] = gain
    given[:, at - 128 :] = jnp.where(row == 0, gain, 0.0)


def final_body(ids, kept, taken, own, by_tensor, by_both, *outs):
    core = ids[0] & 1
    mine, theirs = kept[...], taken[...]
    low = jnp.where(core == 0, mine, theirs)
    high = jnp.where(core == 0, theirs, mine)
    at = 0
    for out in outs[:-4]:
        size = out.shape[1] // 2
        out[:, :size], out[:, size:] = low[:, at : at + size], high[:, at : at + size]
        at += size
    pair = own[...] + taken[0:1, taken.shape[1] - 128 :]
    both = pair + (by_tensor[...] + by_both[...])
    lane = lax.broadcasted_iota(jnp.int32, (1, 128), 1)
    total = jnp.where((lane >= 32) & (lane < 64), pair, both)
    for out, (first, size) in zip(outs[-4:], ((0, 16), (32, 16), (64, 2), (68, 2))):
        part = jnp.where(core == 0, total, pltpu.roll(total, 128 - size, 1))
        part = pltpu.roll(part, 128 - first, 1) if first else part
        out[...] = part[:, :size]


def reduced(own, received):
    part = lax.optimization_barrier((own.astype(F32) + received.astype(F32)).astype(BF))
    return part, tensor_swap(part)


def local(
    layer_input,
    doc_lengths,
    gain_attn,
    w_query,
    w_key,
    w_value,
    gain_query,
    gain_key,
    w_output,
    gain_ffn,
    w_gate,
    w_up,
    w_down,
    cotangent,
):
    dp = lax.axis_index("dp")
    core, chip = dp % 2, dp // 2 % CHIPS
    where = (jnp.reshape(dp, (1,)).astype(jnp.int32), pinned(doc_lengths))
    width = w_gate.shape[1] // 2
    x, dy = layer_input, cotangent
    xo = core_swap(x)
    w_query, w_key, w_value, w_output, w_gate, w_up, w_down = map(
        pinned, (w_query, w_key, w_value, w_output, w_gate, w_up, w_down)
    )
    gf = gain_ffn[None, :]
    ga, gq, gk = pinned(gain_attn[None, :]), pinned(gain_query[None, :]), pinned(gain_key[None, :])
    freqs = np.exp(np.arange(64) * (-2.0 * math.log(ROPE_BASE) / HEAD))
    angles = np.tile(np.arange(128)[:, None] * freqs[None, :], (1, 2))
    tab_c, tab_s = pinned(jnp.asarray(np.cos(angles), F32)), pinned(jnp.asarray(np.sin(angles), F32))
    dma = pltpu.SemaphoreType.DMA
    vmem = pltpu.VMEM
    block = shape((HALF, 512))
    token_rows = shape((HALF, 1024))

    def halved(parts):
        width = sum(part.shape[-1] for part in parts[::4])
        own, send = call(
            halve_body,
            0.5,
            where[:1],
            parts,
            [None] * len(parts),
            [shape((32, width), F32), shape((32, width))],
            [None] * 2,
        )
        return own, y_swap(send)

    x15 = x[:128]
    x15 = jnp.where((chip == CHIPS - 1) & (core == 1), x15, jnp.zeros_like(x15))
    x15 = x15 + chip_links(x15, TREE[0], (1,))
    x15 = x15 + chip_links(x15, TREE[1], (1,))

    normed, kv, kraw, cosine, sine, s1, s2, s3, sr = call(
        key_value_body,
        2.4,
        where,
        [pinned(x), xo, ga, w_key, w_value, gk, tab_c, tab_s],
        [None, None, None, HBM, HBM, None, None, None],
        [stored((512, 1024)), stored((512, 512)), stored((512, 256))]
        + [stored((512, 128), F32)] * 2
        + [block] * 4,
        [None] * 5 + [HBM] * 4,
        [vmem((1024, 256), BF)] * 2 + [dma((6,))],
    )
    normed, kv, kraw, cosine, sine = map(pinned, (normed, kv, kraw, cosine, sine))
    rr = y_swap(sr)
    r1, r2, r3 = [x_shift(value, step) for step, value in zip(STEPS, (s1, s2, s3))]
    kv, x15 = lax.optimization_barrier((kv, x15))
    x15 = x15 + chip_links(x15, TREE[2], (1,))
    q, qraw, acc = call(
        query_body,
        4.5,
        where,
        [normed, w_query, gq, cosine, sine, kv],
        [None, HBM, None, None, None, None],
        [shape((4, 512, 128)), stored((512, 512)), shape((4, 512, 256), F32)],
        [None] * 3,
        [vmem((1024, 512), BF), dma((1,))],
    )
    qraw = pinned(qraw)
    rr, r1, r2, r3, x15, acc = lax.optimization_barrier((rr, r1, r2, r3, x15, acc))
    f1, f2, f3 = [x_shift(rr, step) for step in STEPS]
    x15 = x15 + core_swap(jnp.where(core == 1, x15, jnp.zeros_like(x15)))
    starts = vmem((2, HALF, HALF), jnp.int32)
    acc, last = call(
        near_body,
        3,
        where,
        [q, acc, r1, r2, r3, rr, x15, ga, w_key, w_value, gk, tab_c, tab_s],
        [None] * 8 + [HBM, HBM] + [None] * 3,
        [shape((4, 512, 256), F32), stored((128, 512))],
        [None] * 2,
        [starts] + [vmem((1024, 256), BF)] * 2 + [dma((2,))],
    )
    att, lse, own, send = call(
        far_body,
        3.1,
        where,
        [q, acc, f1, f2, f3, w_output],
        [None] * 5 + [HBM],
        [stored((512, 512)), stored((8, 512), F32), token_rows, token_rows],
        [None] * 4,
        [vmem((4, 512, 256), F32), starts, vmem((512, 1024), BF), dma((1,))],
    )
    q, att, lse, last = map(pinned, (q, att, lse, last))
    send, dy_late = lax.optimization_barrier((send, dy))
    part, other = reduced(own, core_swap(send))
    dyo = core_swap(dy_late)
    inputs = x.astype(F32)
    hidden = inputs + (part.astype(F32) + other.astype(F32))
    inv_mid = inv_rms(hidden)
    mid_hat = hidden * inv_mid
    mid = (mid_hat * gf).astype(BF)
    mido = core_swap(mid)

    dmid, dmids, y, ys, dgate, dup, act = call(
        ffn_body,
        9.9,
        where[:1],
        [mid, mido, dy, dyo, w_gate, w_up, w_down],
        [None] * 4 + [HBM] * 3,
        [token_rows] * 4 + [shape((512, width))] * 3,
        [None] * 7,
        [vmem((1024, width), BF)] * 2 + [vmem((width, 1024), BF), dma((3, 3))],
        mib=28,
    )
    dpart, dother = reduced(dmid, core_swap(dmids))
    dpart, dgate, dup, act = lax.optimization_barrier((dpart, dgate, dup, act))
    part_width = 3 * width // 2
    chunk = pl.BlockSpec((HALF, 256), lambda i: (0, i), memory_space=pltpu.VMEM)
    (ffn_grads,) = call(
        ffn_grad_body,
        4,
        (),
        [mid, mido, dy, dyo, dgate, dup, act],
        [chunk] * 4 + [None] * 3,
        [stored((1024, 3 * width))],
        [pl.BlockSpec((256, 3 * width), lambda i: (i, 0), memory_space=pltpu.VMEM)],
        grid=(4,),
    )
    by_z = dp_groups(lambda core, x, y, z: (core, x, y))
    trade = lambda value: lax.all_to_all(value, "dp", 0, 0, axis_index_groups=by_z)
    early = trade(ffn_grads.reshape(4, 256, -1))
    dother, ffn_grads = lax.optimization_barrier((dother, ffn_grads))
    d_mid = dpart.astype(F32) + dother.astype(F32)
    gain_f = jnp.sum(d_mid * mid_hat, axis=0, keepdims=True)
    d_hidden = dy.astype(F32) + norm_back(d_mid, mid_hat, inv_mid, gf)
    d_attn = d_hidden.astype(BF)
    d_attno = core_swap(d_attn)

    rows8 = shape((2, 8, HALF), F32)
    d_att, lse, delta, dq, g1, g2, g3, glast = call(
        far_back_body,
        8,
        where,
        [d_attn, d_attno, w_output, q, att, lse, pinned(f1), pinned(f2), pinned(f3), last],
        [HBM] * 5 + [None] + [HBM] * 4,
        [shape((4, 512, 128)), rows8, rows8, shape((4, 512, 128), F32)] + [block] * 3 + [shape((128, 512))],
        [None] * 4 + [HBM] * 4,
        [vmem((512, 1024), BF), vmem((4, 512, 128), BF), vmem((512, 512), BF), vmem((3, HALF, 512), BF)]
        + [vmem((128, 512), BF), vmem((HALF, 1024), BF), vmem((HALF, 1024), BF)]
        + [vmem((3, HALF, 512), BF), vmem((128, 512), BF), starts, dma((13,))],
    )
    back = [{b: a for a, b in links.items()} for links in TREE]
    g1, g2, g3, ys = lax.optimization_barrier((g1, g2, g3, ys))
    y_part, y_other = reduced(y, core_swap(ys))
    far = [x_shift(value, -step) for step, value in zip(STEPS, (g1, g2, g3))]
    dq, gr, g1, g2, g3 = call(
        near_back_body,
        6,
        where,
        [q, d_att, lse, delta, dq, pinned(r1), pinned(r2), pinned(r3), pinned(rr)],
        [HBM] + [None] * 4 + [HBM] * 4,
        [shape((4, 512, 128), F32), shape((HALF, 512))] + [block] * 3,
        [None, None] + [HBM] * 3,
        [vmem((4, 512, 128), BF), vmem((4, HALF, 512), BF), vmem((3, HALF, 512), BF), starts, dma((8,))],
    )
    glast, dq = lax.optimization_barrier((glast, dq))
    glast = glast + chip_links(glast, back[2])
    dq, dkv = call(
        own_back_body,
        4,
        where,
        [q, kv, d_att, lse, delta, dq],
        [None] * 6,
        [shape((4, 512, 128), F32), stored((512, 512), F32)],
        [None] * 2,
    )
    dkv = pinned(dkv)
    glast, g1, g2, g3, dkv, *far = lax.optimization_barrier((glast, g1, g2, g3, dkv, *far))
    near = [x_shift(value, -step) for step, value in zip(STEPS, (g1, g2, g3))]
    glast = glast + chip_links(glast, back[1])
    gr = (sum(value.astype(F32) for value in far) + gr.astype(F32)).astype(BF)
    gr, dq, y_other = lax.optimization_barrier((gr, dq, y_other))
    gr = y_swap(gr)
    glast = glast + chip_links(glast, back[0])
    mid_grads, dn, gain_q = call(
        query_back_body,
        0.5,
        where[:1],
        [dq, d_attn, d_attno, att, normed, qraw, cosine, sine, gq, w_query],
        [None] * 3 + [HBM, HBM] + [None] * 4 + [HBM],
        [stored((1024, 1024)), stored((512, 1024)), shape((1, 128), F32)],
        [HBM, None, None],
        [vmem((1024, 512), BF), vmem((512, 512), BF), vmem((512, 1024), BF), vmem((1024, 1024), BF)]
        + [dma((4,))],
    )
    dn = pinned(dn)
    def y_turn(total):
        size = total.shape[-1]
        kept, send = call(
            y_turn_body,
            1,
            where[:1],
            [pinned(total.reshape(4, 2, 4, 32, size))],
            [None],
            [shape((4, 32, size))] * 2,
            [None] * 2,
            mib=24,
        )
        return kept, send

    x_kept, s1, s2, s3, own, send = call(
        key_back_body,
        0.5,
        where,
        [pinned(x), pinned(xo), ga, kraw, cosine, sine, gk, w_key, w_value, dkv, glast, *near, gr, dn, gain_q, gain_f],
        [HBM] * 2 + [None] * 5 + [HBM, HBM] + [None] * 6 + [HBM] + [None] * 2,
        [shape((8, 32, 640))] * 4 + [token_rows] * 2,
        [HBM] * 4 + [None] * 2,
        [vmem((1024, 256), BF)] * 2
        + [vmem((512, 512), F32), vmem((HALF, 1024), BF), vmem((HALF, 1024), BF), vmem((512, 1024), BF)]
        + [vmem((8, 4, 32, 640), BF), dma((9,))],
    )
    def y_turn(total):
        size = total.shape[-1]
        kept, send = call(
            y_turn_body,
            1,
            where[:1],
            [pinned(total.reshape(4, 2, 4, 32, size))],
            [None],
            [shape((4, 32, size))] * 2,
            [None] * 2,
            mib=24,
        )
        return kept, send

    early, mid_grads = lax.optimization_barrier((early, mid_grads))
    own, early, mid_grads = lax.optimization_barrier((own, early, mid_grads))
    middle = trade(mid_grads.reshape(4, 256, -1))
    early_kept, early_send = y_turn(early)
    early = early_kept, y_swap(early_send)
    late = [x_shift(value, step) for step, value in zip(STEPS, (s1, s2, s3))]
    layer_output = (hidden + (y_part.astype(F32) + y_other.astype(F32))).astype(BF)
    part, other = reduced(own, core_swap(send))

    def x_turn(kept, came):
        size = kept.shape[-1]
        parts = call(
            x_turn_body,
            1,
            where[:1],
            [kept, came],
            [None] * 2,
            [shape((32, size))] * 4,
            [HBM] * 4,
            [vmem((4, 32, size), BF), dma((4,))],
        )
        return [parts[0]] + [x_shift(value, step) for step, value in zip(STEPS, parts[1:])]

    early = x_turn(*early)
    late = call(
        z_turn_body,
        1,
        where[:1],
        [x_kept, *late],
        [None] * 4,
        [shape((2, 32, 640))] * 4,
        [HBM] * 4,
        [vmem((4, 2, 32, 640), BF), dma((4,))],
    )
    late = [late[0]] + [z_shift(value, step) for step, value in zip(STEPS, late[1:])]
    middle_kept, middle_send = y_turn(middle)
    middle = x_turn(middle_kept, y_swap(middle_send))
    late[0], *early = lax.optimization_barrier((late[0], *early))
    late[0], middle[0] = lax.optimization_barrier((late[0], middle[0]))
    mine, theirs = halved(late)
    mine, theirs, other = lax.optimization_barrier((mine, theirs, other))
    count = 3 * width + 1024 + 640
    kept, given, gains = call(
        sum_body,
        1,
        where[:1],
        [*early, *middle, mine, theirs],
        [None] * 10,
        [shape((16, count), F32)] * 2 + [shape((1, 128), F32)],
        [None] * 3,
    )
    both = lax.ppermute(
        gains,
        ("dp", "tensor"),
        [(i * 2 + t, (i ^ 1) * 2 + 1 - t) for i in range(64) for t in range(2)],
    )
    widths = [2 * width, 2 * width, 2 * width, 1024, 1024, 512, 512]
    grad_gate, grad_up, grad_down, grad_output, grad_query, grad_key, grad_value, *gains = call(
        final_body,
        1.4,
        where[:1],
        [kept, core_swap(given), gains, tensor_swap(gains), both],
        [None] * 5,
        [shape((16, n), F32) for n in widths] + [shape((1, n), F32) for n in (16, 16, 2, 2)],
        [None] * 11,
    )

    d_normed = part.astype(F32) + other.astype(F32)
    inv_in = inv_rms(inputs)
    grad_input = d_hidden + norm_back(d_normed, inputs * inv_in, inv_in, gain_attn[None, :])
    return (
        layer_output,
        grad_input,
        gains[0].reshape(16),
        grad_query,
        grad_key,
        grad_value,
        gains[2].reshape(2),
        gains[3].reshape(2),
        jnp.transpose(grad_output),
        gains[1].reshape(16),
        grad_gate,
        grad_up,
        jnp.transpose(grad_down),
    )


def solution(mesh):
    placed = (
        P("dp", None),
        P(),
        P(),
        P(None, "tensor"),
        P(None, "tensor"),
        P(None, "tensor"),
        P(),
        P(),
        P("tensor", None),
        P(),
        P(None, "tensor"),
        P(None, "tensor"),
        P("tensor", None),
        P("dp", None),
    )
    return jax.shard_map(
        local,
        mesh=mesh,
        in_specs=placed,
        out_specs=(
            P("dp", None),
            P("dp", None),
            P("dp"),
            P("dp", "tensor"),
            P("dp", "tensor"),
            P("dp", "tensor"),
            P("dp"),
            P("dp"),
            P("tensor", "dp"),
            P("dp"),
            P("dp", "tensor"),
            P("dp", "tensor"),
            P("tensor", "dp"),
        ),
        check_vma=False,
    )
```

```python
import functools
import math

import jax
import jax.numpy as jnp
import numpy as np
from jax import lax
from jax.experimental import pallas as pl
from jax.experimental.pallas import tpu as pltpu
from jax.sharding import PartitionSpec as P

EPS = 1e-06
COST = 1.15e9
ROPE_BASE = 1000000.0
HEAD = 128
HALF = 256
SCALE = HEAD ** (-0.5)
SCALE2 = SCALE * math.log2(math.e)
CHIPS = 8
LAST_START = 1920
STEPS = (1, 2, 3)
BF = jnp.bfloat16
F32 = jnp.float32


def dp_index(core, x, y, z):
    return core | x << 1 | y << 3 | z << 4


def dp_pairs(target):
    return [
        (dp_index(core, x, y, z), dp_index(*target(core, x, y, z)))
        for core in range(2)
        for x in range(4)
        for y in range(2)
        for z in range(4)
        if target(core, x, y, z) is not None
    ]


def core_swap(value):
    return lax.ppermute(value, "dp", dp_pairs(lambda core, x, y, z: (1 - core, x, y, z)))


def tensor_swap(value):
    return lax.ppermute(value, "tensor", [(0, 1), (1, 0)])


def x_shift(value, step):
    return lax.ppermute(
        value, "dp", dp_pairs(lambda core, x, y, z: (core, (x + step) % 4, y, z))
    )


def y_swap(value):
    return lax.ppermute(value, "dp", dp_pairs(lambda core, x, y, z: (core, x, 1 - y, z)))


def x_pair(value, bits):
    return lax.ppermute(value, "dp", dp_pairs(lambda core, x, y, z: (core, x ^ bits, y, z)))


def z_pair(value, bits):
    return lax.ppermute(value, "dp", dp_pairs(lambda core, x, y, z: (core, x, y, z ^ bits)))


def z_shift(value, step):
    return lax.ppermute(
        value, "dp", dp_pairs(lambda core, x, y, z: (core, x, y, (z + step) % 4))
    )


def chip_links(value, links, cores=(0, 1)):
    def target(core, x, y, z):
        chip = links.get(y * 4 + x)
        return None if chip is None or core not in cores else (core, chip % 4, chip // 4, z)

    return lax.ppermute(value, "dp", dp_pairs(target))


def dp_groups(key):
    groups = {}
    for index in range(64):
        core, x, y, z = index & 1, index >> 1 & 3, index >> 3 & 1, index >> 4
        groups.setdefault(key(core, x, y, z), []).append(index)
    return list(groups.values())


TREE = ({7: 3}, {7: 5, 3: 1}, {7: 6, 5: 4, 3: 2, 1: 0})


def nn(left, right):
    return lax.dot_general(left, right, (((1,), (0,)), ((), ())), preferred_element_type=F32)


def nt(left, right):
    return lax.dot_general(left, right, (((1,), (1,)), ((), ())), preferred_element_type=F32)


def tn(left, right):
    return lax.dot_general(left, right, (((0,), (0,)), ((), ())), preferred_element_type=F32)


def inv_rms(values):
    return lax.rsqrt(jnp.mean(values * values, axis=-1, keepdims=True) + EPS)


def norm_back(grad, normal, inverse, gain):
    scaled = grad * gain
    return inverse * (scaled - normal * jnp.mean(scaled * normal, axis=-1, keepdims=True))


class Place:
    def __init__(self, ids, lengths):
        dp = ids[0]
        self.core, self.x, self.y, self.z = dp & 1, dp >> 1 & 3, dp >> 3 & 1, dp >> 4
        self.chip = self.y * 4 + self.x
        first = lengths[self.z, 0]
        second = first + lengths[self.z, 1]
        self.starts = (first, second, second + lengths[self.z, 2])

    def first_key(self, token):
        start = jnp.zeros_like(token)
        for end in self.starts:
            start = jnp.where(token >= end, end, start)
        return start

    def token(self, block, offset):
        if block == 0:
            return self.chip * HALF + (offset ^ (self.core * 128))
        return (15 - self.chip) * HALF + (offset ^ ((1 - self.core) * 128))

    def row_block(self, step):
        lower = step <= self.x
        sel = jnp.where(lower, 0, 1)

        def keys(offset):
            token = (self.chip - step) * HALF + (offset ^ (self.core * 128))
            return jnp.where(lower, token, LAST_START + 128)

        return sel, keys

    def far_block(self, step):
        source = (self.x - step) & 3

        def keys(offset):
            token = source * HALF + (offset ^ (self.core * 128))
            return jnp.where(self.y == 1, token, LAST_START + 128)

        return 1 - self.y, keys


def rows_of(sel):
    return pl.ds(pl.multiple_of(sel * HALF, HALF), HALF)


def full(shape):
    return pl.BlockSpec(shape, lambda *args: (0,) * len(shape), memory_space=pltpu.VMEM)


HBM = pl.BlockSpec(memory_space=pltpu.HBM)


def pinned(value):
    return pltpu.with_memory_space_constraint(value, pltpu.HBM)


def call(body, cost_us, prefetch, args, specs, outs, out_specs, scratch=(), grid=(1,), mib=16, aliases={}):
    return pl.pallas_call(
        body,
        grid_spec=pltpu.PrefetchScalarGridSpec(
            num_scalar_prefetch=len(prefetch),
            grid=grid,
            in_specs=[full(a.shape) if spec is None else spec for a, spec in zip(args, specs)],
            out_specs=[full(o.shape) if spec is None else spec for o, spec in zip(outs, out_specs)],
            scratch_shapes=list(scratch),
        ),
        out_shape=outs,
        compiler_params=pltpu.CompilerParams(vmem_limit_bytes=mib * 2**20),
        cost_estimate=pl.CostEstimate(flops=int(cost_us * COST), bytes_accessed=1, transcendentals=0),
        input_output_aliases=aliases,
    )(*prefetch, *args)


def shape(dims, kind=BF):
    return jax.ShapeDtypeStruct(dims, kind)


def stored(dims, kind=BF):
    return pltpu.HBM(dims, kind)


def columns(ref, core, size):
    return ref.at[:, pl.ds(pl.multiple_of(core * size, size), size)]


def rows(ref, core, size):
    return ref.at[pl.ds(pl.multiple_of(core * size, size), size), :]


def started(source, target, sem):
    copy = pltpu.make_async_copy(source, target, sem)
    copy.start()
    return copy


def pieces(own, other):
    return jnp.concatenate([own[0:128], other[0:128], own[128:256], other[128:256]], axis=0)


def split_rows(value, own, other):
    own[0:128], other[0:128] = value[0:128], value[128:256]
    own[128:256], other[128:256] = value[256:384], value[384:512]


def turned(value, gain, cosine, sine):
    w = value * inv_rms(value) * gain
    return (w * cosine + pltpu.roll(w, 64, 1) * sine).astype(BF)


def key_value_body(
    ids, lengths, x, xo, ga, wk, wv, gk, tab_c, tab_s, normed, kv, kraw, cos, sin, s1, s2, s3, sr, wk_v, wv_v, sem
):
    at = Place(ids, lengths)
    copy_k = started(columns(wk, at.core, 256), wk_v, sem.at[0])
    copy_v = started(columns(wv, at.core, 256), wv_v, sem.at[1])
    row = lax.broadcasted_iota(jnp.int32, (1, 128), 1)
    freq = jnp.exp((row & 63).astype(F32) * (-2.0 * math.log(ROPE_BASE) / HEAD))
    offset = lax.broadcasted_iota(jnp.int32, (128, 128), 0)
    tab_c, tab_s = tab_c[...], tab_s[...]
    bases = [at.token(piece // 2, jnp.int32(piece % 2 * 128)) for piece in range(4)]
    starts = (jnp.int32(0),) + at.starts
    shift = jnp.zeros((16, 128), jnp.int32)
    index = lax.broadcasted_iota(jnp.int32, (16, 128), 0)
    for n in range(16):
        shift = jnp.where(index == n, bases[n // 4] - starts[n % 4], shift)
    shift = shift.astype(F32) * freq
    all_c, all_s = jnp.cos(shift), jnp.sin(shift)
    for piece in range(4):
        base = bases[piece]
        start = at.first_key(base + offset)
        shift_c = shift_s = None
        for n, first in enumerate(starts):
            c, s = (table[4 * piece + n : 4 * piece + n + 1] for table in (all_c, all_s))
            if shift_c is None:
                shift_c, shift_s = jnp.broadcast_to(c, (128, 128)), jnp.broadcast_to(s, (128, 128))
            else:
                shift_c = jnp.where(start == first, c, shift_c)
                shift_s = jnp.where(start == first, s, shift_s)
        cos[piece * 128 : (piece + 1) * 128] = shift_c * tab_c - shift_s * tab_s
        sine = shift_s * tab_c + shift_c * tab_s
        sin[piece * 128 : (piece + 1) * 128] = jnp.where(row < 64, -sine, sine)
    for block in range(2):
        cut = slice(block * 128, (block + 1) * 128)
        here = slice(block * HALF, (block + 1) * HALF)
        value = jnp.concatenate([x[cut], xo[cut]], axis=0).astype(F32)
        n = (value * inv_rms(value) * ga[...]).astype(BF)
        normed[here] = n
        if block == 0:
            copy_k.wait()
            copy_v.wait()
        raw = nn(n, wk_v[...])
        kraw[here] = raw.astype(BF)
        for h in range(2):
            head = slice(h * 128, (h + 1) * 128)
            kv[here, head] = turned(raw[:, head], gk[...], cos[here], sin[here])
        kv[here, 256:] = nn(n, wv_v[...]).astype(BF)
    copies = [
        started(kv.at[rows_of(jnp.where(at.x + step < 4, 0, 1))], out, sem.at[1 + step])
        for step, out in zip(STEPS, (s1, s2, s3))
    ]
    copies.append(started(kv.at[rows_of(at.y)], sr, sem.at[5]))
    for copy in copies:
        copy.wait()


def attend(q, acc, where, pair, mask):
    ones = jnp.ones((pair.shape[0], 128), BF)
    for h in range(4):
        g = h // 2
        keys = pair[:, g * 128 : (g + 1) * 128]
        values = pair[:, 256 + g * 128 : 256 + (g + 1) * 128]
        weights = jnp.exp2(nt(q[h, where, :], keys) * SCALE2)
        if mask is not None:
            weights = jnp.where(mask, weights, 0.0)
        acc[h, where, :] += nn(weights.astype(BF), jnp.concatenate([values, ones], axis=1))


def query_body(
    ids, lengths, normed, wq, gq, cos, sin, kv, q, qraw, acc, wq_v, sem
):
    at = Place(ids, lengths)
    copy = started(columns(wq, at.core, 512), wq_v, sem.at[0])
    acc[...] = jnp.zeros_like(acc)
    copy.wait()
    for block in range(2):
        here = slice(block * HALF, (block + 1) * HALF)
        raw = nn(normed[here], wq_v[...])
        qraw[here] = raw.astype(BF)
        for h in range(4):
            q[h, here] = turned(raw[:, h * 128 : (h + 1) * 128], gq[...], cos[here], sin[here])
        query = at.token(block, lax.broadcasted_iota(jnp.int32, (HALF, 1), 0))
        key = at.token(block, lax.broadcasted_iota(jnp.int32, (1, HALF), 1))
        attend(q, acc, here, kv[here], (key <= query) & (key >= at.first_key(query)))


def set_starts(at, start, dim):
    for block in range(2):
        start[block] = at.first_key(at.token(block, lax.broadcasted_iota(jnp.int32, (HALF, HALF), dim)))


def near_body(
    ids, lengths, q, acc_in, r1, r2, r3, rr, x15, ga, wk, wv, gk, tab_c, tab_s, acc, last, start, wk_v, wv_v, sem
):
    at = Place(ids, lengths)
    copy_k = started(columns(wk, at.core, 256), wk_v, sem.at[0])
    copy_v = started(columns(wv, at.core, 256), wv_v, sem.at[1])
    acc[...] = acc_in[...]
    set_starts(at, start, 0)
    offset = lax.broadcasted_iota(jnp.int32, (1, HALF), 1)
    for step, pair in zip(STEPS, (r1, r2, r3)):
        sel, keys = at.row_block(step)
        attend(q, acc, rows_of(sel), pair[...], keys(offset) >= start[sel])
    sel, keys = at.far_block(0)
    attend(q, acc, rows_of(sel), rr[...], keys(offset) >= start[sel])
    value = x15[...].astype(F32)
    n = (value * inv_rms(value) * ga[...]).astype(BF)
    copy_k.wait()
    copy_v.wait()
    raw = nn(n, wk_v[...])
    sine = tab_s[...]
    sine = jnp.where(lax.broadcasted_iota(jnp.int32, (1, 128), 1) < 64, -sine, sine)
    for h in range(2):
        head = slice(h * 128, (h + 1) * 128)
        last[:, head] = turned(raw[:, head], gk[...], tab_c[...], sine)
    last[:, 256:] = nn(n, wv_v[...]).astype(BF)
    attend(q, acc, pl.ds(HALF, HALF), last[...], None)


def far_body(ids, lengths, q, acc_in, r1, r2, r3, wo, att, lse, own, send, acc, start, wo_v, sem):
    at = Place(ids, lengths)
    copy = started(rows(wo, at.core, 512), wo_v, sem.at[0])
    acc[...] = acc_in[...]
    set_starts(at, start, 0)
    offset = lax.broadcasted_iota(jnp.int32, (1, HALF), 1)
    for step, pair in zip(STEPS, (r1, r2, r3)):
        sel, keys = at.far_block(step)
        attend(q, acc, rows_of(sel), pair[...], keys(offset) >= start[sel])
    for h in range(4):
        total = acc[h, :, 128:]
        att[:, h * 128 : (h + 1) * 128] = (acc[h, :, :128] / total).astype(BF)
        lse[h : h + 1] = jnp.log2(jnp.transpose(total)[0:1])
    lse[4:8] = jnp.zeros((4, 2 * HALF), F32)
    copy.wait()
    split_rows(nn(att[...], wo_v[...]).astype(BF), own, send)


def ffn_body(
    ids, mid, mido, dy, dyo, wg, wu, wd, dmid, dmids, y, ys, dgate, dup, act, wg_v, wu_v, wd_v, sem
):
    copies = []
    for n in range(3):
        cut = pl.multiple_of((ids[0] & 1) * 768 + n * 256, 256)
        here = slice(n * 256, (n + 1) * 256)
        copies.append(
            [
                started(wg.at[:, pl.ds(cut, 256)], wg_v.at[:, here], sem.at[n, 0]),
                started(wu.at[:, pl.ds(cut, 256)], wu_v.at[:, here], sem.at[n, 1]),
                started(wd.at[pl.ds(cut, 256), :], wd_v.at[here], sem.at[n, 2]),
            ]
        )
    mid_all = jnp.concatenate([mid[...], mido[...]], axis=0)
    dy_all = jnp.concatenate([dy[...], dyo[...]], axis=0)
    for n in range(3):
        here = slice(n * 256, (n + 1) * 256)
        for copy in copies[n]:
            copy.wait()
        gate = nn(mid_all, wg_v[:, here])
        up = nn(mid_all, wu_v[:, here])
        d_act = nt(dy_all, wd_v[here])
        sigma = 1.0 / (1.0 + jnp.exp(-gate))
        silu = gate * sigma
        act[:, here] = (silu * up).astype(BF)
        dgate[:, here] = (d_act * up * sigma * (1.0 + gate * (1.0 - sigma))).astype(BF)
        dup[:, here] = (d_act * silu).astype(BF)
    out = (nt(dgate[...], wg_v[...]) + nt(dup[...], wu_v[...])).astype(BF)
    dmid[...], dmids[...] = out[:HALF], out[HALF:]
    out = nn(act[...], wd_v[...]).astype(BF)
    y[...], ys[...] = out[:HALF], out[HALF:]


def ffn_grad_body(mid, mido, dy, dyo, dgate, dup, act, out):
    width = dgate.shape[1]
    left = jnp.concatenate([mid[...], mido[...]], axis=0)
    out[:, :width] = tn(left, dgate[...]).astype(BF)
    out[:, width : 2 * width] = tn(left, dup[...]).astype(BF)
    left = jnp.concatenate([dy[...], dyo[...]], axis=0)
    out[:, 2 * width :] = tn(left, act[...]).astype(BF)


def spread(grads, at, outs, sem, first=0):
    return [
        started(grads.at[at(step)], out, sem.at[first + step])
        for step, out in zip((0,) + STEPS, outs)
    ]


def attend_back(q, d_att, lse, delta, dq, sel, where, pair, mask):
    key_grads, value_grads = [], []
    for g in range(2):
        keys = pair[:, g * 128 : (g + 1) * 128]
        values = pair[:, 256 + g * 128 : 256 + (g + 1) * 128]
        key_grad = value_grad = 0.0
        for h in (2 * g, 2 * g + 1):
            query, upper = q[h, where, :], d_att[h, where, :]
            weights = jnp.exp2(nt(keys, query) * SCALE2 - lse[sel, h : h + 1])
            if mask is not None:
                weights = jnp.where(mask, weights, 0.0)
            d_score = (weights * (nt(values, upper) - delta[sel, h : h + 1])).astype(BF)
            value_grad += nn(weights.astype(BF), upper)
            key_grad += nn(d_score, query)
            dq[h, where, :] += tn(d_score, keys)
        key_grads.append(key_grad * SCALE)
        value_grads.append(value_grad)
    return jnp.concatenate(key_grads + value_grads, axis=1)


def far_back_body(
    ids, lengths, dat_h, dato_h, wo, q_h, att_h, lse_in, r1, r2, r3, last_h, d_att, lse, delta, dq, g1, g2, g3, glast, wo_v, q, att, far_v, last, dat, dato, stage, stage_last, start, sem
):
    at = Place(ids, lengths)
    copy = started(rows(wo, at.core, 512), wo_v, sem.at[0])
    first = [started(dat_h, dat, sem.at[11]), started(dato_h, dato, sem.at[12])]
    loads = [
        started(source, target, sem.at[5 + n])
        for n, (source, target) in enumerate(
            ((att_h, att), (q_h, q), (last_h, last), (r1, far_v.at[0]), (r2, far_v.at[1]), (r3, far_v.at[2]))
        )
    ]
    set_starts(at, start, 1)
    dq[...] = jnp.zeros_like(dq)
    first[0].wait()
    first[1].wait()
    d_attn = pieces(dat[...], dato[...])
    copy.wait()
    grad = nt(d_attn, wo_v[...]).astype(BF)
    lse[...] = jnp.zeros_like(lse)
    delta[...] = jnp.zeros_like(delta)
    loads[0].wait()
    for h in range(4):
        part = grad[:, h * 128 : (h + 1) * 128]
        d_att[h] = part
        prod = part.astype(F32) * att[:, h * 128 : (h + 1) * 128].astype(F32)
        total = jnp.sum(jnp.transpose(prod), axis=0, keepdims=True)
        for block in range(2):
            cut = slice(block * HALF, (block + 1) * HALF)
            delta[block, h : h + 1] = total[:, cut]
            lse[block, h : h + 1] = lse_in[h : h + 1, cut]
    loads[1].wait()
    loads[2].wait()
    out = attend_back(q, d_att, lse, delta, dq, 1, pl.ds(HALF, HALF), last[...], None)
    stage_last[...] = out.astype(BF)
    copies = [started(stage_last, glast, sem.at[1])]
    offset = lax.broadcasted_iota(jnp.int32, (HALF, 1), 0)
    for step, target in zip(STEPS, (g1, g2, g3)):
        sel, keys = at.far_block(step)
        loads[2 + step].wait()
        pair = far_v[step - 1]
        out = attend_back(q, d_att, lse, delta, dq, sel, rows_of(sel), pair, keys(offset) >= start[sel])
        stage[step - 1] = out.astype(BF)
        copies.append(started(stage.at[step - 1], target, sem.at[1 + step]))
    for copy in copies:
        copy.wait()


def near_back_body(
    ids, lengths, q_h, d_att, lse, delta, dq_in, r1, r2, r3, rr, dq, gr, g1, g2, g3, q, near_v, stage, start, sem
):
    at = Place(ids, lengths)
    loads = [
        started(source, target, sem.at[3 + n])
        for n, (source, target) in enumerate(
            ((q_h, q), (rr, near_v.at[0]), (r1, near_v.at[1]), (r2, near_v.at[2]), (r3, near_v.at[3]))
        )
    ]
    set_starts(at, start, 1)
    dq[...] = dq_in[...]
    loads[0].wait()
    loads[1].wait()
    offset = lax.broadcasted_iota(jnp.int32, (HALF, 1), 0)
    copies = []
    sel, keys = at.far_block(0)
    out = attend_back(q, d_att, lse, delta, dq, sel, rows_of(sel), near_v[0], keys(offset) >= start[sel])
    gr[...] = out.astype(BF)
    for step, target in zip(STEPS, (g1, g2, g3)):
        sel, keys = at.row_block(step)
        loads[1 + step].wait()
        out = attend_back(q, d_att, lse, delta, dq, sel, rows_of(sel), near_v[step], keys(offset) >= start[sel])
        stage[step - 1] = out.astype(BF)
        copies.append(started(stage.at[step - 1], target, sem.at[step - 1]))
    for copy in copies:
        copy.wait()


def head_back(grad, value, gain, cosine, sine):
    turned_back = grad * cosine + pltpu.roll(grad * sine, 64, 1)
    inverse = inv_rms(value)
    hat = value * inverse
    gain_part = jnp.sum(turned_back * hat, axis=0, keepdims=True)
    return norm_back(turned_back, hat, inverse, gain).astype(BF), gain_part


def own_back_body(ids, lengths, q, kv, d_att, lse, delta, dq_in, dq, dkv):
    at = Place(ids, lengths)
    dq[...] = dq_in[...]
    for block in range(2):
        here = slice(block * HALF, (block + 1) * HALF)
        key = at.token(block, lax.broadcasted_iota(jnp.int32, (HALF, 1), 0))
        query = at.token(block, lax.broadcasted_iota(jnp.int32, (1, HALF), 1))
        mask = (key <= query) & (key >= at.first_key(query))
        dkv[here] = attend_back(q, d_att, lse, delta, dq, block, here, kv[here], mask)


def query_back_body(
    ids, dq, dat, dato, att_h, normed_h, qraw, cos, sin, gq, wq, grads_h, dn, gain, wq_v, att, normed, grads, sem
):
    copy = started(columns(wq, ids[0] & 1, 512), wq_v, sem.at[0])
    load = started(normed_h, normed, sem.at[1])
    load_att = started(att_h, att, sem.at[3])
    cosine, sine = cos[...], sin[...]
    gain_sum, raw = 0.0, []
    for h in range(4):
        value = qraw[:, h * 128 : (h + 1) * 128].astype(F32)
        out, part = head_back(dq[h] * SCALE, value, gq[...], cosine, sine)
        gain_sum += part
        raw.append(out)
    gain[...] = gain_sum
    dq_raw = jnp.concatenate(raw, axis=1)
    load.wait()
    grads[:, 512:] = tn(normed[...], dq_raw).astype(BF)
    load_att.wait()
    grads[:, :512] = tn(pieces(dat[...], dato[...]), att[...]).astype(BF)
    store = started(grads, grads_h, sem.at[2])
    copy.wait()
    dn[...] = nt(dq_raw, wq_v[...]).astype(BF)
    store.wait()


def key_back_body(
    ids, lengths, x_h, xo_h, ga, kraw, cos, sin, gk, wk, wv, dkv_in, dlast, r1, r2, r3, rr, dn_h, gain_q, gain_f, kept, s1, s2, s3, own, send, wk_v, wv_v, dkv, x, xo, dn, grads, sem
):
    at = Place(ids, lengths)
    copy_k = started(columns(wk, at.core, 256), wk_v, sem.at[0])
    copy_v = started(columns(wv, at.core, 256), wv_v, sem.at[1])
    loads = [
        started(source, target, sem.at[6 + n])
        for n, (source, target) in enumerate(((x_h, x), (xo_h, xo), (dn_h, dn)))
    ]
    dkv[...] = dkv_in[...]
    for step, pair in zip(STEPS, (r1, r2, r3)):
        dkv[rows_of(jnp.where(at.x + step < 4, 0, 1)), :] += pair[...].astype(F32)
    dkv[rows_of(at.y), :] += rr[...].astype(F32)
    row0 = pl.multiple_of(jnp.where(at.core == 1, 0, 128), 128)
    piece = dlast[...].astype(F32)
    dkv[pl.ds(row0, 128), :] += jnp.where(at.chip == CHIPS - 1, piece, jnp.zeros_like(piece))
    gain_k, raw = 0.0, []
    for h in range(2):
        head = slice(h * 128, (h + 1) * 128)
        out, part = head_back(dkv[:, head], kraw[:, head].astype(F32), gk[...], cos[...], sin[...])
        raw.append(out)
        gain_k += part
    dk_raw = jnp.concatenate(raw, axis=1)
    dv_raw = dkv[:, 256:512].astype(BF)
    for load in loads:
        load.wait()
    value = pieces(x[...], xo[...]).astype(F32)
    hat = value * inv_rms(value)
    out = tn((hat * ga[...]).astype(BF), jnp.concatenate([dk_raw, dv_raw], axis=1)).astype(BF)
    grads[:, :, :, :512] = out.reshape(8, 4, 32, 512)
    copy_k.wait()
    copy_v.wait()
    d_normed = dn[...].astype(F32) + nt(dk_raw, wk_v[...]) + nt(dv_raw, wv_v[...])
    gain_a = jnp.sum(d_normed * hat, axis=0, keepdims=True)
    split_rows(d_normed.astype(BF), own, send)
    gains = jnp.concatenate([gain_a, gain_f[...], gain_q[...], gain_k], axis=1)
    count = gains.shape[1]

    def spot(lane):
        wide = lane < 2048
        index = jnp.where(wide, lane & 1023, lane & 127)
        size = jnp.where(wide, 5, 2)
        base = jnp.where(lane < 1024, 0, jnp.where(wide, 32, jnp.where(lane < 2176, 64, 68)))
        return index >> size, base + (index & ((1 << size) - 1))

    holder, _ = spot(lax.broadcasted_iota(jnp.int32, (32, count), 1))
    _, lane = spot(lax.broadcasted_iota(jnp.int32, (count, 128), 0))
    held = holder == lax.broadcasted_iota(jnp.int32, (32, count), 0)
    fold = jnp.where(lane == lax.broadcasted_iota(jnp.int32, (count, 128), 1), 1.0, 0.0).astype(BF)
    picked = nn(jnp.where(held, gains, 0.0).astype(BF), fold)
    first = lax.broadcasted_iota(jnp.int32, (32, 128), 0) == 0
    for n in range(32):
        grads[n // 4, n % 4, :, 512:] = jnp.where(first, picked[n : n + 1], 0.0).astype(BF)
    for copy in spread(grads, lambda step: (slice(None), at.x + step & 3), (kept, s1, s2, s3), sem, 2):
        copy.wait()


def four(refs):
    a, b, c, d = (ref[...].astype(F32) for ref in refs)
    return (a + b) + (c + d)


def z_turn_body(ids, r0, r1, r2, r3, kept, s1, s2, s3, total, sem):
    z = ids[0] >> 4
    total[...] = four((r0, r1, r2, r3)).astype(BF).reshape(total.shape)
    for copy in spread(total, lambda step: z + step & 3, (kept, s1, s2, s3), sem):
        copy.wait()


def y_turn_body(ids, came, kept, send):
    y = ids[0] >> 3 & 1
    for n in range(2):
        part = (came[0, n].astype(F32) + came[1, n].astype(F32)) + (
            came[2, n].astype(F32) + came[3, n].astype(F32)
        )
        part = part.astype(BF)

        @pl.when(y == n)
        def _():
            kept[...] = part

        @pl.when(y != n)
        def _():
            send[...] = part


def x_turn_body(ids, own, came, kept, s1, s2, s3, total, sem):
    x = ids[0] >> 1 & 3
    total[...] = (own[...].astype(F32) + came[...].astype(F32)).astype(BF)
    for copy in spread(total, lambda step: x + step & 3, (kept, s1, s2, s3), sem):
        copy.wait()


def halve_body(ids, *refs):
    y = ids[0] >> 3 & 1
    own, send = refs[-2:]
    at = 0
    for n in range(0, len(refs) - 2, 4):
        part = four(refs[n : n + 4])
        size = part.shape[2]
        own[:, at : at + size] = jnp.where(y == 0, part[0], part[1])
        send[:, at : at + size] = jnp.where(y == 0, part[1], part[0]).astype(BF)
        at += size


def sum_body(ids, *refs):
    mine, theirs, kept, given, gains = refs[8:]
    core = ids[0] & 1
    row = lax.broadcasted_iota(jnp.int32, (16, 128), 0)
    at = 0
    for total in (four(refs[0:4]), four(refs[4:8]), mine[...] + theirs[...].astype(F32)):
        size = total.shape[1]
        kept[:, at : at + size] = jnp.where(core == 0, total[:16], total[16:])
        given[:, at : at + size] = jnp.where(core == 0, total[16:], total[:16])
        at += size
    gain = total[0:1, size - 128 :]
    gains[...] = gain
    given[:, at - 128 :] = jnp.where(row == 0, gain, 0.0)


def final_body(ids, kept, taken, own, by_tensor, by_both, *outs):
    core = ids[0] & 1
    mine, theirs = kept[...], taken[...]
    low = jnp.where(core == 0, mine, theirs)
    high = jnp.where(core == 0, theirs, mine)
    at = 0
    for out in outs[:-4]:
        size = out.shape[1] // 2
        out[:, :size], out[:, size:] = low[:, at : at + size], high[:, at : at + size]
        at += size
    pair = own[...] + taken[0:1, taken.shape[1] - 128 :]
    both = pair + (by_tensor[...] + by_both[...])
    lane = lax.broadcasted_iota(jnp.int32, (1, 128), 1)
    total = jnp.where((lane >= 32) & (lane < 64), pair, both)
    for out, (first, size) in zip(outs[-4:], ((0, 16), (32, 16), (64, 2), (68, 2))):
        part = jnp.where(core == 0, total, pltpu.roll(total, 128 - size, 1))
        part = pltpu.roll(part, 128 - first, 1) if first else part
        out[...] = part[:, :size]


def reduced(own, received):
    part = lax.optimization_barrier((own.astype(F32) + received.astype(F32)).astype(BF))
    return part, tensor_swap(part)


def local(
    layer_input,
    doc_lengths,
    gain_attn,
    w_query,
    w_key,
    w_value,
    gain_query,
    gain_key,
    w_output,
    gain_ffn,
    w_gate,
    w_up,
    w_down,
    cotangent,
):
    dp = lax.axis_index("dp")
    core, chip = dp % 2, dp // 2 % CHIPS
    where = (jnp.reshape(dp, (1,)).astype(jnp.int32), pinned(doc_lengths))
    width = w_gate.shape[1] // 2
    x, dy = layer_input, cotangent
    xo = core_swap(x)
    w_query, w_key, w_value, w_output, w_gate, w_up, w_down = map(
        pinned, (w_query, w_key, w_value, w_output, w_gate, w_up, w_down)
    )
    gf = gain_ffn[None, :]
    ga, gq, gk = pinned(gain_attn[None, :]), pinned(gain_query[None, :]), pinned(gain_key[None, :])
    freqs = np.exp(np.arange(64) * (-2.0 * math.log(ROPE_BASE) / HEAD))
    angles = np.tile(np.arange(128)[:, None] * freqs[None, :], (1, 2))
    tab_c, tab_s = pinned(jnp.asarray(np.cos(angles), F32)), pinned(jnp.asarray(np.sin(angles), F32))
    dma = pltpu.SemaphoreType.DMA
    vmem = pltpu.VMEM
    block = shape((HALF, 512))
    token_rows = shape((HALF, 1024))

    def halved(parts):
        width = sum(part.shape[-1] for part in parts[::4])
        own, send = call(
            halve_body,
            0.5,
            where[:1],
            parts,
            [None] * len(parts),
            [shape((32, width), F32), shape((32, width))],
            [None] * 2,
        )
        return own, y_swap(send)

    x15 = x[:128]
    x15 = jnp.where((chip == CHIPS - 1) & (core == 1), x15, jnp.zeros_like(x15))
    x15 = x15 + chip_links(x15, TREE[0], (1,))
    x15 = x15 + chip_links(x15, TREE[1], (1,))

    normed, kv, kraw, cosine, sine, s1, s2, s3, sr = call(
        key_value_body,
        2.4,
        where,
        [pinned(x), xo, ga, w_key, w_value, gk, tab_c, tab_s],
        [None, None, None, HBM, HBM, None, None, None],
        [stored((512, 1024)), stored((512, 512)), stored((512, 256))]
        + [stored((512, 128), F32)] * 2
        + [block] * 4,
        [None] * 5 + [HBM] * 4,
        [vmem((1024, 256), BF)] * 2 + [dma((6,))],
    )
    normed, kv, kraw, cosine, sine = map(pinned, (normed, kv, kraw, cosine, sine))
    rr = y_swap(sr)
    r1, r2, r3 = [x_shift(value, step) for step, value in zip(STEPS, (s1, s2, s3))]
    kv, x15 = lax.optimization_barrier((kv, x15))
    x15 = x15 + chip_links(x15, TREE[2], (1,))
    q, qraw, acc = call(
        query_body,
        4.5,
        where,
        [normed, w_query, gq, cosine, sine, kv],
        [None, HBM, None, None, None, None],
        [shape((4, 512, 128)), stored((512, 512)), shape((4, 512, 256), F32)],
        [None] * 3,
        [vmem((1024, 512), BF), dma((1,))],
    )
    qraw = pinned(qraw)
    rr, r1, r2, r3, x15, acc = lax.optimization_barrier((rr, r1, r2, r3, x15, acc))
    f1, f2, f3 = [x_shift(rr, step) for step in STEPS]
    x15 = x15 + core_swap(jnp.where(core == 1, x15, jnp.zeros_like(x15)))
    starts = vmem((2, HALF, HALF), jnp.int32)
    acc, last = call(
        near_body,
        3,
        where,
        [q, acc, r1, r2, r3, rr, x15, ga, w_key, w_value, gk, tab_c, tab_s],
        [None] * 8 + [HBM, HBM] + [None] * 3,
        [shape((4, 512, 256), F32), stored((128, 512))],
        [None] * 2,
        [starts] + [vmem((1024, 256), BF)] * 2 + [dma((2,))],
    )
    att, lse, own, send = call(
        far_body,
        3.1,
        where,
        [q, acc, f1, f2, f3, w_output],
        [None] * 5 + [HBM],
        [stored((512, 512)), stored((8, 512), F32), token_rows, token_rows],
        [None] * 4,
        [vmem((4, 512, 256), F32), starts, vmem((512, 1024), BF), dma((1,))],
    )
    q, att, lse, last = map(pinned, (q, att, lse, last))
    send, dy_late = lax.optimization_barrier((send, dy))
    part, other = reduced(own, core_swap(send))
    dyo = core_swap(dy_late)
    inputs = x.astype(F32)
    hidden = inputs + (part.astype(F32) + other.astype(F32))
    inv_mid = inv_rms(hidden)
    mid_hat = hidden * inv_mid
    mid = (mid_hat * gf).astype(BF)
    mido = core_swap(mid)

    dmid, dmids, y, ys, dgate, dup, act = call(
        ffn_body,
        9.9,
        where[:1],
        [mid, mido, dy, dyo, w_gate, w_up, w_down],
        [None] * 4 + [HBM] * 3,
        [token_rows] * 4 + [shape((512, width))] * 3,
        [None] * 7,
        [vmem((1024, width), BF)] * 2 + [vmem((width, 1024), BF), dma((3, 3))],
        mib=28,
    )
    dpart, dother = reduced(dmid, core_swap(dmids))
    dpart, dgate, dup, act = lax.optimization_barrier((dpart, dgate, dup, act))
    part_width = 3 * width // 2
    chunk = pl.BlockSpec((HALF, 256), lambda i: (0, i), memory_space=pltpu.VMEM)
    (ffn_grads,) = call(
        ffn_grad_body,
        4,
        (),
        [mid, mido, dy, dyo, dgate, dup, act],
        [chunk] * 4 + [None] * 3,
        [stored((1024, 3 * width))],
        [pl.BlockSpec((256, 3 * width), lambda i: (i, 0), memory_space=pltpu.VMEM)],
        grid=(4,),
    )
    by_z = dp_groups(lambda core, x, y, z: (core, x, y))
    trade = lambda value: lax.all_to_all(value, "dp", 0, 0, axis_index_groups=by_z)
    early = trade(ffn_grads.reshape(4, 256, -1))
    dother, ffn_grads = lax.optimization_barrier((dother, ffn_grads))
    d_mid = dpart.astype(F32) + dother.astype(F32)
    gain_f = jnp.sum(d_mid * mid_hat, axis=0, keepdims=True)
    d_hidden = dy.astype(F32) + norm_back(d_mid, mid_hat, inv_mid, gf)
    d_attn = d_hidden.astype(BF)
    d_attno = core_swap(d_attn)

    rows8 = shape((2, 8, HALF), F32)
    d_att, lse, delta, dq, g1, g2, g3, glast = call(
        far_back_body,
        8,
        where,
        [d_attn, d_attno, w_output, q, att, lse, pinned(f1), pinned(f2), pinned(f3), last],
        [HBM] * 5 + [None] + [HBM] * 4,
        [shape((4, 512, 128)), rows8, rows8, shape((4, 512, 128), F32)] + [block] * 3 + [shape((128, 512))],
        [None] * 4 + [HBM] * 4,
        [vmem((512, 1024), BF), vmem((4, 512, 128), BF), vmem((512, 512), BF), vmem((3, HALF, 512), BF)]
        + [vmem((128, 512), BF), vmem((HALF, 1024), BF), vmem((HALF, 1024), BF)]
        + [vmem((3, HALF, 512), BF), vmem((128, 512), BF), starts, dma((13,))],
    )
    back = [{b: a for a, b in links.items()} for links in TREE]
    g1, g2, g3, ys = lax.optimization_barrier((g1, g2, g3, ys))
    y_part, y_other = reduced(y, core_swap(ys))
    far = [x_shift(value, -step) for step, value in zip(STEPS, (g1, g2, g3))]
    dq, gr, g1, g2, g3 = call(
        near_back_body,
        6,
        where,
        [q, d_att, lse, delta, dq, pinned(r1), pinned(r2), pinned(r3), pinned(rr)],
        [HBM] + [None] * 4 + [HBM] * 4,
        [shape((4, 512, 128), F32), shape((HALF, 512))] + [block] * 3,
        [None, None] + [HBM] * 3,
        [vmem((4, 512, 128), BF), vmem((4, HALF, 512), BF), vmem((3, HALF, 512), BF), starts, dma((8,))],
    )
    glast, dq = lax.optimization_barrier((glast, dq))
    glast = glast + chip_links(glast, back[2])
    dq, dkv = call(
        own_back_body,
        4,
        where,
        [q, kv, d_att, lse, delta, dq],
        [None] * 6,
        [shape((4, 512, 128), F32), stored((512, 512), F32)],
        [None] * 2,
    )
    dkv = pinned(dkv)
    glast, g1, g2, g3, dkv, *far = lax.optimization_barrier((glast, g1, g2, g3, dkv, *far))
    near = [x_shift(value, -step) for step, value in zip(STEPS, (g1, g2, g3))]
    glast = glast + chip_links(glast, back[1])
    gr = (sum(value.astype(F32) for value in far) + gr.astype(F32)).astype(BF)
    gr, dq, y_other = lax.optimization_barrier((gr, dq, y_other))
    gr = y_swap(gr)
    glast = glast + chip_links(glast, back[0])
    mid_grads, dn, gain_q = call(
        query_back_body,
        0.5,
        where[:1],
        [dq, d_attn, d_attno, att, normed, qraw, cosine, sine, gq, w_query],
        [None] * 3 + [HBM, HBM] + [None] * 4 + [HBM],
        [stored((1024, 1024)), stored((512, 1024)), shape((1, 128), F32)],
        [HBM, None, None],
        [vmem((1024, 512), BF), vmem((512, 512), BF), vmem((512, 1024), BF), vmem((1024, 1024), BF)]
        + [dma((4,))],
    )
    dn = pinned(dn)
    def y_turn(total):
        size = total.shape[-1]
        kept, send = call(
            y_turn_body,
            1,
            where[:1],
            [pinned(total.reshape(4, 2, 4, 32, size))],
            [None],
            [shape((4, 32, size))] * 2,
            [None] * 2,
            mib=24,
        )
        return kept, send

    x_kept, s1, s2, s3, own, send = call(
        key_back_body,
        0.5,
        where,
        [pinned(x), pinned(xo), ga, kraw, cosine, sine, gk, w_key, w_value, dkv, glast, *near, gr, dn, gain_q, gain_f],
        [HBM] * 2 + [None] * 5 + [HBM, HBM] + [None] * 6 + [HBM] + [None] * 2,
        [shape((8, 32, 640))] * 4 + [token_rows] * 2,
        [HBM] * 4 + [None] * 2,
        [vmem((1024, 256), BF)] * 2
        + [vmem((512, 512), F32), vmem((HALF, 1024), BF), vmem((HALF, 1024), BF), vmem((512, 1024), BF)]
        + [vmem((8, 4, 32, 640), BF), dma((9,))],
    )
    def y_turn(total):
        size = total.shape[-1]
        kept, send = call(
            y_turn_body,
            1,
            where[:1],
            [pinned(total.reshape(4, 2, 4, 32, size))],
            [None],
            [shape((4, 32, size))] * 2,
            [None] * 2,
            mib=24,
        )
        return kept, send

    early, mid_grads = lax.optimization_barrier((early, mid_grads))
    own, early, mid_grads = lax.optimization_barrier((own, early, mid_grads))
    middle = trade(mid_grads.reshape(4, 256, -1))
    early_kept, early_send = y_turn(early)
    early = early_kept, y_swap(early_send)
    late = [x_shift(value, step) for step, value in zip(STEPS, (s1, s2, s3))]
    layer_output = (hidden + (y_part.astype(F32) + y_other.astype(F32))).astype(BF)
    part, other = reduced(own, core_swap(send))

    def x_turn(kept, came):
        size = kept.shape[-1]
        parts = call(
            x_turn_body,
            1,
            where[:1],
            [kept, came],
            [None] * 2,
            [shape((32, size))] * 4,
            [HBM] * 4,
            [vmem((4, 32, size), BF), dma((4,))],
        )
        return [parts[0]] + [x_shift(value, step) for step, value in zip(STEPS, parts[1:])]

    early = x_turn(*early)
    late = call(
        z_turn_body,
        1,
        where[:1],
        [x_kept, *late],
        [None] * 4,
        [shape((2, 32, 640))] * 4,
        [HBM] * 4,
        [vmem((4, 2, 32, 640), BF), dma((4,))],
    )
    late = [late[0]] + [z_shift(value, step) for step, value in zip(STEPS, late[1:])]
    middle_kept, middle_send = y_turn(middle)
    middle = x_turn(middle_kept, y_swap(middle_send))
    late[0], *early = lax.optimization_barrier((late[0], *early))
    late[0], middle[0] = lax.optimization_barrier((late[0], middle[0]))
    mine, theirs = halved(late)
    mine, theirs, other = lax.optimization_barrier((mine, theirs, other))
    count = 3 * width + 1024 + 640
    kept, given, gains = call(
        sum_body,
        1,
        where[:1],
        [*early, *middle, mine, theirs],
        [None] * 10,
        [shape((16, count), F32)] * 2 + [shape((1, 128), F32)],
        [None] * 3,
    )
    both = lax.ppermute(
        gains,
        ("dp", "tensor"),
        [(i * 2 + t, (i ^ 1) * 2 + 1 - t) for i in range(64) for t in range(2)],
    )
    widths = [2 * width, 2 * width, 2 * width, 1024, 1024, 512, 512]
    grad_gate, grad_up, grad_down, grad_output, grad_query, grad_key, grad_value, *gains = call(
        final_body,
        1.4,
        where[:1],
        [kept, core_swap(given), gains, tensor_swap(gains), both],
        [None] * 5,
        [shape((16, n), F32) for n in widths] + [shape((1, n), F32) for n in (16, 16, 2, 2)],
        [None] * 11,
    )

    d_normed = part.astype(F32) + other.astype(F32)
    inv_in = inv_rms(inputs)
    grad_input = d_hidden + norm_back(d_normed, inputs * inv_in, inv_in, gain_attn[None, :])
    return (
        layer_output,
        grad_input,
        gains[0].reshape(16),
        grad_query,
        grad_key,
        grad_value,
        gains[2].reshape(2),
        gains[3].reshape(2),
        jnp.transpose(grad_output),
        gains[1].reshape(16),
        grad_gate,
        grad_up,
        jnp.transpose(grad_down),
    )


def solution(mesh):
    placed = (
        P("dp", None),
        P(),
        P(),
        P(None, "tensor"),
        P(None, "tensor"),
        P(None, "tensor"),
        P(),
        P(),
        P("tensor", None),
        P(),
        P(None, "tensor"),
        P(None, "tensor"),
        P("tensor", None),
        P("dp", None),
    )
    return jax.shard_map(
        local,
        mesh=mesh,
        in_specs=placed,
        out_specs=(
            P("dp", None),
            P("dp", None),
            P("dp"),
            P("dp", "tensor"),
            P("dp", "tensor"),
            P("dp", "tensor"),
            P("dp"),
            P("dp"),
            P("tensor", "dp"),
            P("dp"),
            P("dp", "tensor"),
            P("dp", "tensor"),
            P("tensor", "dp"),
        ),
        check_vma=False,
    )
```
